128 devices in a mesh: row: 16 (over y, z), col: 8 (over x, core).
Axes of the slice: x: 4, y: 4, z: 4, core: 2. Of those that a mesh axis runs over, the one named last changes fastest.
Arguments:
- interior_residual: float32 [16, 8, 1024, 512], P('row', 'col'), may hold values from -6 to 6
- interface_residual: float32 [16, 8, 2, 512, 512], P('row', 'col'), may hold values from -6 to 6
- owner_face_weight: float32 [16, 8, 2, 512], P('row', 'col'), may hold values from 0.2 to 0.8
- interior_inverse_block: bfloat16 [16, 8, 1024, 1024], P('row', 'col'), may hold values from -0.1875 to 0.1875
- coupling: bfloat16 [16, 8, 1024, 2048], P('row', 'col'), may hold values from -0.125 to 0.125
- interface_block: bfloat16 [16, 8, 2048, 2048], P('row', 'col'), may hold values from -0.125 to 0.125
- corner_trace_basis: bfloat16 [16, 8, 4, 2048], P('row', 'col'), may hold values from -0.5 to 0.5
- coarse_inv: float32 [153, 153], replicated, may hold values from -0.5 to 0.5
- corner_map: int32 [16, 8, 4], replicated, may hold values from 0 to 152, as said below
- contact: int32 [16, 8, 4, 512], P('row', 'col'), may hold values from 0 to 4
Outputs:
- interior_output: float32 [16, 8, 1024, 512], P('row', 'col')
- z_face: float32 [16, 8, 2, 512, 512], P('row', 'col')
- currents: float32 [4, 512], replicated
The draws below stay inside these ranges and needn't reach their ends.
Inputs may be any that keep to these rules, and one draw needn't show every extreme that they name: `corner_map`: A permutation of the 153 corner numbers of a 17 by 8 + 1 lattice; corners 0..3 of subdomain (i, j) are lattice points (i, j), (i, j+1), (i+1, j), (i+1, j+1), so neighbours agree on shared corners.
All inputs are finite; a program needn't handle non-finite values.
Results may differ from the reference program's by a relative error of at most 0.0042.
Values may be sent and summed in bfloat16 or wider, within the bound.
No kernel may reach another device: no remote copies, remote signals or barrier semaphores. Data moves between devices by JAX's collectives and lax.ppermute only.
A program may use at most 128 MiB of HBM per device.

```python
import jax
import jax.numpy as jnp
from jax import lax

INTERIOR_UNKNOWNS = 1024
FACE_UNKNOWNS = 512
RHS_COUNT = 512
NTERM = 4
SUBDOMAIN_ROWS = 16
SUBDOMAIN_COLUMNS = 8
NC = 153


def draw_corner_map(key, part):
    key = jax.random.fold_in(key, 7)
    labels = jax.random.permutation(key, NC).astype(jnp.int32)
    block_rows = jnp.arange(SUBDOMAIN_ROWS, dtype=jnp.int32)[:, None, None]
    cols = jnp.arange(SUBDOMAIN_COLUMNS, dtype=jnp.int32)[None, :, None]
    corner = jnp.arange(4, dtype=jnp.int32)[None, None, :]
    lattice = (block_rows + corner // 2) * (SUBDOMAIN_COLUMNS + 1) + cols + corner % 2
    return labels[lattice]


def touch_ends(array, key, low, top_value):
    place = [jax.random.randint(jax.random.fold_in(key, axis), (), 0, length) for axis, length in enumerate(array.shape)]
    widest = array.shape.index(max(array.shape))
    beside = place[:widest] + [(place[widest] + 1) % array.shape[widest]] + place[widest + 1:]
    return array.at[tuple(place)].set(low).at[tuple(beside)].set(top_value)


def levels(rng, dims, cuts, low, top_value):
    loudness = 1.0
    for axis_at, parts in cuts:
        heights = jax.random.uniform(jax.random.fold_in(jax.random.fold_in(rng, 6), axis_at), (parts,), jnp.float32, low / len(cuts), top_value / len(cuts))
        loudness = loudness * jnp.repeat(jnp.exp(heights), dims[axis_at] // parts).reshape((-1,) + (1,) * (len(dims) - 1 - axis_at))
    return loudness


def centred(rng, extent, spread, most, pieces=(), kind=jnp.bfloat16):
    values = spread * jax.random.normal(rng, extent, jnp.float32)
    if pieces:
        values = values * levels(rng, extent, pieces, -0.22, 0.18)
    return jnp.clip(values, -most, most).astype(kind)


def setup_inputs(seed: int = 0) -> dict:
    seeds = jax.random.split(jax.random.key(seed), 11)
    return {
        "interior_residual": centred(seeds[0], (SUBDOMAIN_ROWS, SUBDOMAIN_COLUMNS, INTERIOR_UNKNOWNS, RHS_COUNT), 1.0, 6.0, ((0, 16), (1, 8)), jnp.float32),
        "interface_residual": centred(seeds[1], (SUBDOMAIN_ROWS, SUBDOMAIN_COLUMNS, 2, FACE_UNKNOWNS, RHS_COUNT), 1.0, 6.0, ((0, 16), (1, 8)), jnp.float32),
        "owner_face_weight": jnp.clip(0.2 + 0.6 * jax.random.uniform(seeds[2], (SUBDOMAIN_ROWS, SUBDOMAIN_COLUMNS, 2, FACE_UNKNOWNS), jnp.float32) ** levels(seeds[2], (SUBDOMAIN_ROWS, SUBDOMAIN_COLUMNS, 2, FACE_UNKNOWNS), ((0, 16), (1, 8)), -0.2, 0.2), 0.2, 0.8),
        "interior_inverse_block": centred(seeds[3], (SUBDOMAIN_ROWS, SUBDOMAIN_COLUMNS, INTERIOR_UNKNOWNS, INTERIOR_UNKNOWNS), INTERIOR_UNKNOWNS ** -0.5, 0.1875, ((0, 16), (1, 8))),
        "coupling": centred(seeds[4], (SUBDOMAIN_ROWS, SUBDOMAIN_COLUMNS, INTERIOR_UNKNOWNS, 4 * FACE_UNKNOWNS), (4 * FACE_UNKNOWNS) ** -0.5, 0.125, ((0, 16), (1, 8))),
        "interface_block": centred(seeds[5], (SUBDOMAIN_ROWS, SUBDOMAIN_COLUMNS, 4 * FACE_UNKNOWNS, 4 * FACE_UNKNOWNS), (4 * FACE_UNKNOWNS) ** -0.5, 0.125, ((0, 16), (1, 8))),
        "corner_trace_basis": centred(seeds[6], (SUBDOMAIN_ROWS, SUBDOMAIN_COLUMNS, 4, 4 * FACE_UNKNOWNS), 0.08, 0.5, ((0, 16), (1, 8))),
        "coarse_inv": centred(seeds[7], (NC, NC), NC ** -0.5, 0.5, (), jnp.float32),
        "corner_map": draw_corner_map(jax.random.fold_in(seeds[10], 71), 0),
        "contact": touch_ends(jax.random.randint(seeds[9], (SUBDOMAIN_ROWS, SUBDOMAIN_COLUMNS, 4, FACE_UNKNOWNS), 0, 5), jax.random.fold_in(seeds[9], 1), 0, 4).astype(jnp.int32),
    }


def local_parts(items):
    gb, r_int, inv, coup, block, basis, contact = items
    t = (r_int - jnp.dot(coup, gb, preferred_element_type=jnp.float32)).astype(jnp.bfloat16)
    solution_state = jnp.dot(inv, t, preferred_element_type=jnp.float32)
    mesh_spacing = jnp.dot(block, gb, preferred_element_type=jnp.float32) + jnp.dot(coup.T, solution_state.astype(jnp.bfloat16), preferred_element_type=jnp.float32)
    q = jnp.dot(basis.astype(jnp.float32), mesh_spacing, precision=lax.Precision.HIGHEST)
    labels = jnp.arange(1, NTERM + 1, dtype=jnp.int32)
    table = (contact.reshape(-1)[None, :] == labels[:, None]).astype(jnp.float32)
    cur = jnp.dot(table, mesh_spacing, precision=lax.Precision.HIGHEST)
    return solution_state, mesh_spacing, q, cur


def reference(interior_residual, interface_residual, owner_face_weight, interior_inverse_block, coupling, interface_block, corner_trace_basis, coarse_inv, corner_map, contact):
    east = interface_residual[:, :, 0]
    north = interface_residual[:, :, 1]
    w_east = owner_face_weight[:, :, 0][..., None]
    w_north = owner_face_weight[:, :, 1][..., None]
    send_east = ((1.0 - w_east) * east).astype(jnp.bfloat16)
    send_north = ((1.0 - w_north) * north).astype(jnp.bfloat16)
    west = jnp.concatenate([jnp.zeros_like(send_east[:, :1]), send_east[:, :-1]], axis=1)
    south = jnp.concatenate([jnp.zeros_like(send_north[:1]), send_north[:-1]], axis=0)
    own_east = (w_east * east).astype(jnp.bfloat16)
    own_north = (w_north * north).astype(jnp.bfloat16)
    gb = jnp.stack([own_east, own_north, west, south], axis=2)
    total_count = SUBDOMAIN_ROWS * SUBDOMAIN_COLUMNS
    gb = gb.reshape(total_count, 4 * FACE_UNKNOWNS, RHS_COUNT)
    basis_all = corner_trace_basis.reshape(total_count, 4, 4 * FACE_UNKNOWNS)
    items = (gb, interior_residual.reshape(total_count, INTERIOR_UNKNOWNS, RHS_COUNT), interior_inverse_block.reshape(total_count, INTERIOR_UNKNOWNS, INTERIOR_UNKNOWNS),
             coupling.reshape(total_count, INTERIOR_UNKNOWNS, 4 * FACE_UNKNOWNS), interface_block.reshape(total_count, 4 * FACE_UNKNOWNS, 4 * FACE_UNKNOWNS),
             basis_all, contact.reshape(total_count, 4, FACE_UNKNOWNS))
    solution_state, mesh_spacing, q, cur = lax.map(local_parts, items)
    currents = jnp.sum(cur, axis=0) / FACE_UNKNOWNS
    ids = corner_map.reshape(-1).astype(jnp.int32)
    coarse_rhs = jnp.zeros((NC, RHS_COUNT), jnp.float32).at[ids].add(q.reshape(-1, RHS_COUNT))
    coarse = jnp.dot(coarse_inv, coarse_rhs, precision=lax.Precision.HIGHEST)
    selected_rows = coarse[ids].reshape(total_count, 4, RHS_COUNT)
    back_solve = jnp.einsum("gpt,gpv->gtv", basis_all.astype(jnp.float32), selected_rows, precision=lax.Precision.HIGHEST)
    face_index = (mesh_spacing + back_solve).reshape(SUBDOMAIN_ROWS, SUBDOMAIN_COLUMNS, 4, FACE_UNKNOWNS, RHS_COUNT)
    f_west = face_index[:, :, 2]
    f_south = face_index[:, :, 3]
    from_east = jnp.concatenate([f_west[:, 1:], jnp.zeros_like(f_west[:, :1])], axis=1)
    from_north = jnp.concatenate([f_south[1:], jnp.zeros_like(f_south[:1])], axis=0)
    z_east = w_east * face_index[:, :, 0] + (1.0 - w_east) * from_east
    z_north = w_north * face_index[:, :, 1] + (1.0 - w_north) * from_north
    z_face = jnp.stack([z_east, z_north], axis=2)
    interior_output = solution_state.reshape(SUBDOMAIN_ROWS, SUBDOMAIN_COLUMNS, INTERIOR_UNKNOWNS, RHS_COUNT)
    return interior_output, z_face, currents
```

```python
import jax
import jax.numpy as jnp
from jax import lax
from jax.experimental import pallas as pl
from jax.experimental.pallas import tpu as pltpu
from jax.sharding import PartitionSpec as P

FACE = 512
RHS = 512
INTERIOR = 1024
NTERM = 4
SENT = FACE + 16
HIGHEST = lax.Precision.HIGHEST
F32 = jnp.float32
BF16 = jnp.bfloat16
VMEM = pl.BlockSpec(memory_space=pltpu.VMEM)
SMEM = pl.BlockSpec(memory_space=pltpu.SMEM)
ANY = pl.BlockSpec(memory_space=pl.ANY)


def mm(a, b):
    return jnp.dot(a, b, preferred_element_type=F32)


def mm_nt(a, b):
    return lax.dot_general(a, b, (((1,), (1,)), ((), ())), preferred_element_type=F32)


def mm_tn(a, b):
    return lax.dot_general(a, b, (((0,), (0,)), ((), ())), preferred_element_type=F32)


def two_terms(a):
    high = a.astype(BF16)
    low = (a - high.astype(F32)).astype(BF16)
    return jnp.concatenate([high, low], axis=0)


def folded(a):
    half = a.shape[0] // 2
    return a[:half] + a[half:]


def column(row):
    return jnp.transpose(jnp.broadcast_to(row, (8, row.shape[1])))[:, :1]


def call(kernel, outs, in_specs, out_specs, scratch=(), flops=0, moved=0, vmem=40):
    return pl.pallas_call(
        kernel,
        out_shape=outs,
        in_specs=in_specs,
        out_specs=out_specs,
        scratch_shapes=list(scratch),
        compiler_params=pltpu.CompilerParams(vmem_limit_bytes=vmem << 20),
        cost_estimate=pl.CostEstimate(flops=flops, bytes_accessed=moved, transcendentals=0),
    )


def shape(rows, kind, columns=RHS):
    return jax.ShapeDtypeStruct((rows, columns), kind)


def send_kernel(pos, face, w, out):
    keep = (pos[0] > 0).astype(F32)
    out[...] = ((1.0 - column(w[...])) * keep * face[...]).astype(BF16)


def sent_face(keep, face, w):
    return call(send_kernel, shape(FACE, BF16), [SMEM, VMEM, VMEM], VMEM, moved=3 << 19)(keep, face, w)


def own_kernel(faces, w, out):
    for f in range(2):
        out[f * FACE : (f + 1) * FACE] = (column(w[f : f + 1, :]) * faces[f]).astype(BF16)


def early_kernel(coup_h, inv_h, block_h, r_h, own, basis, contact, p_h, h_h, q_out, k_out,
                 coup, inv, block, r, hbuf, pbuf, bt, gt, kacc, si, so):
    rows = 256
    own_n = 2 * FACE

    def get_coup(c):
        return pltpu.make_async_copy(coup_h.at[pl.ds(c * rows, rows)], coup.at[pl.ds(c * rows, rows)], si.at[c])

    def get_r(c):
        return pltpu.make_async_copy(r_h.at[pl.ds(c * rows, rows)], r.at[pl.ds(c * rows, rows)], si.at[4 + c])

    def get_block(c):
        return pltpu.make_async_copy(block_h.at[pl.ds(c * rows, rows)], block.at[pl.ds(c * rows, rows)], si.at[8 + c])

    get_inv = pltpu.make_async_copy(inv_h, inv, si.at[16])

    def put_p(c):
        return pltpu.make_async_copy(pbuf.at[pl.ds(c * rows, rows)], p_h.at[pl.ds(c * rows, rows)], so.at[c])

    def put_h(c):
        return pltpu.make_async_copy(hbuf.at[pl.ds(c * rows, rows)], h_h.at[pl.ds(c * rows, rows)], so.at[4 + c])

    for c in range(4):
        get_coup(c).start()
        get_r(c).start()
    get_inv.start()
    for c in range(8):
        get_block(c).start()

    labels = lax.broadcasted_iota(jnp.int32, (NTERM, FACE), 0) + 1
    bt32 = jnp.concatenate(
        [basis[...].astype(F32)]
        + [jnp.concatenate([(contact[f : f + 1, :] == labels).astype(F32) for f in range(4)], axis=1)],
        axis=0,
    )
    bt[...] = bt32.astype(BF16)

    def coup_step(c, _):
        get_coup(c).wait()
        get_r(c).wait()
        at = pl.ds(c * rows, rows)
        pbuf[at] = r[at] - mm(coup[at, :own_n], own[...])
        put_p(c).start()
        gt[c] = mm_nt(bt[...], coup[at])
        return 0

    lax.fori_loop(0, 4, coup_step, 0)
    g = jnp.concatenate([gt[c] for c in range(4)], axis=1)
    get_inv.wait()
    m = folded(mm(two_terms(g), inv[...]))
    m2 = two_terms(m)
    kacc[...] = -folded(mm(m2, coup[...]))
    rh = r[...].astype(BF16)
    rl = (r[...] - rh.astype(F32)).astype(BF16)
    qr = folded(mm(m2, rh)) + mm(m2[:8], rl)

    def block_step(c, _):
        get_block(c).wait()
        at = pl.ds(c * rows, rows)
        hbuf[at] = mm(block[at, :own_n], own[...])
        put_h(c).start()
        kacc[...] += mm(bt[:, pl.ds(pl.multiple_of(c * rows, rows), rows)], block[at])
        return 0

    lax.fori_loop(0, 8, block_step, 0)
    k2 = two_terms(kacc[...])
    q_out[...] = qr + folded(mm(k2[:, :own_n], own[...]))
    k_out[...] = k2[:, own_n:]
    for c in range(4):
        put_p(c).wait()
    for c in range(8):
        put_h(c).wait()


def early(coup, inv, block, r, own, basis, contact):
    return call(
        early_kernel,
        (shape(INTERIOR, F32), shape(4 * FACE, F32), shape(8, F32), shape(16, BF16, 2 * FACE)),
        [ANY, ANY, ANY, ANY, VMEM, VMEM, VMEM],
        (ANY, ANY, VMEM, VMEM),
        [
            pltpu.VMEM((INTERIOR, 4 * FACE), BF16),
            pltpu.VMEM((INTERIOR, INTERIOR), BF16),
            pltpu.VMEM((4 * FACE, 4 * FACE), BF16),
            pltpu.VMEM((INTERIOR, RHS), F32),
            pltpu.VMEM((4 * FACE, RHS), F32),
            pltpu.VMEM((INTERIOR, RHS), F32),
            pltpu.VMEM((8, 4 * FACE), BF16),
            pltpu.VMEM((4, 8, 256), F32),
            pltpu.VMEM((8, 4 * FACE), F32),
            pltpu.SemaphoreType.DMA((17,)),
            pltpu.SemaphoreType.DMA((12,)),
        ],
        flops=3_500_000_000,
        moved=23 << 20,
    )(coup, inv, block, r, own, basis, contact)


def corner_kernel(q, k, west, south, out):
    out[...] = q[...] + folded(mm(k[:, :FACE], west[...]) + mm(k[:, FACE:], south[...]))


def solve_kernel(pos, coup_h, inv_h, block_h, p_h, h_h, west, south, basis, x_h, sent, ub,
                 coup, inv, block, p, h, t, xbuf, si, so):
    rows = 256
    own_n = 2 * FACE

    def get_coup(c):
        return pltpu.make_async_copy(coup_h.at[pl.ds(c * rows, rows), pl.ds(own_n, own_n)], coup.at[pl.ds(c * rows, rows)], si.at[c])

    def get_p(c):
        return pltpu.make_async_copy(p_h.at[pl.ds(c * rows, rows)], p.at[pl.ds(c * rows, rows)], si.at[4 + c])

    def get_inv(c):
        return pltpu.make_async_copy(inv_h.at[pl.ds(c * rows, rows)], inv.at[pl.ds(c * rows, rows)], si.at[8 + c])

    get_block = pltpu.make_async_copy(block_h.at[pl.ds(3 * FACE, FACE), pl.ds(own_n, own_n)], block, si.at[12])
    get_h = pltpu.make_async_copy(h_h.at[pl.ds(3 * FACE, FACE)], h, si.at[13])

    def put_x(c):
        return pltpu.make_async_copy(xbuf.at[pl.ds(c * rows, rows)], x_h.at[pl.ds(c * rows, rows)], so.at[c])

    for c in range(4):
        get_coup(c).start()
        get_p(c).start()
    for c in range(4):
        get_inv(c).start()
    get_block.start()
    get_h.start()

    def t_step(c, _):
        get_coup(c).wait()
        get_p(c).wait()
        at = pl.ds(c * rows, rows)
        t[at] = (p[at] - mm(coup[at, :FACE], west[...]) - mm(coup[at, FACE:], south[...])).astype(BF16)
        return 0

    lax.fori_loop(0, 4, t_step, 0)

    def x_step(c, _):
        get_inv(c).wait()
        at = pl.ds(c * rows, rows)
        x = mm(inv[at], t[...])
        xbuf[at] = x
        ub[at] = x.astype(BF16)
        put_x(c).start()
        return 0

    lax.fori_loop(0, 4, x_step, 0)
    get_block.wait()
    get_h.wait()
    keep = (pos[0] > 0).astype(F32)
    for c in range(2):
        at = slice(c * rows, (c + 1) * rows)
        s = h[at] + mm(block[at, :FACE], west[...]) + mm(block[at, FACE:], south[...])
        s = s + mm_tn(coup[:, FACE + c * rows : FACE + (c + 1) * rows], ub[...])
        sent[at] = (s * keep).astype(BF16)
    sent[FACE:] = (jnp.concatenate([basis[...].astype(F32), jnp.zeros((12, FACE), F32)], axis=0) * keep).astype(BF16)
    for c in range(4):
        put_x(c).wait()


def solve(keep, coup, inv, block, p, h, west, south, basis):
    return call(
        solve_kernel,
        (shape(INTERIOR, F32), shape(SENT, BF16), shape(INTERIOR, BF16)),
        [SMEM, ANY, ANY, ANY, ANY, ANY, VMEM, VMEM, VMEM],
        (ANY, VMEM, VMEM),
        [
            pltpu.VMEM((INTERIOR, 2 * FACE), BF16),
            pltpu.VMEM((INTERIOR, INTERIOR), BF16),
            pltpu.VMEM((FACE, 2 * FACE), BF16),
            pltpu.VMEM((INTERIOR, RHS), F32),
            pltpu.VMEM((FACE, RHS), F32),
            pltpu.VMEM((INTERIOR, RHS), BF16),
            pltpu.VMEM((INTERIOR, RHS), F32),
            pltpu.SemaphoreType.DMA((14,)),
            pltpu.SemaphoreType.DMA((4,)),
        ],
        flops=3_300_000_000,
        moved=12 << 20,
    )(keep, coup, inv, block, p, h, west, south, basis)


def faces_kernel(pos, coup_h, block_h, h_h, ub, west, south, basis, sent, kept, coup, block, h, si):
    rows = 256
    own_n = 2 * FACE
    order = (4, 5, 0, 1, 2, 3)

    def get(n):
        at = pl.ds(order[n] * rows, rows)
        return (
            pltpu.make_async_copy(coup_h.at[:, at], coup.at[n], si.at[n]),
            pltpu.make_async_copy(block_h.at[at, pl.ds(own_n, own_n)], block.at[n], si.at[6 + n]),
            pltpu.make_async_copy(h_h.at[at], h.at[n], si.at[12 + n]),
        )

    for n in range(6):
        for copy in get(n):
            copy.start()
    keep = (pos[0] > 0).astype(F32)
    for n in range(6):
        for copy in get(n):
            copy.wait()
        s = h[n] + mm(block[n, :, :FACE], west[...]) + mm(block[n, :, FACE:], south[...]) + mm_tn(coup[n], ub[...])
        if n < 2:
            sent[n * rows : (n + 1) * rows] = (s * keep).astype(BF16)
        else:
            kept[(n - 2) * rows : (n - 1) * rows] = s
    sent[FACE:] = (jnp.concatenate([basis[...].astype(F32), jnp.zeros((12, FACE), F32)], axis=0) * keep).astype(BF16)


def faces(keep, coup, block, h, ub, west, south, basis):
    return call(
        faces_kernel,
        (shape(SENT, BF16), shape(2 * FACE, F32)),
        [SMEM, ANY, ANY, ANY, VMEM, VMEM, VMEM, VMEM],
        (VMEM, VMEM),
        [
            pltpu.VMEM((6, INTERIOR, 256), BF16),
            pltpu.VMEM((6, 256, 2 * FACE), BF16),
            pltpu.VMEM((6, 256, RHS), F32),
            pltpu.SemaphoreType.DMA((18,)),
        ],
        flops=3_300_000_000,
        moved=14 << 20,
    )(keep, coup, block, h, ub, west, south, basis)


def pair_kernel(pos, mine, theirs, out):
    first = pos[0] == 0
    a, b = mine[...], theirs[...]
    low = jnp.where(first, a, b)
    high = jnp.where(first, b, a)
    for r in range(2):
        out[3 * r : 3 * r + 1] = low[2 * r : 2 * r + 1]
        out[3 * r + 1 : 3 * r + 2] = low[2 * r + 1 : 2 * r + 2] + high[2 * r : 2 * r + 1]
        out[3 * r + 2 : 3 * r + 3] = high[2 * r + 1 : 2 * r + 2]
    out[6:10] = low[4:8] + high[4:8]


def placed(pos, blocks, slots):
    for k, block in enumerate(blocks):
        slots[lax.rem(pos[0] + k, 4)] = block[...]


def columns_kernel(pos, b0, b1, b2, b3, out, slots):
    placed(pos, (b0, b1, b2, b3), slots)
    for r in range(2):
        for c in range(9):
            b, e = min(c // 2, 3), 3 * r + c - 2 * min(c // 2, 3)
            row = slots[b, e : e + 1]
            if c % 2 == 0 and 0 < c < 8:
                row = slots[b - 1, 3 * r + 2 : 3 * r + 3] + row
            out[9 * r + c : 9 * r + c + 1] = row
    out[18:22] = (slots[0, 6:10] + slots[1, 6:10]) + (slots[2, 6:10] + slots[3, 6:10])


def rows_kernel(pos, b0, b1, b2, b3, out, slots):
    placed(pos, (b0, b1, b2, b3), slots)
    out[0:9] = slots[0, 0:9]
    for b in range(1, 4):
        out[9 * b : 9 * b + 9] = slots[b - 1, 9:18] + slots[b, 0:9]
    out[36:45] = slots[3, 9:18]
    out[45:49] = (slots[0, 18:22] + slots[1, 18:22]) + (slots[2, 18:22] + slots[3, 18:22])


def merged(kernel, at, blocks, rows):
    return call(
        kernel,
        shape(rows, F32),
        [SMEM] + [VMEM] * 4,
        VMEM,
        [pltpu.VMEM((4,) + blocks[0].shape, F32)],
        moved=1 << 18,
    )(at, *blocks)


def final_kernel(pos, b0, b1, b2, b3, e, kept, from_east, from_north, w, basis, z, cur, slots):
    cc = jnp.zeros((16, RHS), F32)
    for k, block in enumerate((b0, b1, b2, b3)):
        cc = cc + jnp.dot(e[lax.rem(pos[0] + k, 4)], block[...], precision=HIGHEST, preferred_element_type=F32)
        slots[lax.rem(pos[0] + k, 4)] = block[45:49]
    cur[...] = ((slots[0] + slots[1]) + (slots[2] + slots[3])) / FACE
    for f, got in enumerate((from_east, from_north)):
        wr = w[f : f + 1, :]
        mine = basis[:, f * FACE : (f + 1) * FACE].astype(F32) * wr
        other = got[FACE : FACE + 16].astype(F32)[:4] * (1.0 - wr)
        x = jnp.concatenate([mine, other], axis=0)
        c = jnp.concatenate([cc[0:4], cc[4 + 4 * f : 8 + 4 * f]], axis=0)
        corr = lax.dot_general(x, c, (((0,), (0,)), ((), ())), precision=HIGHEST, preferred_element_type=F32)
        wc = column(wr)
        z[f] = wc * kept[f * FACE : (f + 1) * FACE] + (1.0 - wc) * got[:FACE].astype(F32) + corr


def final(at, blocks, e, kept, from_east, from_north, w, basis):
    return call(
        final_kernel,
        (jax.ShapeDtypeStruct((2, FACE, RHS), F32), shape(NTERM, F32)),
        [SMEM] + [VMEM] * 10,
        (VMEM, VMEM),
        [pltpu.VMEM((4, NTERM, RHS), F32)],
        moved=7 << 20,
    )(at, *blocks, e, kept, from_east, from_north, w, basis)


def along(x, axis, d):
    n = lax.axis_size(axis)
    return lax.ppermute(x, axis, [(s, (s + d) % n) for s in range(n)])


def swapped(x, axis, stride, size, k):
    n = lax.axis_size(axis)
    route = []
    for dst in range(n):
        at = (dst // stride) % size
        route.append((dst + ((at + k) % size - at) * stride, dst))
    return lax.ppermute(x, axis, route)


def gathered(x, axis, stride):
    return [x] + [swapped(x, axis, stride, 4, k) for k in (1, 3, 2)]


def four(x, axis, stride):
    a, b, d, c = gathered(x, axis, stride)
    return a, b, c, d


def corner_table(coarse_inv, corner_map, i, j, y_blocks=4):
    corners = coarse_inv.shape[0]
    n_i, n_j = corner_map.shape[:2]
    ids = jnp.concatenate(
        [
            jnp.concatenate([corner_map[:, :, 0], corner_map[:, n_j - 1 :, 1]], axis=1),
            jnp.concatenate([corner_map[n_i - 1 :, :, 2], corner_map[n_i - 1 :, n_j - 1 :, 3]], axis=1),
        ],
        axis=0,
    )
    need = jnp.concatenate(
        [
            corner_map[i, j],
            corner_map[i, jnp.minimum(j + 1, n_j - 1)],
            corner_map[jnp.minimum(i + 1, n_i - 1), j],
            jnp.full((4,), -1, jnp.int32),
        ]
    )
    blocks = jnp.stack([ids[4 * b : 4 * b + 5].reshape(-1) for b in range(y_blocks)])
    blocks = jnp.concatenate([blocks, jnp.full((y_blocks, 4), -1, jnp.int32)], axis=1).reshape(-1)
    slots = jnp.arange(corners, dtype=jnp.int32)
    pick = (need[:, None] == slots[None, :]).astype(F32)
    place = (slots[:, None] == blocks[None, :]).astype(F32)
    e = jnp.dot(jnp.dot(pick, coarse_inv, precision=HIGHEST), place, precision=HIGHEST)
    return e.reshape(16, y_blocks, -1).transpose(1, 0, 2)


def local(
    interior_residual,
    interface_residual,
    owner_face_weight,
    interior_inverse_block,
    coupling,
    interface_block,
    corner_trace_basis,
    coarse_inv,
    corner_map,
    contact,
):
    i = lax.axis_index("row")
    j = lax.axis_index("col")
    last_i = lax.axis_size("row") - 1
    last_j = lax.axis_size("col") - 1
    one = lambda v: v.astype(jnp.int32).reshape(1)
    faces_in = interface_residual[0, 0]
    w = owner_face_weight[0, 0]
    inv, coup, block = interior_inverse_block[0, 0], coupling[0, 0], interface_block[0, 0]
    basis = corner_trace_basis[0, 0]
    south = along(sent_face(one(i < last_i), faces_in[1], w[1:2]), "row", 1)
    west = along(sent_face(one(j < last_j), faces_in[0], w[0:1]), "col", 1)
    own = call(own_kernel, shape(2 * FACE, BF16), [VMEM, VMEM], VMEM, moved=3 << 20)(faces_in, w)
    e = corner_table(coarse_inv, corner_map, i, j)
    p, h, q, k = early(coup, inv, block, interior_residual[0, 0], own, basis, contact[0, 0])

    sums = call(corner_kernel, shape(8, F32), [VMEM] * 4, VMEM, moved=1 << 20)(q, k, west, south)
    other = lax.ppermute(sums, "col", [(s, s ^ 1) for s in range(last_j + 1)])
    sums = call(pair_kernel, shape(10, F32), [SMEM, VMEM, VMEM], VMEM, moved=1 << 16)(one(j % 2), sums, other)

    x, to_south, ub = solve(one(i > 0), coup, inv, block, p, h, west, south, basis[:, 3 * FACE :])
    from_north = along(to_south, "row", -1)
    sums = merged(columns_kernel, one(j // 2), four(sums, "col", 2), 22)
    to_west, kept = faces(one(j > 0), coup, block, h, ub, west, south, basis[:, 2 * FACE : 3 * FACE])
    from_east = along(to_west, "col", -1)
    sums = merged(rows_kernel, one(i % 4), four(sums, "row", 1), 49)
    z, currents = final(one(i // 4), four(sums, "row", 4), e, kept, from_east, from_north, w, basis)
    return x[None, None], z[None, None], currents


def solution(mesh):
    return jax.shard_map(
        local,
        mesh=mesh,
        in_specs=(
            P("row", "col", None, None),
            P("row", "col", None, None, None),
            P("row", "col", None, None),
            P("row", "col", None, None),
            P("row", "col", None, None),
            P("row", "col", None, None),
            P("row", "col", None, None),
            P(),
            P(),
            P("row", "col", None, None),
        ),
        out_specs=(P("row", "col", None, None), P("row", "col", None, None, None), P()),
        check_vma=False,
    )
```

```python
import jax
import jax.numpy as jnp
from jax import lax
from jax.experimental import pallas as pl
from jax.experimental.pallas import tpu as pltpu
from jax.sharding import PartitionSpec as P

FACE = 512
RHS = 512
INTERIOR = 1024
NTERM = 4
ROWS = 16
COLS = 8
SENT = FACE + 16
HIGHEST = lax.Precision.HIGHEST
F32 = jnp.float32
BF16 = jnp.bfloat16
VMEM = pl.BlockSpec(memory_space=pltpu.VMEM)
SMEM = pl.BlockSpec(memory_space=pltpu.SMEM)
ANY = pl.BlockSpec(memory_space=pl.ANY)


def mm(a, b):
    return jnp.dot(a, b, preferred_element_type=F32)


def mm_nt(a, b):
    return lax.dot_general(a, b, (((1,), (1,)), ((), ())), preferred_element_type=F32)


def mm_tn(a, b):
    return lax.dot_general(a, b, (((0,), (0,)), ((), ())), preferred_element_type=F32)


def two_terms(a):
    high = a.astype(BF16)
    low = (a - high.astype(F32)).astype(BF16)
    return jnp.concatenate([high, low], axis=0)


def folded(a):
    half = a.shape[0] // 2
    return a[:half] + a[half:]


def column(row):
    return jnp.transpose(jnp.broadcast_to(row, (8, row.shape[1])))[:, :1]


def call(kernel, outs, in_specs, out_specs, scratch=(), after=(), vmem=16, cost=0):
    n = len(in_specs)

    def body(*refs):
        kernel(*refs[:n], *refs[n + len(after) :])

    run = pl.pallas_call(
        body,
        name=kernel.__name__,
        out_shape=outs,
        in_specs=list(in_specs) + [ANY] * len(after),
        out_specs=out_specs,
        scratch_shapes=list(scratch),
        compiler_params=pltpu.CompilerParams(vmem_limit_bytes=vmem << 20),
        cost_estimate=pl.CostEstimate(flops=1000 + cost * 1_000_000_000, bytes_accessed=1000 + cost * 3_000_000, transcendentals=0),
    )
    return lambda *args: run(*args, *after)


def shape(rows, kind, columns=RHS):
    return jax.ShapeDtypeStruct((rows, columns), kind)


def north_kernel(pos, faces, w, out):
    keep = (pos[0] < ROWS - 1).astype(F32)
    out[...] = ((1.0 - column(w[1:2, :])) * keep * faces[1]).astype(BF16)


def north_face(i, faces, w):
    return call(north_kernel, shape(FACE, BF16), [SMEM, VMEM, VMEM], VMEM, cost=4)(i, faces, w)


def east_kernel(pos, faces, w, out, own):
    keep = (pos[0] < COLS - 1).astype(F32)
    c = column(w[0:1, :])
    out[...] = ((1.0 - c) * keep * faces[0]).astype(BF16)
    own[:FACE] = (c * faces[0]).astype(BF16)
    own[FACE:] = (column(w[1:2, :]) * faces[1]).astype(BF16)


def east_face(j, faces, w, after):
    return call(east_kernel, (shape(FACE, BF16), shape(2 * FACE, BF16)), [SMEM, VMEM, VMEM], (VMEM, VMEM), after=after, cost=4)(j, faces, w)


def table_kernel(i, j, cm, cmv, cinv, out, rows):
    n_i, n_j = ROWS, COLS
    corners = cinv.shape[0]
    own_i, own_j = i[0], j[0]
    east_j = jnp.minimum(own_j + 1, n_j - 1)
    north_i = jnp.minimum(own_i + 1, n_i - 1)
    rows[...] = jnp.zeros_like(rows)
    for g, (a, b) in enumerate(((own_i, own_j), (own_i, east_j), (north_i, own_j))):
        for c in range(4):
            rows[4 * g + c : 4 * g + c + 1] = cinv[pl.ds(cm[4 * b + c, a], 1), :]
    ids = cmv[...].astype(F32)
    at = lax.broadcasted_iota(jnp.int32, (4 * n_j, n_j + 1), 0)
    col = lax.broadcasted_iota(jnp.int32, (4 * n_j, n_j + 1), 1)
    first = (at == jnp.where(col == n_j, 4 * n_j - 3, 4 * col)).astype(F32)
    last = (at == jnp.where(col == n_j, 4 * n_j - 1, 4 * col + 2)).astype(F32)
    flip = lambda s: lax.dot_general(ids, s, (((0,), (0,)), ((), ())), precision=HIGHEST, preferred_element_type=F32)
    low, high = flip(first), flip(last)
    slots = lax.broadcasted_iota(jnp.int32, (corners, 5 * (n_j + 1)), 0).astype(F32)
    for b in range(4):
        line = [low[a : a + 1] for a in range(4 * b, min(4 * b + 5, n_i))]
        if b == 3:
            line.append(high[n_i - 1 : n_i])
        place = (slots == jnp.concatenate(line, axis=1)).astype(F32)
        out[b, :, :45] = jnp.dot(rows[...], place, precision=HIGHEST, preferred_element_type=F32)
        out[b, :, 45:] = jnp.zeros((16, 4), F32)


def table(i, j, corner_map, coarse_inv, after):
    cm = corner_map.transpose(1, 2, 0).reshape(4 * COLS, ROWS)
    return call(
        table_kernel,
        jax.ShapeDtypeStruct((4, 16, 49), F32),
        [SMEM, SMEM, SMEM, VMEM, VMEM],
        VMEM,
        [pltpu.VMEM((16, coarse_inv.shape[0]), F32)],
        after=after,
        cost=20,
    )(i, j, cm, cm, coarse_inv)


def early_a_kernel(coup, r, own, basis, contact, p, g, bt):
    labels = lax.broadcasted_iota(jnp.int32, (NTERM, FACE), 0) + 1
    marks = jnp.concatenate([(contact[f : f + 1, :] == labels).astype(F32) for f in range(4)], axis=1)
    bt[...] = jnp.concatenate([basis[...].astype(F32), marks], axis=0).astype(BF16)
    g[...] = mm_nt(bt[...], coup[...])
    for c in range(2):
        at = slice(512 * c, 512 * c + 512)
        p[at] = r[at] - mm(coup[at, : 2 * FACE], own[...])


def early_b_kernel(g, inv, coup, r, k, q):
    m = folded(mm(two_terms(g[...]), inv[...]))
    m2 = two_terms(m)
    k[...] = -folded(mm(m2, coup[...]))
    high = r[...].astype(BF16)
    low = (r[...] - high.astype(F32)).astype(BF16)
    q[...] = folded(mm(m2, high)) + mm(m2[:8], low)


def early_c_kernel(bt, block, own, k, qr, h, q, k_out):
    k2 = two_terms(k[...] + mm(bt[...], block[...]))
    q[...] = qr[...] + folded(mm(k2[:, : 2 * FACE], own[...]))
    k_out[...] = k2[:, 2 * FACE :]
    for c in range(4):
        at = slice(512 * c, 512 * c + 512)
        h[at] = mm(block[at, : 2 * FACE], own[...])


def corner_kernel(q, k, west, south, out):
    out[...] = q[...] + folded(mm(k[:, :FACE], west[...]) + mm(k[:, FACE:], south[...]))


def tail(basis, keep):
    return (jnp.concatenate([basis.astype(F32), jnp.zeros((12, FACE), F32)], axis=0) * keep).astype(BF16)


def inner_kernel(coup, p, west, south, t):
    for c in range(2):
        at = slice(c * 512, (c + 1) * 512)
        t[at] = (p[at] - (mm(coup[at, 2 * FACE : 3 * FACE], west[...]) + mm(coup[at, 3 * FACE :], south[...]))).astype(BF16)


def result(f, coup, block, h, ub, west, south):
    at = slice(f * FACE, (f + 1) * FACE)
    own_n = 2 * FACE
    return h[at] + mm(block[at, own_n : 3 * FACE], west[...]) + mm(block[at, 3 * FACE :], south[...]) + mm_tn(coup[:, at], ub[...])


def tail(basis, f, keep):
    rows = basis[:, f * FACE : (f + 1) * FACE].astype(F32)
    return (jnp.concatenate([rows, jnp.zeros((12, FACE), F32)], axis=0) * keep).astype(BF16)


def solve_kernel(pos, coup, inv, block, t, h, west, south, basis, x_h, sent, ub, xbuf, sem):
    rows = 512
    copies = []
    for c in range(2):
        at = slice(c * rows, (c + 1) * rows)
        x = mm(inv[at], t[...])
        xbuf[at] = x
        ub[at] = x.astype(BF16)
        copies.append(pltpu.make_async_copy(xbuf.at[pl.ds(c * rows, rows)], x_h.at[pl.ds(c * rows, rows)], sem.at[c]))
        copies[c].start()
    keep = (pos[0] > 0).astype(F32)
    sent[:FACE] = (result(3, coup, block, h, ub, west, south) * keep).astype(BF16)
    sent[FACE:] = tail(basis, 3, keep)
    for copy in copies:
        copy.wait()


def west_kernel(pos, coup, block, h, ub, west, south, basis, sent):
    keep = (pos[0] > 0).astype(F32)
    sent[:FACE] = (result(2, coup, block, h, ub, west, south) * keep).astype(BF16)
    sent[FACE:] = tail(basis, 2, keep)


def kept_kernel(coup, block, h, ub, west, south, kept):
    for f in range(2):
        kept[f * FACE : (f + 1) * FACE] = result(f, coup, block, h, ub, west, south)


def pair_kernel(pos, mine, theirs, out):
    first = lax.rem(pos[0], 2) == 0
    a, b = mine[...], theirs[...]
    low = jnp.where(first, a, b)
    high = jnp.where(first, b, a)
    for r in range(2):
        out[3 * r : 3 * r + 1] = low[2 * r : 2 * r + 1]
        out[3 * r + 1 : 3 * r + 2] = low[2 * r + 1 : 2 * r + 2] + high[2 * r : 2 * r + 1]
        out[3 * r + 2 : 3 * r + 3] = high[2 * r + 1 : 2 * r + 2]
    out[6:10] = low[4:8] + high[4:8]


def placed(at, blocks, slots):
    for k, block in enumerate(blocks):
        slots[lax.rem(at + k, 4)] = block[...]


def columns_kernel(pos, b0, b1, b2, b3, out, slots):
    placed(lax.div(pos[0], 2), (b0, b1, b2, b3), slots)
    for r in range(2):
        for c in range(9):
            b, e = min(c // 2, 3), 3 * r + c - 2 * min(c // 2, 3)
            row = slots[b, e : e + 1]
            if c % 2 == 0 and 0 < c < 8:
                row = slots[b - 1, 3 * r + 2 : 3 * r + 3] + row
            out[9 * r + c : 9 * r + c + 1] = row
    out[18:22] = (slots[0, 6:10] + slots[1, 6:10]) + (slots[2, 6:10] + slots[3, 6:10])


def rows_kernel(pos, b0, b1, b2, b3, out, slots):
    placed(lax.rem(pos[0], 4), (b0, b1, b2, b3), slots)
    out[0:9] = slots[0, 0:9]
    for b in range(1, 4):
        out[9 * b : 9 * b + 9] = slots[b - 1, 9:18] + slots[b, 0:9]
    out[36:45] = slots[3, 9:18]
    out[45:49] = (slots[0, 18:22] + slots[1, 18:22]) + (slots[2, 18:22] + slots[3, 18:22])


def merged(kernel, at, blocks, rows, after=()):
    return call(
        kernel,
        shape(rows, F32),
        [SMEM] + [VMEM] * 4,
        VMEM,
        [pltpu.VMEM((4,) + blocks[0].shape, F32)],
        after=after,
    )(at, *blocks)


def final_kernel(pos, b0, b1, b2, b3, e, kept, from_east, from_north, w, basis, z, cur, slots, zbuf, sem):
    cc = jnp.zeros((16, RHS), F32)
    at = lax.div(pos[0], 4)
    for k, block in enumerate((b0, b1, b2, b3)):
        cc = cc + jnp.dot(e[lax.rem(at + k, 4)], block[...], precision=HIGHEST, preferred_element_type=F32)
        slots[lax.rem(at + k, 4)] = block[45:49]
    cur[...] = ((slots[0] + slots[1]) + (slots[2] + slots[3])) / FACE
    copies = []
    for f, got in enumerate((from_east, from_north)):
        wr = w[f : f + 1, :]
        mine = basis[:, f * FACE : (f + 1) * FACE].astype(F32) * wr
        other = got[FACE:].astype(F32)[:4] * (1.0 - wr)
        x = jnp.concatenate([mine, other], axis=0)
        c = jnp.concatenate([cc[0:4], cc[4 + 4 * f : 8 + 4 * f]], axis=0)
        xh, ch = x.astype(BF16).astype(F32), c.astype(BF16).astype(F32)
        pad = jnp.zeros((8, RHS), F32)
        left = jnp.concatenate([xh, x - xh, xh, pad], axis=0).astype(BF16)
        right = jnp.concatenate([ch, ch, c - ch, pad], axis=0).astype(BF16)
        wc = column(wr)
        for n in range(2):
            rows = slice(n * 256, (n + 1) * 256)
            part = wc[rows] * kept[f * FACE + n * 256 : f * FACE + (n + 1) * 256] + (1.0 - wc[rows]) * got[rows].astype(F32)
            zbuf[f, rows] = part + mm_tn(left[:, rows], right)
            here = pl.ds(n * 256, 256)
            copy = pltpu.make_async_copy(zbuf.at[f, here], z.at[f, here], sem.at[2 * f + n])
            copy.start()
            copies.append(copy)
    for copy in copies:
        copy.wait()


def final(at, blocks, e, kept, from_east, from_north, w, basis):
    return call(
        final_kernel,
        (jax.ShapeDtypeStruct((2, FACE, RHS), F32), shape(NTERM, F32)),
        [SMEM] + [VMEM] * 10,
        (ANY, VMEM),
        [
            pltpu.VMEM((4, NTERM, RHS), F32),
            pltpu.VMEM((2, FACE, RHS), F32),
            pltpu.SemaphoreType.DMA((4,)),
        ],
    )(at, *blocks, e, kept, from_east, from_north, w, basis)


def along(x, axis, d):
    n = lax.axis_size(axis)
    return lax.ppermute(x, axis, [(s, (s + d) % n) for s in range(n)])


def swapped(x, axis, stride, size, k):
    n = lax.axis_size(axis)
    route = []
    for dst in range(n):
        at = (dst // stride) % size
        route.append((dst + ((at + k) % size - at) * stride, dst))
    return lax.ppermute(x, axis, route)


def gathered(x, axis, stride):
    return [x] + [swapped(x, axis, stride, 4, k) for k in (1, 3, 2)]


def four(x, axis, stride):
    a, b, d, c = gathered(x, axis, stride)
    return a, b, c, d


def local(
    interior_residual,
    interface_residual,
    owner_face_weight,
    interior_inverse_block,
    coupling,
    interface_block,
    corner_trace_basis,
    coarse_inv,
    corner_map,
    contact,
):
    i = lax.axis_index("row").astype(jnp.int32).reshape(1)
    j = lax.axis_index("col").astype(jnp.int32).reshape(1)
    faces_in = interface_residual[0, 0]
    r = interior_residual[0, 0]
    w = owner_face_weight[0, 0]
    inv, coup, block = interior_inverse_block[0, 0], coupling[0, 0], interface_block[0, 0]
    basis = corner_trace_basis[0, 0]

    to_north = north_face(i, faces_in, w)
    south = along(to_north, "row", 1)
    to_east, own = east_face(j, faces_in, w, (to_north,))
    west = along(to_east, "col", 1)
    p, g, bt = call(
        early_a_kernel,
        (shape(INTERIOR, F32), shape(8, F32, INTERIOR), shape(8, BF16, 4 * FACE)),
        [VMEM] * 5,
        (VMEM,) * 3,
        cost=10,
    )(coup, r, own, basis, contact[0, 0])
    k, q = call(early_b_kernel, (shape(8, F32, 4 * FACE), shape(8, F32)), [VMEM] * 4, (VMEM,) * 2, cost=10)(g, inv, coup, r)
    h, q, k = call(
        early_c_kernel,
        (shape(4 * FACE, F32), shape(8, F32), shape(16, BF16, 2 * FACE)),
        [VMEM] * 5,
        (VMEM,) * 3,
        cost=10,
    )(bt, block, own, k, q)

    sums = call(corner_kernel, shape(8, F32), [VMEM] * 4, VMEM)(q, k, west, south)
    other = lax.ppermute(sums, "col", [(s, s ^ 1) for s in range(COLS)])
    t = call(inner_kernel, shape(INTERIOR, BF16), [VMEM] * 4, VMEM, after=(sums,), cost=1)(coup, p, west, south)
    sums = call(pair_kernel, shape(10, F32), [SMEM, VMEM, VMEM], VMEM, after=(t,))(j, sums, other)
    blocks = four(sums, "col", 2)
    x, to_south, ub = call(
        solve_kernel,
        (shape(INTERIOR, F32), shape(SENT, BF16), shape(INTERIOR, BF16)),
        [SMEM] + [VMEM] * 8,
        (ANY, VMEM, VMEM),
        [pltpu.VMEM((INTERIOR, RHS), F32), pltpu.SemaphoreType.DMA((2,))],
        after=(sums,),
        cost=4,
    )(i, coup, inv, block, t, h, west, south, basis)
    from_north = along(to_south, "row", -1)
    to_west = call(west_kernel, shape(SENT, BF16), [SMEM] + [VMEM] * 7, VMEM, after=(to_south,), cost=1)(
        j, coup, block, h, ub, west, south, basis
    )
    from_east = along(to_west, "col", -1)
    sums = merged(columns_kernel, j, blocks, 22, (to_west,))
    blocks = four(sums, "row", 1)
    kept = call(kept_kernel, shape(2 * FACE, F32), [VMEM] * 6, VMEM, after=(sums,), cost=3)(coup, block, h, ub, west, south)
    sums = merged(rows_kernel, i, blocks, 49, (kept,))
    blocks = four(sums, "row", 4)
    e = table(i, j, corner_map, coarse_inv, (sums,))
    z, currents = final(i, blocks, e, kept, from_east, from_north, w, basis)
    return x[None, None], z[None, None], currents


def solution(mesh):
    return jax.shard_map(
        local,
        mesh=mesh,
        in_specs=(
            P("row", "col", None, None),
            P("row", "col", None, None, None),
            P("row", "col", None, None),
            P("row", "col", None, None),
            P("row", "col", None, None),
            P("row", "col", None, None),
            P("row", "col", None, None),
            P(),
            P(),
            P("row", "col", None, None),
        ),
        out_specs=(P("row", "col", None, None), P("row", "col", None, None, None), P()),
        check_vma=False,
    )
```

```python
import jax
import jax.numpy as jnp
from jax import lax
from jax.experimental import pallas as pl
from jax.experimental.pallas import tpu as pltpu
from jax.sharding import PartitionSpec as P

FACE = 512
RHS = 512
INTERIOR = 1024
NTERM = 4
ROWS = 16
COLS = 8
SENT = FACE + 16
HIGHEST = lax.Precision.HIGHEST
F32 = jnp.float32
BF16 = jnp.bfloat16
VMEM = pl.BlockSpec(memory_space=pltpu.VMEM)
SMEM = pl.BlockSpec(memory_space=pltpu.SMEM)
ANY = pl.BlockSpec(memory_space=pl.ANY)


def mm(a, b):
    return jnp.dot(a, b, preferred_element_type=F32)


def mm_nt(a, b):
    return lax.dot_general(a, b, (((1,), (1,)), ((), ())), preferred_element_type=F32)


def mm_tn(a, b):
    return lax.dot_general(a, b, (((0,), (0,)), ((), ())), preferred_element_type=F32)


def two_terms(a):
    high = a.astype(BF16)
    low = (a - high.astype(F32)).astype(BF16)
    return jnp.concatenate([high, low], axis=0)


def folded(a):
    half = a.shape[0] // 2
    return a[:half] + a[half:]


def column(row):
    return jnp.transpose(jnp.broadcast_to(row, (8, row.shape[1])))[:, :1]


def call(kernel, outs, in_specs, out_specs, scratch=(), after=(), through=None, vmem=16, cost=0):
    n = len(in_specs)
    several = isinstance(outs, tuple)
    outs, out_specs = (outs, out_specs) if several else ((outs,), (out_specs,))
    extra = list(after)
    aliases = {}
    if through is not None:
        aliases = {n + len(extra): len(outs)}
        extra.append(through)
        outs = (*outs, jax.ShapeDtypeStruct(through.shape, through.dtype))
        out_specs = (*out_specs, ANY)
    m = len(outs) - len(aliases)

    def body(*refs):
        rest = refs[n + len(extra) :]
        kernel(*refs[:n], *rest[:m], *rest[len(outs) :])

    run = pl.pallas_call(
        body,
        name=kernel.__name__,
        out_shape=outs,
        in_specs=list(in_specs) + [ANY] * len(extra),
        out_specs=out_specs,
        scratch_shapes=list(scratch),
        input_output_aliases=aliases,
        compiler_params=pltpu.CompilerParams(vmem_limit_bytes=vmem << 20),
        cost_estimate=pl.CostEstimate(flops=1000 + cost * 1_000_000_000, bytes_accessed=1000 + cost * 3_000_000, transcendentals=0),
    )

    def made(*args):
        result = run(*args, *extra)
        return result if several or aliases else result[0]

    return made


def shape(rows, kind, columns=RHS):
    return jax.ShapeDtypeStruct((rows, columns), kind)


def north_kernel(pos, faces, w, out):
    keep = (pos[0] < ROWS - 1).astype(F32)
    out[...] = ((1.0 - column(w[1:2, :])) * keep * faces[1]).astype(BF16)


def north_face(i, faces, w):
    return call(north_kernel, shape(FACE, BF16), [SMEM, VMEM, VMEM], VMEM, cost=4)(i, faces, w)


def east_kernel(pos, faces, w, out, own):
    keep = (pos[0] < COLS - 1).astype(F32)
    c = column(w[0:1, :])
    out[...] = ((1.0 - c) * keep * faces[0]).astype(BF16)
    own[:FACE] = (c * faces[0]).astype(BF16)
    own[FACE:] = (column(w[1:2, :]) * faces[1]).astype(BF16)


def east_face(j, faces, w, after):
    return call(east_kernel, (shape(FACE, BF16), shape(2 * FACE, BF16)), [SMEM, VMEM, VMEM], (VMEM, VMEM), after=after, cost=4)(j, faces, w)


def table_kernel(i, j, cm, cmv, cinv, out, rows):
    n_i, n_j = ROWS, COLS
    corners = cinv.shape[0]
    own_i, own_j = i[0], j[0]
    east_j = jnp.minimum(own_j + 1, n_j - 1)
    north_i = jnp.minimum(own_i + 1, n_i - 1)
    rows[...] = jnp.zeros_like(rows)
    for g, (a, b) in enumerate(((own_i, own_j), (own_i, east_j), (north_i, own_j))):
        for c in range(4):
            rows[4 * g + c : 4 * g + c + 1] = cinv[pl.ds(cm[4 * b + c, a], 1), :]
    ids = cmv[...].astype(F32)
    at = lax.broadcasted_iota(jnp.int32, (4 * n_j, n_j + 1), 0)
    col = lax.broadcasted_iota(jnp.int32, (4 * n_j, n_j + 1), 1)
    first = (at == jnp.where(col == n_j, 4 * n_j - 3, 4 * col)).astype(F32)
    last = (at == jnp.where(col == n_j, 4 * n_j - 1, 4 * col + 2)).astype(F32)
    flip = lambda s: lax.dot_general(ids, s, (((0,), (0,)), ((), ())), precision=HIGHEST, preferred_element_type=F32)
    low, high = flip(first), flip(last)
    slots = lax.broadcasted_iota(jnp.int32, (corners, 5 * (n_j + 1)), 0).astype(F32)
    for b in range(4):
        line = [low[a : a + 1] for a in range(4 * b, min(4 * b + 5, n_i))]
        if b == 3:
            line.append(high[n_i - 1 : n_i])
        place = (slots == jnp.concatenate(line, axis=1)).astype(F32)
        out[b, :, :45] = jnp.dot(rows[...], place, precision=HIGHEST, preferred_element_type=F32)
        out[b, :, 45:] = jnp.zeros((16, 19), F32)


def table(i, j, corner_map, coarse_inv, after):
    cm = corner_map.transpose(1, 2, 0).reshape(4 * COLS, ROWS)
    return call(
        table_kernel,
        jax.ShapeDtypeStruct((4, 16, 64), F32),
        [SMEM, SMEM, SMEM, VMEM, VMEM],
        VMEM,
        [pltpu.VMEM((16, coarse_inv.shape[0]), F32)],
        after=after,
        cost=20,
    )(i, j, cm, cm, coarse_inv)


def early_a_kernel(coup, r, own, basis, contact, p, g, bt):
    labels = lax.broadcasted_iota(jnp.int32, (NTERM, FACE), 0) + 1
    marks = jnp.concatenate([(contact[f : f + 1, :] == labels).astype(F32) for f in range(4)], axis=1)
    bt[...] = jnp.concatenate([basis[...].astype(F32), marks], axis=0).astype(BF16)
    g[...] = mm_nt(bt[...], coup[...])
    for c in range(2):
        at = slice(512 * c, 512 * c + 512)
        p[at] = r[at] - mm(coup[at, : 2 * FACE], own[...])


def early_b_kernel(g, inv, coup, r, k, q):
    m = folded(mm(two_terms(g[...]), inv[...]))
    m2 = two_terms(m)
    k[...] = -folded(mm(m2, coup[...]))
    high = r[...].astype(BF16)
    low = (r[...] - high.astype(F32)).astype(BF16)
    q[...] = folded(mm(m2, high)) + mm(m2[:8], low)


def early_c_kernel(bt, block, own, k, qr, h, q, k_out):
    k2 = two_terms(k[...] + mm(bt[...], block[...]))
    q[...] = qr[...] + folded(mm(k2[:, : 2 * FACE], own[...]))
    k_out[...] = k2[:, 2 * FACE :]
    for c in range(4):
        at = slice(512 * c, 512 * c + 512)
        h[at] = mm(block[at, : 2 * FACE], own[...])


def corner_kernel(q, k, west, south, out):
    out[...] = q[...] + folded(mm(k[:, :FACE], west[...]) + mm(k[:, FACE:], south[...]))


def tail(basis, keep):
    return (jnp.concatenate([basis.astype(F32), jnp.zeros((12, FACE), F32)], axis=0) * keep).astype(BF16)


def inner_kernel(coup, p, west, south, t):
    for c in range(2):
        at = slice(c * 512, (c + 1) * 512)
        t[at] = (p[at] - (mm(coup[at, 2 * FACE : 3 * FACE], west[...]) + mm(coup[at, 3 * FACE :], south[...]))).astype(BF16)


def result(f, coup, block, h, ub, west, south):
    at = slice(f * FACE, (f + 1) * FACE)
    own_n = 2 * FACE
    return h[at] + mm(block[at, own_n : 3 * FACE], west[...]) + mm(block[at, 3 * FACE :], south[...]) + mm_tn(coup[:, at], ub[...])


def tail(basis, f, keep):
    rows = basis[:, f * FACE : (f + 1) * FACE].astype(F32)
    return (jnp.concatenate([rows, jnp.zeros((12, FACE), F32)], axis=0) * keep).astype(BF16)


def solve_kernel(pos, coup, inv, block, t, h, west, south, basis, x_h, sent, ub, xbuf, sem):
    rows = 512
    copies = []
    for c in range(2):
        at = slice(c * rows, (c + 1) * rows)
        x = mm(inv[at], t[...])
        xbuf[at] = x
        ub[at] = x.astype(BF16)
        copies.append(pltpu.make_async_copy(xbuf.at[pl.ds(c * rows, rows)], x_h.at[pl.ds(c * rows, rows)], sem.at[c]))
        copies[c].start()
    keep = (pos[0] > 0).astype(F32)
    sent[:FACE] = (result(3, coup, block, h, ub, west, south) * keep).astype(BF16)
    sent[FACE:] = tail(basis, 3, keep)
    for copy in copies:
        copy.wait()


def west_kernel(pos, coup, block, h, ub, west, south, basis, sent):
    keep = (pos[0] > 0).astype(F32)
    sent[:FACE] = (result(2, coup, block, h, ub, west, south) * keep).astype(BF16)
    sent[FACE:] = tail(basis, 2, keep)


def kept_kernel(coup, block, h, ub, west, south, kept):
    for f in range(2):
        kept[f * FACE : (f + 1) * FACE] = result(f, coup, block, h, ub, west, south)


def pair_kernel(pos, mine, theirs, out):
    first = lax.rem(pos[0], 2) == 0
    a, b = mine[...], theirs[...]
    low = jnp.where(first, a, b)
    high = jnp.where(first, b, a)
    for r in range(2):
        out[3 * r : 3 * r + 1] = low[2 * r : 2 * r + 1]
        out[3 * r + 1 : 3 * r + 2] = low[2 * r + 1 : 2 * r + 2] + high[2 * r : 2 * r + 1]
        out[3 * r + 2 : 3 * r + 3] = high[2 * r + 1 : 2 * r + 2]
    out[6:10] = low[4:8] + high[4:8]


def placed(at, blocks, slots):
    for k, block in enumerate(blocks):
        slots[lax.rem(at + k, 4)] = block[...]


def summed(slots, n):
    return (slots[0, n : n + 4] + slots[1, n : n + 4]) + (slots[2, n : n + 4] + slots[3, n : n + 4])


def rows_kernel(pos, b0, b1, b2, b3, out, slots):
    placed(lax.rem(pos[0], 4), (b0, b1, b2, b3), slots)
    out[0:3] = slots[0, 0:3]
    for b in range(1, 4):
        out[3 * b : 3 * b + 3] = slots[b - 1, 3:6] + slots[b, 0:3]
    out[12:15] = slots[3, 3:6]
    out[15:19] = summed(slots, 6)


def columns_kernel(pos, b0, b1, b2, b3, out, slots, full):
    placed(lax.div(pos[0], 2), (b0, b1, b2, b3), slots)
    full[40:] = jnp.zeros((24, RHS), F32)
    for r in range(5):
        for c in range(9):
            b = min(c // 2, 3)
            e = 3 * r + c - 2 * b
            row = slots[b, e : e + 1]
            if c % 2 == 0 and 0 < c < 8:
                row = slots[b - 1, 3 * r + 2 : 3 * r + 3] + row
            full[9 * r + c : 9 * r + c + 1] = row
    total = summed(slots, 15)
    high = total.astype(BF16).astype(F32)
    full[48:52] = high
    full[52:56] = total - high
    out[...] = full[...].astype(BF16)


def final_kernel(pos, b0, b1, b2, b3, e, kept, from_east, from_north, w, basis, z, cur, slots, zbuf, sem):
    cc = jnp.zeros((16, RHS), F32)
    at = lax.div(pos[0], 4)
    for k, block in enumerate((b0, b1, b2, b3)):
        cc = cc + folded(mm(two_terms(e[lax.rem(at + k, 4)]), block[...]))
        terms = block[48:64].astype(F32)
        slots[lax.rem(at + k, 4)] = terms[0:4] + terms[4:8]
    cur[...] = summed(slots, 0) / FACE
    copies = []
    for f, got in enumerate((from_east, from_north)):
        wr = w[f : f + 1, :]
        mine = basis[:, f * FACE : (f + 1) * FACE].astype(F32) * wr
        other = got[FACE:].astype(F32)[:4] * (1.0 - wr)
        x = jnp.concatenate([mine, other], axis=0)
        c = jnp.concatenate([cc[0:4], cc[4 + 4 * f : 8 + 4 * f]], axis=0)
        xh, ch = x.astype(BF16).astype(F32), c.astype(BF16).astype(F32)
        pad = jnp.zeros((8, RHS), F32)
        left = jnp.concatenate([xh, x - xh, xh, pad], axis=0).astype(BF16)
        right = jnp.concatenate([ch, ch, c - ch, pad], axis=0).astype(BF16)
        wc = column(wr)
        for n in range(2):
            rows = slice(n * 256, (n + 1) * 256)
            part = wc[rows] * kept[f * FACE + n * 256 : f * FACE + (n + 1) * 256] + (1.0 - wc[rows]) * got[rows].astype(F32)
            zbuf[f, rows] = part + mm_tn(left[:, rows], right)
            here = pl.ds(n * 256, 256)
            copy = pltpu.make_async_copy(zbuf.at[f, here], z.at[f, here], sem.at[2 * f + n])
            copy.start()
            copies.append(copy)
    for copy in copies:
        copy.wait()


def final(at, blocks, e, kept, from_east, from_north, w, basis):
    return call(
        final_kernel,
        (jax.ShapeDtypeStruct((2, FACE, RHS), F32), shape(NTERM, F32)),
        [SMEM] + [VMEM] * 10,
        (ANY, VMEM),
        [
            pltpu.VMEM((4, NTERM, RHS), F32),
            pltpu.VMEM((2, FACE, RHS), F32),
            pltpu.SemaphoreType.DMA((4,)),
        ],
    )(at, *blocks, e, kept, from_east, from_north, w, basis)


def along(x, axis, d):
    n = lax.axis_size(axis)
    return lax.ppermute(x, axis, [(s, (s + d) % n) for s in range(n)])


def swapped(x, axis, stride, size, k):
    n = lax.axis_size(axis)
    route = []
    for dst in range(n):
        at = (dst // stride) % size
        route.append((dst + ((at + k) % size - at) * stride, dst))
    return lax.ppermute(x, axis, route)


def gathered(x, axis, stride):
    return [x] + [swapped(x, axis, stride, 4, k) for k in (1, 3, 2)]


def four(x, axis, stride):
    a, b, d, c = gathered(x, axis, stride)
    return a, b, c, d


def local(
    interior_residual,
    interface_residual,
    owner_face_weight,
    interior_inverse_block,
    coupling,
    interface_block,
    corner_trace_basis,
    coarse_inv,
    corner_map,
    contact,
):
    i = lax.axis_index("row").astype(jnp.int32).reshape(1)
    j = lax.axis_index("col").astype(jnp.int32).reshape(1)
    faces_in = interface_residual[0, 0]
    r = interior_residual[0, 0]
    w = owner_face_weight[0, 0]
    inv, coup, block = interior_inverse_block[0, 0], coupling[0, 0], interface_block[0, 0]
    basis = corner_trace_basis[0, 0]

    to_north = north_face(i, faces_in, w)
    south = lax.ppermute(to_north, "row", [(s, s + 1) for s in range(ROWS - 1)])
    to_east, own = east_face(j, faces_in, w, (to_north,))
    west = along(to_east, "col", 1)
    p, g, bt = call(
        early_a_kernel,
        (shape(INTERIOR, F32), shape(8, F32, INTERIOR), shape(8, BF16, 4 * FACE)),
        [VMEM] * 5,
        (VMEM,) * 3,
        cost=10,
    )(coup, r, own, basis, contact[0, 0])
    k, q = call(early_b_kernel, (shape(8, F32, 4 * FACE), shape(8, F32)), [VMEM] * 4, (VMEM,) * 2, cost=10)(g, inv, coup, r)
    h, q, k = call(
        early_c_kernel,
        (shape(4 * FACE, F32), shape(8, F32), shape(16, BF16, 2 * FACE)),
        [VMEM] * 5,
        (VMEM,) * 3,
        cost=10,
    )(bt, block, own, k, q)

    sums = call(corner_kernel, shape(8, F32), [VMEM] * 4, VMEM)(q, k, west, south)
    other = lax.ppermute(sums, "col", [(s, s ^ 1) for s in range(COLS)])
    t = call(inner_kernel, shape(INTERIOR, BF16), [VMEM] * 4, VMEM, after=(sums,), cost=1)(coup, p, west, south)
    sums = call(pair_kernel, shape(10, F32), [SMEM, VMEM, VMEM], VMEM, after=(t,))(j, sums, other)
    blocks = four(sums, "row", 1)
    x, to_south, ub = call(
        solve_kernel,
        (shape(INTERIOR, F32), shape(SENT, BF16), shape(INTERIOR, BF16)),
        [SMEM] + [VMEM] * 8,
        (ANY, VMEM, VMEM),
        [pltpu.VMEM((INTERIOR, RHS), F32), pltpu.SemaphoreType.DMA((2,))],
        after=(sums,),
        cost=4,
    )(i, coup, inv, block, t, h, west, south, basis)
    from_north = along(to_south, "row", -1)
    sums = call(
        rows_kernel, shape(19, F32), [SMEM] + [VMEM] * 4, VMEM, [pltpu.VMEM((4, 10, RHS), F32)], after=(to_south,)
    )(i, *blocks)
    blocks = four(sums, "col", 2)
    to_west = call(west_kernel, shape(SENT, BF16), [SMEM] + [VMEM] * 7, VMEM, after=(sums,), cost=1)(
        j, coup, block, h, ub, west, south, basis
    )
    kept = call(kept_kernel, shape(2 * FACE, F32), [VMEM] * 6, VMEM, after=(sums,), cost=3)(coup, block, h, ub, west, south)
    sums, to_west = call(
        columns_kernel,
        shape(64, BF16),
        [SMEM] + [VMEM] * 4,
        VMEM,
        [pltpu.VMEM((4, 19, RHS), F32), pltpu.VMEM((64, RHS), F32)],
        after=(kept,),
        through=to_west,
    )(j, *blocks)
    from_east = along(to_west, "col", -1)
    blocks = four(sums, "row", 4)
    e = table(i, j, corner_map, coarse_inv, (sums,))
    z, currents = final(i, blocks, e, kept, from_east, from_north, w, basis)
    return x[None, None], z[None, None], currents


def solution(mesh):
    return jax.shard_map(
        local,
        mesh=mesh,
        in_specs=(
            P("row", "col", None, None),
            P("row", "col", None, None, None),
            P("row", "col", None, None),
            P("row", "col", None, None),
            P("row", "col", None, None),
            P("row", "col", None, None),
            P("row", "col", None, None),
            P(),
            P(),
            P("row", "col", None, None),
        ),
        out_specs=(P("row", "col", None, None), P("row", "col", None, None, None), P()),
        check_vma=False,
    )
```

```python
import jax
import jax.numpy as jnp
from jax import lax
from jax.experimental import pallas as pl
from jax.experimental.pallas import tpu as pltpu
from jax.sharding import PartitionSpec as P

FACE = 512
RHS = 512
INTERIOR = 1024
NTERM = 4
ROWS = 16
COLS = 8
SENT = FACE + 16
HIGHEST = lax.Precision.HIGHEST
F32 = jnp.float32
BF16 = jnp.bfloat16
VMEM = pl.BlockSpec(memory_space=pltpu.VMEM)
SMEM = pl.BlockSpec(memory_space=pltpu.SMEM)
ANY = pl.BlockSpec(memory_space=pl.ANY)


def mm(a, b):
    return jnp.dot(a, b, preferred_element_type=F32)


def mm_nt(a, b):
    return lax.dot_general(a, b, (((1,), (1,)), ((), ())), preferred_element_type=F32)


def mm_tn(a, b):
    return lax.dot_general(a, b, (((0,), (0,)), ((), ())), preferred_element_type=F32)


def two_terms(a):
    high = a.astype(BF16)
    low = (a - high.astype(F32)).astype(BF16)
    return jnp.concatenate([high, low], axis=0)


def folded(a):
    half = a.shape[0] // 2
    return a[:half] + a[half:]


def column(row):
    return jnp.transpose(jnp.broadcast_to(row, (8, row.shape[1])))[:, :1]


def call(kernel, outs, in_specs, out_specs, scratch=(), after=(), through=None, vmem=16, cost=0):
    n = len(in_specs)
    several = isinstance(outs, tuple)
    outs, out_specs = (outs, out_specs) if several else ((outs,), (out_specs,))
    extra = list(after)
    aliases = {}
    if through is not None:
        aliases = {n + len(extra): len(outs)}
        extra.append(through)
        outs = (*outs, jax.ShapeDtypeStruct(through.shape, through.dtype))
        out_specs = (*out_specs, ANY)
    m = len(outs) - len(aliases)

    def body(*refs):
        rest = refs[n + len(extra) :]
        kernel(*refs[:n], *rest[:m], *rest[len(outs) :])

    run = pl.pallas_call(
        body,
        name=kernel.__name__,
        out_shape=outs,
        in_specs=list(in_specs) + [ANY] * len(extra),
        out_specs=out_specs,
        scratch_shapes=list(scratch),
        input_output_aliases=aliases,
        compiler_params=pltpu.CompilerParams(vmem_limit_bytes=vmem << 20),
        cost_estimate=pl.CostEstimate(flops=1000 + cost * 1_000_000_000, bytes_accessed=1000 + cost * 3_000_000, transcendentals=0),
    )

    def made(*args):
        result = run(*args, *extra)
        return result if several or aliases else result[0]

    return made


def shape(rows, kind, columns=RHS):
    return jax.ShapeDtypeStruct((rows, columns), kind)


def north_kernel(pos, faces, w, out):
    keep = (pos[0] < ROWS - 1).astype(F32)
    out[...] = ((1.0 - column(w[1:2, :])) * keep * faces[1]).astype(BF16)


def north_face(i, faces, w):
    return call(north_kernel, shape(FACE, BF16), [SMEM, VMEM, VMEM], VMEM, cost=4)(i, faces, w)


def east_kernel(pos, faces, w, out, own):
    keep = (pos[0] < COLS - 1).astype(F32)
    c = column(w[0:1, :])
    out[...] = ((1.0 - c) * keep * faces[0]).astype(BF16)
    own[:FACE] = (c * faces[0]).astype(BF16)
    own[FACE:] = (column(w[1:2, :]) * faces[1]).astype(BF16)


def east_face(j, faces, w, after):
    return call(east_kernel, (shape(FACE, BF16), shape(2 * FACE, BF16)), [SMEM, VMEM, VMEM], (VMEM, VMEM), after=after, cost=4)(j, faces, w)


def table_kernel(i, j, cm, cmv, cinv, out, rows, lat):
    n_i, n_j = ROWS, COLS
    corners = cinv.shape[0]
    own_j = j[0]
    east_j = jnp.minimum(own_j + 1, n_j - 1)
    rows[...] = jnp.zeros_like(rows)
    for y in range(4):
        own_i = 4 * y + lax.rem(i[0], 4)
        north_i = jnp.minimum(own_i + 1, n_i - 1)
        for g, (a, b) in enumerate(((own_i, own_j), (own_i, east_j), (north_i, own_j))):
            for c in range(4):
                n = 16 * y + 4 * g + c
                rows[n : n + 1] = cinv[pl.ds(cm[4 * b + c, a], 1), :]
    ids = cmv[...].astype(F32)
    at = lax.broadcasted_iota(jnp.int32, (4 * n_j, n_j + 1), 0)
    col = lax.broadcasted_iota(jnp.int32, (4 * n_j, n_j + 1), 1)
    first = (at == jnp.where(col == n_j, 4 * n_j - 3, 4 * col)).astype(F32)
    last = (at == jnp.where(col == n_j, 4 * n_j - 1, 4 * col + 2)).astype(F32)
    flip = lambda s: lax.dot_general(ids, s, (((0,), (0,)), ((), ())), precision=HIGHEST, preferred_element_type=F32)
    lat[0:n_i] = flip(first)
    lat[n_i : n_i + 1] = flip(last)[n_i - 1 : n_i]
    base = 4 * lax.div(i[0], 4)
    line = jnp.concatenate([lat[pl.ds(base + a, 1), :] for a in range(5)], axis=1)
    slots = lax.broadcasted_iota(jnp.int32, (corners, 5 * (n_j + 1)), 0).astype(F32)
    out[:, :45] = jnp.dot(rows[...], (slots == line).astype(F32), precision=HIGHEST, preferred_element_type=F32)
    out[:, 45:] = jnp.zeros((64, 3), F32)


def table(i, j, corner_map, coarse_inv, after):
    cm = corner_map.transpose(1, 2, 0).reshape(4 * COLS, ROWS)
    return call(
        table_kernel,
        jax.ShapeDtypeStruct((64, 48), F32),
        [SMEM, SMEM, SMEM, VMEM, VMEM],
        VMEM,
        [pltpu.VMEM((64, coarse_inv.shape[0]), F32), pltpu.VMEM((24, COLS + 1), F32)],
        after=after,
        cost=0,
    )(i, j, cm, cm, coarse_inv)


def early_a_kernel(coup, r, own, basis, contact, p, g, bt):
    labels = lax.broadcasted_iota(jnp.int32, (NTERM, FACE), 0) + 1
    marks = jnp.concatenate([(contact[f : f + 1, :] == labels).astype(F32) for f in range(4)], axis=1)
    bt[...] = jnp.concatenate([basis[...].astype(F32), marks], axis=0).astype(BF16)
    g[...] = mm_nt(bt[...], coup[...])
    for c in range(2):
        at = slice(512 * c, 512 * c + 512)
        p[at] = r[at] - mm(coup[at, : 2 * FACE], own[...])


def early_b_kernel(g, inv, coup, r, k, q):
    m = folded(mm(two_terms(g[...]), inv[...]))
    m2 = two_terms(m)
    k[...] = -folded(mm(m2, coup[...]))
    high = r[...].astype(BF16)
    low = (r[...] - high.astype(F32)).astype(BF16)
    q[...] = folded(mm(m2, high)) + mm(m2[:8], low)


def early_c_kernel(bt, block, own, k, qr, h, q, k_out):
    k2 = two_terms(k[...] + mm(bt[...], block[...]))
    q[...] = qr[...] + folded(mm(k2[:, : 2 * FACE], own[...]))
    k_out[...] = k2[:, 2 * FACE :]
    for c in range(4):
        at = slice(512 * c, 512 * c + 512)
        h[at] = mm(block[at, : 2 * FACE], own[...])


def corner_kernel(q, k, west, south, out):
    out[...] = q[...] + folded(mm(k[:, :FACE], west[...]) + mm(k[:, FACE:], south[...]))


def tail(basis, keep):
    return (jnp.concatenate([basis.astype(F32), jnp.zeros((12, FACE), F32)], axis=0) * keep).astype(BF16)


def inner_kernel(coup, p, west, south, t):
    for c in range(2):
        at = slice(c * 512, (c + 1) * 512)
        t[at] = (p[at] - (mm(coup[at, 2 * FACE : 3 * FACE], west[...]) + mm(coup[at, 3 * FACE :], south[...]))).astype(BF16)


def result(f, coup, block, h, ub, west, south):
    at = slice(f * FACE, (f + 1) * FACE)
    own_n = 2 * FACE
    return h[at] + mm(block[at, own_n : 3 * FACE], west[...]) + mm(block[at, 3 * FACE :], south[...]) + mm_tn(coup[:, at], ub[...])


def tail(basis, f, keep):
    rows = basis[:, f * FACE : (f + 1) * FACE].astype(F32)
    return (jnp.concatenate([rows, jnp.zeros((12, FACE), F32)], axis=0) * keep).astype(BF16)


def solve_kernel(pos, coup, inv, block, t, h, west, south, basis, x_h, sent, ub, xbuf, sem):
    rows = 512
    copies = []
    for c in range(2):
        at = slice(c * rows, (c + 1) * rows)
        x = mm(inv[at], t[...])
        xbuf[at] = x
        ub[at] = x.astype(BF16)
        copies.append(pltpu.make_async_copy(xbuf.at[pl.ds(c * rows, rows)], x_h.at[pl.ds(c * rows, rows)], sem.at[c]))
        copies[c].start()
    keep = (pos[0] > 0).astype(F32)
    sent[:FACE] = (result(3, coup, block, h, ub, west, south) * keep).astype(BF16)
    sent[FACE:] = tail(basis, 3, keep)
    for copy in copies:
        copy.wait()


def west_kernel(pos, coup, block, h, ub, west, south, basis, sent):
    keep = (pos[0] > 0).astype(F32)
    sent[:FACE] = (result(2, coup, block, h, ub, west, south) * keep).astype(BF16)
    sent[FACE:] = tail(basis, 2, keep)


def kept_kernel(coup, block, h, ub, west, south, kept):
    for f in range(2):
        kept[f * FACE : (f + 1) * FACE] = result(f, coup, block, h, ub, west, south)


def pair_kernel(pos, mine, theirs, out):
    first = lax.rem(pos[0], 2) == 0
    a, b = mine[...], theirs[...]
    low = jnp.where(first, a, b)
    high = jnp.where(first, b, a)
    for r in range(2):
        out[3 * r : 3 * r + 1] = low[2 * r : 2 * r + 1]
        out[3 * r + 1 : 3 * r + 2] = low[2 * r + 1 : 2 * r + 2] + high[2 * r : 2 * r + 1]
        out[3 * r + 2 : 3 * r + 3] = high[2 * r + 1 : 2 * r + 2]
    out[6:10] = low[4:8] + high[4:8]


def placed(at, blocks, slots):
    for k, block in enumerate(blocks):
        slots[at ^ k] = block[...]


def summed(slots, n):
    return (slots[0, n : n + 4] + slots[1, n : n + 4]) + (slots[2, n : n + 4] + slots[3, n : n + 4])


def rows_kernel(pos, b0, b1, b2, b3, out, slots):
    placed(lax.rem(pos[0], 4), (b0, b1, b2, b3), slots)
    out[0:3] = slots[0, 0:3]
    for b in range(1, 4):
        out[3 * b : 3 * b + 3] = slots[b - 1, 3:6] + slots[b, 0:3]
    out[12:15] = slots[3, 3:6]
    out[15:19] = summed(slots, 6)


def columns_kernel(i, j, b0, b1, b2, b3, e, o0, o1, o2, o3, slots, full, shares):
    placed(lax.div(j[0], 2), (b0, b1, b2, b3), slots)
    full[40:] = jnp.zeros((8, RHS), F32)
    for r in range(5):
        for c in range(9):
            b = min(c // 2, 3)
            n = 3 * r + c - 2 * b
            row = slots[b, n : n + 1]
            if c % 2 == 0 and 0 < c < 8:
                row = slots[b - 1, 3 * r + 2 : 3 * r + 3] + row
            full[9 * r + c : 9 * r + c + 1] = row
    e2, q2 = two_terms(e[...]), two_terms(full[...])
    all_shares = folded(mm(e2, q2[:48])) + mm(e2[:64], q2[48:])
    total = summed(slots, 15)
    for y in range(4):
        shares[y] = all_shares[16 * y : 16 * y + 16]
        shares[y, 12:16] = total
    at = lax.div(i[0], 4)
    for k, out in enumerate((o0, o1, o2, o3)):
        out[...] = shares[at ^ k]


def final_kernel(pos, b0, b1, b2, b3, kept, from_east, from_north, w, basis, z, cur, slots, zbuf, sem):
    placed(lax.div(pos[0], 4), (b0, b1, b2, b3), slots)
    cur[...] = summed(slots, 12) / FACE
    cc = (slots[0] + slots[1]) + (slots[2] + slots[3])
    copies = []
    for f, got in enumerate((from_east, from_north)):
        wr = w[f : f + 1, :]
        mine = basis[:, f * FACE : (f + 1) * FACE].astype(F32) * wr
        other = got[FACE:].astype(F32)[:4] * (1.0 - wr)
        x = jnp.concatenate([mine, other], axis=0)
        c = jnp.concatenate([cc[0:4], cc[4 + 4 * f : 8 + 4 * f]], axis=0)
        xh, ch = x.astype(BF16).astype(F32), c.astype(BF16).astype(F32)
        pad = jnp.zeros((8, RHS), F32)
        left = jnp.concatenate([xh, x - xh, xh, pad], axis=0).astype(BF16)
        right = jnp.concatenate([ch, ch, c - ch, pad], axis=0).astype(BF16)
        wc = column(wr)
        for n in range(2):
            rows = slice(n * 256, (n + 1) * 256)
            part = wc[rows] * kept[f * FACE + n * 256 : f * FACE + (n + 1) * 256] + (1.0 - wc[rows]) * got[rows].astype(F32)
            zbuf[f, rows] = part + mm_tn(left[:, rows], right)
            here = pl.ds(n * 256, 256)
            copy = pltpu.make_async_copy(zbuf.at[f, here], z.at[f, here], sem.at[2 * f + n])
            copy.start()
            copies.append(copy)
    for copy in copies:
        copy.wait()


def final(at, blocks, kept, from_east, from_north, w, basis):
    return call(
        final_kernel,
        (jax.ShapeDtypeStruct((2, FACE, RHS), F32), shape(NTERM, F32)),
        [SMEM] + [VMEM] * 9,
        (ANY, VMEM),
        [
            pltpu.VMEM((4, 16, RHS), F32),
            pltpu.VMEM((2, FACE, RHS), F32),
            pltpu.SemaphoreType.DMA((4,)),
        ],
    )(at, *blocks, kept, from_east, from_north, w, basis)


def along(x, axis, d):
    n = lax.axis_size(axis)
    return lax.ppermute(x, axis, [(s, (s + d) % n) for s in range(n)])


def exchanged(x, axis, stride, k):
    return lax.ppermute(x, axis, [(d ^ (k * stride), d) for d in range(lax.axis_size(axis))])


def four(x, axis, stride):
    return [x] + [exchanged(x, axis, stride, k) for k in (1, 2, 3)]


def local(
    interior_residual,
    interface_residual,
    owner_face_weight,
    interior_inverse_block,
    coupling,
    interface_block,
    corner_trace_basis,
    coarse_inv,
    corner_map,
    contact,
):
    i = lax.axis_index("row").astype(jnp.int32).reshape(1)
    j = lax.axis_index("col").astype(jnp.int32).reshape(1)
    faces_in = interface_residual[0, 0]
    r = interior_residual[0, 0]
    w = owner_face_weight[0, 0]
    inv, coup, block = interior_inverse_block[0, 0], coupling[0, 0], interface_block[0, 0]
    basis = corner_trace_basis[0, 0]

    to_north = north_face(i, faces_in, w)
    south = lax.ppermute(to_north, "row", [(s, s + 1) for s in range(ROWS - 1)])
    to_east, own = east_face(j, faces_in, w, (to_north,))
    west = along(to_east, "col", 1)
    e = table(i, j, corner_map, coarse_inv, (own,))
    p, g, bt = call(
        early_a_kernel,
        (shape(INTERIOR, F32), shape(8, F32, INTERIOR), shape(8, BF16, 4 * FACE)),
        [VMEM] * 5,
        (VMEM,) * 3,
        after=(e,),
        cost=10,
    )(coup, r, own, basis, contact[0, 0])
    k, q = call(early_b_kernel, (shape(8, F32, 4 * FACE), shape(8, F32)), [VMEM] * 4, (VMEM,) * 2, cost=10)(g, inv, coup, r)
    h, q, k = call(
        early_c_kernel,
        (shape(4 * FACE, F32), shape(8, F32), shape(16, BF16, 2 * FACE)),
        [VMEM] * 5,
        (VMEM,) * 3,
        cost=10,
    )(bt, block, own, k, q)

    sums = call(corner_kernel, shape(8, F32), [VMEM] * 4, VMEM)(q, k, west, south)
    other = lax.ppermute(sums, "col", [(s, s ^ 1) for s in range(COLS)])
    t = call(inner_kernel, shape(INTERIOR, BF16), [VMEM] * 4, VMEM, after=(sums,), cost=1)(coup, p, west, south)
    sums = call(pair_kernel, shape(10, F32), [SMEM, VMEM, VMEM], VMEM, after=(t,))(j, sums, other)
    blocks = four(sums, "row", 1)
    x, to_south, ub = call(
        solve_kernel,
        (shape(INTERIOR, F32), shape(SENT, BF16), shape(INTERIOR, BF16)),
        [SMEM] + [VMEM] * 8,
        (ANY, VMEM, VMEM),
        [pltpu.VMEM((INTERIOR, RHS), F32), pltpu.SemaphoreType.DMA((2,))],
        after=(sums,),
        cost=4,
    )(i, coup, inv, block, t, h, west, south, basis)
    from_north = along(to_south, "row", -1)
    sums = call(
        rows_kernel, shape(19, F32), [SMEM] + [VMEM] * 4, VMEM, [pltpu.VMEM((4, 10, RHS), F32)], after=(to_south,)
    )(i, *blocks)
    blocks = four(sums, "col", 2)
    to_west = call(west_kernel, shape(SENT, BF16), [SMEM] + [VMEM] * 7, VMEM, after=(sums,), cost=1)(
        j, coup, block, h, ub, west, south, basis
    )
    from_east = along(to_west, "col", -1)
    shares = call(
        columns_kernel,
        (shape(16, F32),) * 4,
        [SMEM, SMEM] + [VMEM] * 5,
        (VMEM,) * 4,
        [pltpu.VMEM((4, 19, RHS), F32), pltpu.VMEM((48, RHS), F32), pltpu.VMEM((4, 16, RHS), F32)],
        after=(to_west,),
    )(i, j, *blocks, e)
    kept = call(kept_kernel, shape(2 * FACE, F32), [VMEM] * 6, VMEM, after=(shares[0],), cost=30)(
        coup, block, h, ub, west, south
    )
    blocks = [shares[0]] + [exchanged(shares[k], "row", 4, k) for k in (1, 2, 3)]
    z, currents = final(i, blocks, kept, from_east, from_north, w, basis)
    return x[None, None], z[None, None], currents


def solution(mesh):
    return jax.shard_map(
        local,
        mesh=mesh,
        in_specs=(
            P("row", "col", None, None),
            P("row", "col", None, None, None),
            P("row", "col", None, None),
            P("row", "col", None, None),
            P("row", "col", None, None),
            P("row", "col", None, None),
            P("row", "col", None, None),
            P(),
            P(),
            P("row", "col", None, None),
        ),
        out_specs=(P("row", "col", None, None), P("row", "col", None, None, None), P()),
        check_vma=False,
    )
```

```python
import jax
import jax.numpy as jnp
from jax import lax
from jax.experimental import pallas as pl
from jax.experimental.pallas import tpu as pltpu
from jax.sharding import PartitionSpec as P

FACE = 512
RHS = 512
INTERIOR = 1024
NTERM = 4
ROWS = 16
COLS = 8
SENT = FACE + 16
HIGHEST = lax.Precision.HIGHEST
F32 = jnp.float32
BF16 = jnp.bfloat16
VMEM = pl.BlockSpec(memory_space=pltpu.VMEM)
SMEM = pl.BlockSpec(memory_space=pltpu.SMEM)
ANY = pl.BlockSpec(memory_space=pl.ANY)


def mm(a, b):
    return jnp.dot(a, b, preferred_element_type=F32)


def mm_nt(a, b):
    return lax.dot_general(a, b, (((1,), (1,)), ((), ())), preferred_element_type=F32)


def mm_tn(a, b):
    return lax.dot_general(a, b, (((0,), (0,)), ((), ())), preferred_element_type=F32)


def two_terms(a):
    high = a.astype(BF16)
    low = (a - high.astype(F32)).astype(BF16)
    return jnp.concatenate([high, low], axis=0)


def folded(a):
    half = a.shape[0] // 2
    return a[:half] + a[half:]


def column(row):
    return jnp.transpose(jnp.broadcast_to(row, (8, row.shape[1])))[:, :1]


def call(kernel, outs, in_specs, out_specs, scratch=(), after=(), through=None, vmem=16, cost=0):
    n = len(in_specs)
    several = isinstance(outs, tuple)
    outs, out_specs = (outs, out_specs) if several else ((outs,), (out_specs,))
    extra = list(after)
    aliases = {}
    if through is not None:
        aliases = {n + len(extra): len(outs)}
        extra.append(through)
        outs = (*outs, jax.ShapeDtypeStruct(through.shape, through.dtype))
        out_specs = (*out_specs, ANY)
    m = len(outs) - len(aliases)

    def body(*refs):
        rest = refs[n + len(extra) :]
        kernel(*refs[:n], *rest[:m], *rest[len(outs) :])

    run = pl.pallas_call(
        body,
        name=kernel.__name__,
        out_shape=outs,
        in_specs=list(in_specs) + [ANY] * len(extra),
        out_specs=out_specs,
        scratch_shapes=list(scratch),
        input_output_aliases=aliases,
        compiler_params=pltpu.CompilerParams(vmem_limit_bytes=vmem << 20),
        cost_estimate=pl.CostEstimate(flops=1000 + cost * 1_000_000_000, bytes_accessed=1000 + cost * 3_000_000, transcendentals=0),
    )

    def made(*args):
        result = run(*args, *extra)
        return result if several or aliases else result[0]

    return made


def shape(rows, kind, columns=RHS):
    return jax.ShapeDtypeStruct((rows, columns), kind)


def north_kernel(pos, faces, weights, out, face, w, sem):
    parts, rows = 4, FACE // 4
    get_w = pltpu.make_async_copy(weights, w, sem.at[parts])
    get_w.start()
    copies = [
        pltpu.make_async_copy(faces.at[1, pl.ds(c * rows, rows)], face.at[pl.ds(c * rows, rows)], sem.at[c])
        for c in range(parts)
    ]
    for copy in copies:
        copy.start()
    get_w.wait()
    keep = (pos[0] < ROWS - 1).astype(F32)
    scale = (1.0 - column(w[1:2, :])) * keep
    for c, copy in enumerate(copies):
        copy.wait()
        at = slice(c * rows, (c + 1) * rows)
        out[at] = (scale[at] * face[at]).astype(BF16)


def north_face(i, faces, w):
    return call(
        north_kernel,
        shape(FACE, BF16),
        [SMEM, ANY, ANY],
        VMEM,
        [pltpu.VMEM((FACE, RHS), F32), pltpu.VMEM((2, FACE), F32), pltpu.SemaphoreType.DMA((5,))],
        vmem=52,
        cost=4,
    )(i, faces, w)


def east_kernel(pos, faces, w, out, own):
    keep = (pos[0] < COLS - 1).astype(F32)
    c = column(w[0:1, :])
    out[...] = ((1.0 - c) * keep * faces[0]).astype(BF16)
    own[:FACE] = (c * faces[0]).astype(BF16)
    own[FACE:] = (column(w[1:2, :]) * faces[1]).astype(BF16)


def east_face(j, faces, w, after):
    return call(east_kernel, (shape(FACE, BF16), shape(2 * FACE, BF16)), [SMEM, VMEM, VMEM], (VMEM, VMEM), after=after, cost=4)(j, faces, w)


def table_kernel(i, j, cm, cmv, cinv, out, rows, lat):
    n_i, n_j = ROWS, COLS
    corners = cinv.shape[0]
    own_j = j[0]
    east_j = jnp.minimum(own_j + 1, n_j - 1)
    rows[...] = jnp.zeros_like(rows)
    for y in range(4):
        own_i = 4 * y + lax.rem(i[0], 4)
        north_i = jnp.minimum(own_i + 1, n_i - 1)
        for g, (a, b) in enumerate(((own_i, own_j), (own_i, east_j), (north_i, own_j))):
            for c in range(4):
                n = 16 * y + 4 * g + c
                rows[n : n + 1] = cinv[pl.ds(cm[4 * b + c, a], 1), :]
    ids = cmv[...].astype(F32)
    at = lax.broadcasted_iota(jnp.int32, (4 * n_j, n_j + 1), 0)
    col = lax.broadcasted_iota(jnp.int32, (4 * n_j, n_j + 1), 1)
    first = (at == jnp.where(col == n_j, 4 * n_j - 3, 4 * col)).astype(F32)
    last = (at == jnp.where(col == n_j, 4 * n_j - 1, 4 * col + 2)).astype(F32)
    flip = lambda s: lax.dot_general(ids, s, (((0,), (0,)), ((), ())), precision=HIGHEST, preferred_element_type=F32)
    lat[0:n_i] = flip(first)
    lat[n_i : n_i + 1] = flip(last)[n_i - 1 : n_i]
    base = 4 * lax.div(i[0], 4)
    line = jnp.concatenate([lat[pl.ds(base + a, 1), :] for a in range(5)], axis=1)
    slots = lax.broadcasted_iota(jnp.int32, (corners, 5 * (n_j + 1)), 0).astype(F32)
    out[:, :45] = jnp.dot(rows[...], (slots == line).astype(F32), precision=HIGHEST, preferred_element_type=F32)
    out[:, 45:] = jnp.zeros((64, 3), F32)


def table(i, j, corner_map, coarse_inv, after):
    cm = corner_map.transpose(1, 2, 0).reshape(4 * COLS, ROWS)
    return call(
        table_kernel,
        jax.ShapeDtypeStruct((64, 48), F32),
        [SMEM, SMEM, SMEM, VMEM, VMEM],
        VMEM,
        [pltpu.VMEM((64, coarse_inv.shape[0]), F32), pltpu.VMEM((24, COLS + 1), F32)],
        after=after,
    )(i, j, cm, cm, coarse_inv)


def early_a_kernel(coup, r, own, basis, contact, p, g, bt):
    labels = lax.broadcasted_iota(jnp.int32, (NTERM, FACE), 0) + 1
    marks = jnp.concatenate([(contact[f : f + 1, :] == labels).astype(F32) for f in range(4)], axis=1)
    bt[...] = jnp.concatenate([basis[...].astype(F32), marks], axis=0).astype(BF16)
    g[...] = mm_nt(bt[...], coup[...])
    for c in range(2):
        at = slice(512 * c, 512 * c + 512)
        p[at] = r[at] - mm(coup[at, : 2 * FACE], own[...])


def early_b_kernel(g, inv, coup, r, k, q):
    m = folded(mm(two_terms(g[...]), inv[...]))
    m2 = two_terms(m)
    k[...] = -folded(mm(m2, coup[...]))
    high = r[...].astype(BF16)
    low = (r[...] - high.astype(F32)).astype(BF16)
    q[...] = folded(mm(m2, high)) + mm(m2[:8], low)


def early_c_kernel(bt, block, own, k, qr, h, q, k_out):
    k2 = two_terms(k[...] + mm(bt[...], block[...]))
    q[...] = qr[...] + folded(mm(k2[:, : 2 * FACE], own[...]))
    k_out[...] = k2[:, 2 * FACE :]
    for c in range(4):
        at = slice(512 * c, 512 * c + 512)
        h[at] = mm(block[at, : 2 * FACE], own[...])


def corner_kernel(q, k, west, south, out):
    out[...] = q[...] + folded(mm(k[:, :FACE], west[...]) + mm(k[:, FACE:], south[...]))


def tail(basis, keep):
    return (jnp.concatenate([basis.astype(F32), jnp.zeros((12, FACE), F32)], axis=0) * keep).astype(BF16)


def inner_kernel(coup, p, west, south, t):
    for c in range(2):
        at = slice(c * 512, (c + 1) * 512)
        t[at] = (p[at] - (mm(coup[at, 2 * FACE : 3 * FACE], west[...]) + mm(coup[at, 3 * FACE :], south[...]))).astype(BF16)


def result(f, coup, block, h, ub, west, south):
    at = slice(f * FACE, (f + 1) * FACE)
    own_n = 2 * FACE
    return h[at] + mm(block[at, own_n : 3 * FACE], west[...]) + mm(block[at, 3 * FACE :], south[...]) + mm_tn(coup[:, at], ub[...])


def tail(basis, f, keep):
    rows = basis[:, f * FACE : (f + 1) * FACE].astype(F32)
    return (jnp.concatenate([rows, jnp.zeros((12, FACE), F32)], axis=0) * keep).astype(BF16)


def solve_kernel(pos, coup, inv, block, t, h, west, south, basis, x_h, sent, ub, xbuf, sem):
    rows = 512
    copies = []
    for c in range(2):
        at = slice(c * rows, (c + 1) * rows)
        x = mm(inv[at], t[...])
        xbuf[at] = x
        ub[at] = x.astype(BF16)
        copies.append(pltpu.make_async_copy(xbuf.at[pl.ds(c * rows, rows)], x_h.at[pl.ds(c * rows, rows)], sem.at[c]))
        copies[c].start()
    keep = (pos[0] > 0).astype(F32)
    sent[:FACE] = (result(3, coup, block, h, ub, west, south) * keep).astype(BF16)
    sent[FACE:] = tail(basis, 3, keep)
    for copy in copies:
        copy.wait()


def west_kernel(pos, coup, block, h, ub, west, south, basis, sent):
    keep = (pos[0] > 0).astype(F32)
    sent[:FACE] = (result(2, coup, block, h, ub, west, south) * keep).astype(BF16)
    sent[FACE:] = tail(basis, 2, keep)


def kept_kernel(coup, block, h, ub, west, south, kept):
    for f in range(2):
        kept[f * FACE : (f + 1) * FACE] = result(f, coup, block, h, ub, west, south)


def pair_kernel(pos, mine, theirs, out):
    first = lax.rem(pos[0], 2) == 0
    a, b = mine[...], theirs[...]
    low = jnp.where(first, a, b)
    high = jnp.where(first, b, a)
    for r in range(2):
        out[3 * r : 3 * r + 1] = low[2 * r : 2 * r + 1]
        out[3 * r + 1 : 3 * r + 2] = low[2 * r + 1 : 2 * r + 2] + high[2 * r : 2 * r + 1]
        out[3 * r + 2 : 3 * r + 3] = high[2 * r + 1 : 2 * r + 2]
    out[6:10] = low[4:8] + high[4:8]


def placed(at, blocks, slots):
    for k, block in enumerate(blocks):
        slots[at ^ k] = block[...]


def summed(slots, n):
    return (slots[0, n : n + 4] + slots[1, n : n + 4]) + (slots[2, n : n + 4] + slots[3, n : n + 4])


def rows_kernel(pos, b0, b1, b2, b3, out, slots):
    placed(lax.rem(pos[0], 4), (b0, b1, b2, b3), slots)
    out[0:3] = slots[0, 0:3]
    for b in range(1, 4):
        out[3 * b : 3 * b + 3] = slots[b - 1, 3:6] + slots[b, 0:3]
    out[12:15] = slots[3, 3:6]
    out[15:19] = summed(slots, 6)


def columns_kernel(i, j, b0, b1, b2, b3, e, o0, o1, o2, o3, slots, full, shares):
    placed(lax.div(j[0], 2), (b0, b1, b2, b3), slots)
    full[40:] = jnp.zeros((8, RHS), F32)
    for r in range(5):
        for c in range(9):
            b = min(c // 2, 3)
            n = 3 * r + c - 2 * b
            row = slots[b, n : n + 1]
            if c % 2 == 0 and 0 < c < 8:
                row = slots[b - 1, 3 * r + 2 : 3 * r + 3] + row
            full[9 * r + c : 9 * r + c + 1] = row
    e2, q2 = two_terms(e[...]), two_terms(full[...])
    all_shares = folded(mm(e2, q2[:48])) + mm(e2[:64], q2[48:])
    total = summed(slots, 15)
    for y in range(4):
        shares[y] = all_shares[16 * y : 16 * y + 16]
        shares[y, 12:16] = total
    at = lax.div(i[0], 4)
    for k, out in enumerate((o0, o1, o2, o3)):
        out[...] = shares[at ^ k]


def final_kernel(pos, b0, b1, b2, b3, kept, from_east, from_north, w, basis, z, cur, slots, zbuf, sem):
    placed(lax.div(pos[0], 4), (b0, b1, b2, b3), slots)
    cur[...] = summed(slots, 12) / FACE
    cc = (slots[0] + slots[1]) + (slots[2] + slots[3])
    copies = []
    for f, got in enumerate((from_east, from_north)):
        wr = w[f : f + 1, :]
        mine = basis[:, f * FACE : (f + 1) * FACE].astype(F32) * wr
        other = got[FACE:].astype(F32)[:4] * (1.0 - wr)
        x = jnp.concatenate([mine, other], axis=0)
        c = jnp.concatenate([cc[0:4], cc[4 + 4 * f : 8 + 4 * f]], axis=0)
        xh, ch = x.astype(BF16).astype(F32), c.astype(BF16).astype(F32)
        pad = jnp.zeros((8, RHS), F32)
        left = jnp.concatenate([xh, x - xh, xh, pad], axis=0).astype(BF16)
        right = jnp.concatenate([ch, ch, c - ch, pad], axis=0).astype(BF16)
        wc = column(wr)
        for n in range(2):
            rows = slice(n * 256, (n + 1) * 256)
            part = wc[rows] * kept[f * FACE + n * 256 : f * FACE + (n + 1) * 256] + (1.0 - wc[rows]) * got[rows].astype(F32)
            zbuf[f, rows] = part + mm_tn(left[:, rows], right)
            here = pl.ds(n * 256, 256)
            copy = pltpu.make_async_copy(zbuf.at[f, here], z.at[f, here], sem.at[2 * f + n])
            copy.start()
            copies.append(copy)
    for copy in copies:
        copy.wait()


def final(at, blocks, kept, from_east, from_north, w, basis):
    return call(
        final_kernel,
        (jax.ShapeDtypeStruct((2, FACE, RHS), F32), shape(NTERM, F32)),
        [SMEM] + [VMEM] * 9,
        (ANY, VMEM),
        [
            pltpu.VMEM((4, 16, RHS), F32),
            pltpu.VMEM((2, FACE, RHS), F32),
            pltpu.SemaphoreType.DMA((4,)),
        ],
    )(at, *blocks, kept, from_east, from_north, w, basis)


def along(x, axis, d):
    n = lax.axis_size(axis)
    return lax.ppermute(x, axis, [(s, (s + d) % n) for s in range(n)])


def exchanged(x, axis, stride, k):
    return lax.ppermute(x, axis, [(d ^ (k * stride), d) for d in range(lax.axis_size(axis))])


def four(x, axis, stride):
    return [x] + [exchanged(x, axis, stride, k) for k in (1, 2, 3)]


def local(
    interior_residual,
    interface_residual,
    owner_face_weight,
    interior_inverse_block,
    coupling,
    interface_block,
    corner_trace_basis,
    coarse_inv,
    corner_map,
    contact,
):
    i = lax.axis_index("row").astype(jnp.int32).reshape(1)
    j = lax.axis_index("col").astype(jnp.int32).reshape(1)
    faces_in = interface_residual[0, 0]
    r = interior_residual[0, 0]
    w = owner_face_weight[0, 0]
    inv, coup, block = interior_inverse_block[0, 0], coupling[0, 0], interface_block[0, 0]
    basis = corner_trace_basis[0, 0]

    to_north = north_face(i, faces_in, w)
    south = lax.ppermute(to_north, "row", [(s, s + 1) for s in range(ROWS - 1)])
    to_east, own = east_face(j, faces_in, w, (to_north,))
    west = along(to_east, "col", 1)
    e = table(i, j, corner_map, coarse_inv, (own,))
    p, g, bt = call(
        early_a_kernel,
        (shape(INTERIOR, F32), shape(8, F32, INTERIOR), shape(8, BF16, 4 * FACE)),
        [VMEM] * 5,
        (VMEM,) * 3,
        after=(e,),
        cost=10,
    )(coup, r, own, basis, contact[0, 0])
    k, q = call(early_b_kernel, (shape(8, F32, 4 * FACE), shape(8, F32)), [VMEM] * 4, (VMEM,) * 2, cost=10)(g, inv, coup, r)
    h, q, k = call(
        early_c_kernel,
        (shape(4 * FACE, F32), shape(8, F32), shape(16, BF16, 2 * FACE)),
        [VMEM] * 5,
        (VMEM,) * 3,
        cost=10,
    )(bt, block, own, k, q)

    sums = call(corner_kernel, shape(8, F32), [VMEM] * 4, VMEM)(q, k, west, south)
    other = lax.ppermute(sums, "col", [(s, s ^ 1) for s in range(COLS)])
    t = call(inner_kernel, shape(INTERIOR, BF16), [VMEM] * 4, VMEM, after=(sums,), cost=1)(coup, p, west, south)
    sums = call(pair_kernel, shape(10, F32), [SMEM, VMEM, VMEM], VMEM, after=(t,))(j, sums, other)
    blocks = four(sums, "row", 1)
    x, to_south, ub = call(
        solve_kernel,
        (shape(INTERIOR, F32), shape(SENT, BF16), shape(INTERIOR, BF16)),
        [SMEM] + [VMEM] * 8,
        (ANY, VMEM, VMEM),
        [pltpu.VMEM((INTERIOR, RHS), F32), pltpu.SemaphoreType.DMA((2,))],
        after=(sums,),
        cost=4,
    )(i, coup, inv, block, t, h, west, south, basis)
    from_north = lax.ppermute(to_south, "row", [(s + 1, s) for s in range(ROWS - 1)])
    sums = call(
        rows_kernel, shape(19, F32), [SMEM] + [VMEM] * 4, VMEM, [pltpu.VMEM((4, 10, RHS), F32)], after=(to_south,)
    )(i, *blocks)
    blocks = four(sums, "col", 2)
    to_west = call(west_kernel, shape(SENT, BF16), [SMEM] + [VMEM] * 7, VMEM, after=(sums,), cost=1)(
        j, coup, block, h, ub, west, south, basis
    )
    from_east = along(to_west, "col", -1)
    shares = call(
        columns_kernel,
        (shape(16, F32),) * 4,
        [SMEM, SMEM] + [VMEM] * 5,
        (VMEM,) * 4,
        [pltpu.VMEM((4, 19, RHS), F32), pltpu.VMEM((48, RHS), F32), pltpu.VMEM((4, 16, RHS), F32)],
        after=(to_west,),
    )(i, j, *blocks, e)
    kept = call(kept_kernel, shape(2 * FACE, F32), [VMEM] * 6, VMEM, after=(shares[0],), cost=30)(
        coup, block, h, ub, west, south
    )
    blocks = [shares[0]] + [exchanged(shares[k], "row", 4, k) for k in (1, 2, 3)]
    z, currents = final(i, blocks, kept, from_east, from_north, w, basis)
    return x[None, None], z[None, None], currents


def solution(mesh):
    return jax.shard_map(
        local,
        mesh=mesh,
        in_specs=(
            P("row", "col", None, None),
            P("row", "col", None, None, None),
            P("row", "col", None, None),
            P("row", "col", None, None),
            P("row", "col", None, None),
            P("row", "col", None, None),
            P("row", "col", None, None),
            P(),
            P(),
            P("row", "col", None, None),
        ),
        out_specs=(P("row", "col", None, None), P("row", "col", None, None, None), P()),
        check_vma=False,
    )
```

```python
import jax
import jax.numpy as jnp
from jax import lax
from jax.experimental import pallas as pl
from jax.experimental.pallas import tpu as pltpu
from jax.sharding import PartitionSpec as P

FACE = 512
RHS = 512
INTERIOR = 1024
NTERM = 4
ROWS = 16
COLS = 8
SENT = FACE + 16
HIGHEST = lax.Precision.HIGHEST
F32 = jnp.float32
BF16 = jnp.bfloat16
VMEM = pl.BlockSpec(memory_space=pltpu.VMEM)
SMEM = pl.BlockSpec(memory_space=pltpu.SMEM)
ANY = pl.BlockSpec(memory_space=pl.ANY)


def mm(a, b):
    return jnp.dot(a, b, preferred_element_type=F32)


def mm_nt(a, b):
    return lax.dot_general(a, b, (((1,), (1,)), ((), ())), preferred_element_type=F32)


def mm_tn(a, b):
    return lax.dot_general(a, b, (((0,), (0,)), ((), ())), preferred_element_type=F32)


def two_terms(a):
    high = a.astype(BF16)
    low = (a - high.astype(F32)).astype(BF16)
    return jnp.concatenate([high, low], axis=0)


def folded(a):
    half = a.shape[0] // 2
    return a[:half] + a[half:]


def column(row):
    return jnp.transpose(jnp.broadcast_to(row, (8, row.shape[1])))[:, :1]


def call(kernel, outs, in_specs, out_specs, scratch=(), after=(), through=None, vmem=16, cost=0):
    n = len(in_specs)
    several = isinstance(outs, tuple)
    outs, out_specs = (outs, out_specs) if several else ((outs,), (out_specs,))
    extra = list(after)
    aliases = {}
    if through is not None:
        aliases = {n + len(extra): len(outs)}
        extra.append(through)
        outs = (*outs, jax.ShapeDtypeStruct(through.shape, through.dtype))
        out_specs = (*out_specs, ANY)
    m = len(outs) - len(aliases)

    def body(*refs):
        rest = refs[n + len(extra) :]
        kernel(*refs[:n], *rest[:m], *rest[len(outs) :])

    run = pl.pallas_call(
        body,
        name=kernel.__name__,
        out_shape=outs,
        in_specs=list(in_specs) + [ANY] * len(extra),
        out_specs=out_specs,
        scratch_shapes=list(scratch),
        input_output_aliases=aliases,
        compiler_params=pltpu.CompilerParams(vmem_limit_bytes=vmem << 20),
        cost_estimate=pl.CostEstimate(flops=1000 + cost * 1_000_000_000, bytes_accessed=1000 + cost * 3_000_000, transcendentals=0),
    )

    def made(*args):
        result = run(*args, *extra)
        return result if several or aliases else result[0]

    return made


def shape(rows, kind, columns=RHS):
    return jax.ShapeDtypeStruct((rows, columns), kind)


def north_kernel(pos, faces, weights, out, face, w, sem):
    parts, rows = 4, FACE // 4
    get_w = pltpu.make_async_copy(weights, w, sem.at[parts])
    get_w.start()
    copies = [
        pltpu.make_async_copy(faces.at[1, pl.ds(c * rows, rows)], face.at[pl.ds(c * rows, rows)], sem.at[c])
        for c in range(parts)
    ]
    for copy in copies:
        copy.start()
    get_w.wait()
    keep = (pos[0] < ROWS - 1).astype(F32)
    scale = (1.0 - column(w[1:2, :])) * keep
    for c, copy in enumerate(copies):
        copy.wait()
        at = slice(c * rows, (c + 1) * rows)
        out[at] = (scale[at] * face[at]).astype(BF16)


def north_face(i, faces, w):
    return call(
        north_kernel,
        shape(FACE, BF16),
        [SMEM, ANY, ANY],
        VMEM,
        [pltpu.VMEM((FACE, RHS), F32), pltpu.VMEM((2, FACE), F32), pltpu.SemaphoreType.DMA((5,))],
        vmem=52,
        cost=4,
    )(i, faces, w)


def east_kernel(pos, faces, w, out, own):
    keep = (pos[0] < COLS - 1).astype(F32)
    c = column(w[0:1, :])
    out[...] = ((1.0 - c) * keep * faces[0]).astype(BF16)
    own[:FACE] = (c * faces[0]).astype(BF16)
    own[FACE:] = (column(w[1:2, :]) * faces[1]).astype(BF16)


def east_face(j, faces, w, after):
    return call(east_kernel, (shape(FACE, BF16), shape(2 * FACE, BF16)), [SMEM, VMEM, VMEM], (VMEM, VMEM), after=after, cost=4)(j, faces, w)


def table_kernel(i, j, cm, cmv, cinv, out, rows, lat):
    n_i, n_j = ROWS, COLS
    corners = cinv.shape[0]
    own_j = j[0]
    east_j = jnp.minimum(own_j + 1, n_j - 1)
    rows[...] = jnp.zeros_like(rows)
    for y in range(4):
        own_i = 4 * y + lax.rem(i[0], 4)
        north_i = jnp.minimum(own_i + 1, n_i - 1)
        for g, (a, b) in enumerate(((own_i, own_j), (own_i, east_j), (north_i, own_j))):
            for c in range(4):
                n = 16 * y + 4 * g + c
                rows[n : n + 1] = cinv[pl.ds(cm[4 * b + c, a], 1), :]
    ids = cmv[...].astype(F32)
    at = lax.broadcasted_iota(jnp.int32, (4 * n_j, n_j + 1), 0)
    col = lax.broadcasted_iota(jnp.int32, (4 * n_j, n_j + 1), 1)
    first = (at == jnp.where(col == n_j, 4 * n_j - 3, 4 * col)).astype(F32)
    last = (at == jnp.where(col == n_j, 4 * n_j - 1, 4 * col + 2)).astype(F32)
    flip = lambda s: lax.dot_general(ids, s, (((0,), (0,)), ((), ())), precision=HIGHEST, preferred_element_type=F32)
    lat[0:n_i] = flip(first)
    lat[n_i : n_i + 1] = flip(last)[n_i - 1 : n_i]
    base = 4 * lax.div(i[0], 4)
    line = jnp.concatenate([lat[pl.ds(base + a, 1), :] for a in range(5)], axis=1)
    slots = lax.broadcasted_iota(jnp.int32, (corners, 5 * (n_j + 1)), 0).astype(F32)
    out[:, :45] = jnp.dot(rows[...], (slots == line).astype(F32), precision=HIGHEST, preferred_element_type=F32)
    out[:, 45:] = jnp.zeros((64, 3), F32)


def table(i, j, corner_map, coarse_inv, after):
    cm = corner_map.transpose(1, 2, 0).reshape(4 * COLS, ROWS)
    return call(
        table_kernel,
        jax.ShapeDtypeStruct((64, 48), F32),
        [SMEM, SMEM, SMEM, VMEM, VMEM],
        VMEM,
        [pltpu.VMEM((64, coarse_inv.shape[0]), F32), pltpu.VMEM((24, COLS + 1), F32)],
        after=after,
    )(i, j, cm, cm, coarse_inv)


def early_a_kernel(coup, r, own, basis, contact, p, g, bt):
    labels = lax.broadcasted_iota(jnp.int32, (NTERM, FACE), 0) + 1
    marks = jnp.concatenate([(contact[f : f + 1, :] == labels).astype(F32) for f in range(4)], axis=1)
    bt[...] = jnp.concatenate([basis[...].astype(F32), marks], axis=0).astype(BF16)
    g[...] = mm_nt(bt[...], coup[...])
    for c in range(2):
        at = slice(512 * c, 512 * c + 512)
        p[at] = r[at] - mm(coup[at, : 2 * FACE], own[...])


def early_b_kernel(g, inv, coup, r, k, q):
    m = folded(mm(two_terms(g[...]), inv[...]))
    m2 = two_terms(m)
    k[...] = -folded(mm(m2, coup[...]))
    high = r[...].astype(BF16)
    low = (r[...] - high.astype(F32)).astype(BF16)
    q[...] = folded(mm(m2, high)) + mm(m2[:8], low)


def early_c_kernel(bt, block, own, k, qr, h, q, k_out):
    k2 = two_terms(k[...] + mm(bt[...], block[...]))
    q[...] = qr[...] + folded(mm(k2[:, : 2 * FACE], own[...]))
    k_out[...] = k2[:, 2 * FACE :]
    for c in range(4):
        at = slice(512 * c, 512 * c + 512)
        h[at] = mm(block[at, : 2 * FACE], own[...])


def corner_kernel(q, k, west, south, out):
    out[...] = q[...] + folded(mm(k[:, :FACE], west[...]) + mm(k[:, FACE:], south[...]))


def tail(basis, keep):
    return (jnp.concatenate([basis.astype(F32), jnp.zeros((12, FACE), F32)], axis=0) * keep).astype(BF16)


def inner_kernel(coup, p, west, south, t):
    for c in range(2):
        at = slice(c * 512, (c + 1) * 512)
        t[at] = (p[at] - (mm(coup[at, 2 * FACE : 3 * FACE], west[...]) + mm(coup[at, 3 * FACE :], south[...]))).astype(BF16)


def result(f, coup, block, h, ub, west, south):
    at = slice(f * FACE, (f + 1) * FACE)
    own_n = 2 * FACE
    return h[at] + mm(block[at, own_n : 3 * FACE], west[...]) + mm(block[at, 3 * FACE :], south[...]) + mm_tn(coup[:, at], ub[...])


def tail(basis, f, keep):
    rows = basis[:, f * FACE : (f + 1) * FACE].astype(F32)
    return (jnp.concatenate([rows, jnp.zeros((12, FACE), F32)], axis=0) * keep).astype(BF16)


def solve_kernel(pos, coup, inv, block, t, h, west, south, basis, x_h, sent, ub, xbuf, sem):
    rows = 512
    copies = []
    for c in range(2):
        at = slice(c * rows, (c + 1) * rows)
        x = mm(inv[at], t[...])
        xbuf[at] = x
        ub[at] = x.astype(BF16)
        copies.append(pltpu.make_async_copy(xbuf.at[pl.ds(c * rows, rows)], x_h.at[pl.ds(c * rows, rows)], sem.at[c]))
        copies[c].start()
    keep = (pos[0] > 0).astype(F32)
    sent[:FACE] = (result(3, coup, block, h, ub, west, south) * keep).astype(BF16)
    sent[FACE:] = tail(basis, 3, keep)
    for copy in copies:
        copy.wait()


def west_kernel(pos, coup, block, h, ub, west, south, basis, sent):
    keep = (pos[0] > 0).astype(F32)
    sent[:FACE] = (result(2, coup, block, h, ub, west, south) * keep).astype(BF16)
    sent[FACE:] = tail(basis, 2, keep)


def kept_kernel(coup, block, h, ub, west, south, kept):
    for f in range(2):
        kept[f * FACE : (f + 1) * FACE] = result(f, coup, block, h, ub, west, south)


def pair_kernel(pos, mine, theirs, out):
    first = lax.rem(pos[0], 2) == 0
    a, b = mine[...], theirs[...]
    low = jnp.where(first, a, b)
    high = jnp.where(first, b, a)
    for r in range(2):
        out[3 * r : 3 * r + 1] = low[2 * r : 2 * r + 1]
        out[3 * r + 1 : 3 * r + 2] = low[2 * r + 1 : 2 * r + 2] + high[2 * r : 2 * r + 1]
        out[3 * r + 2 : 3 * r + 3] = high[2 * r + 1 : 2 * r + 2]
    out[6:10] = low[4:8] + high[4:8]


def placed(at, blocks, slots):
    for k, block in enumerate(blocks):
        slots[at ^ k] = block[...]


def summed(slots, n):
    return (slots[0, n : n + 4] + slots[1, n : n + 4]) + (slots[2, n : n + 4] + slots[3, n : n + 4])


def rows_kernel(pos, b0, b1, b2, b3, out, slots):
    placed(lax.rem(pos[0], 4), (b0, b1, b2, b3), slots)
    out[0:3] = slots[0, 0:3]
    for b in range(1, 4):
        out[3 * b : 3 * b + 3] = slots[b - 1, 3:6] + slots[b, 0:3]
    out[12:15] = slots[3, 3:6]
    out[15:19] = summed(slots, 6)


def columns_kernel(i, j, b0, b1, b2, b3, e, o0, o1, o2, o3, slots, full, shares):
    placed(lax.div(j[0], 2), (b0, b1, b2, b3), slots)
    full[40:] = jnp.zeros((8, RHS), F32)
    for r in range(5):
        for c in range(9):
            b = min(c // 2, 3)
            n = 3 * r + c - 2 * b
            row = slots[b, n : n + 1]
            if c % 2 == 0 and 0 < c < 8:
                row = slots[b - 1, 3 * r + 2 : 3 * r + 3] + row
            full[9 * r + c : 9 * r + c + 1] = row
    e2, q2 = two_terms(e[...]), two_terms(full[...])
    all_shares = folded(mm(e2, q2[:48])) + mm(e2[:64], q2[48:])
    total = summed(slots, 15)
    for y in range(4):
        shares[y] = all_shares[16 * y : 16 * y + 16]
        shares[y, 12:16] = total
    at = lax.div(i[0], 4)
    for k, out in enumerate((o0, o1, o2, o3)):
        out[...] = shares[at ^ k]


def final_kernel(pos, b0, b1, b2, b3, kept, from_east, from_north, w, basis, z, cur, slots, zbuf, sem):
    placed(lax.div(pos[0], 4), (b0, b1, b2, b3), slots)
    cur[...] = summed(slots, 12) / FACE
    cc = (slots[0] + slots[1]) + (slots[2] + slots[3])
    copies = []
    for f, got in enumerate((from_east, from_north)):
        wr = w[f : f + 1, :]
        mine = basis[:, f * FACE : (f + 1) * FACE].astype(F32) * wr
        other = got[FACE:].astype(F32)[:4] * (1.0 - wr)
        x = jnp.concatenate([mine, other], axis=0)
        c = jnp.concatenate([cc[0:4], cc[4 + 4 * f : 8 + 4 * f]], axis=0)
        xh, ch = x.astype(BF16).astype(F32), c.astype(BF16).astype(F32)
        pad = jnp.zeros((8, RHS), F32)
        left = jnp.concatenate([xh, x - xh, xh, pad], axis=0).astype(BF16)
        right = jnp.concatenate([ch, ch, c - ch, pad], axis=0).astype(BF16)
        wc = column(wr)
        for n in range(2):
            rows = slice(n * 256, (n + 1) * 256)
            part = wc[rows] * kept[f * FACE + n * 256 : f * FACE + (n + 1) * 256] + (1.0 - wc[rows]) * got[rows].astype(F32)
            zbuf[f, rows] = part + mm_tn(left[:, rows], right)
            here = pl.ds(n * 256, 256)
            copy = pltpu.make_async_copy(zbuf.at[f, here], z.at[f, here], sem.at[2 * f + n])
            copy.start()
            copies.append(copy)
    for copy in copies:
        copy.wait()


def final(at, blocks, kept, from_east, from_north, w, basis):
    return call(
        final_kernel,
        (jax.ShapeDtypeStruct((2, FACE, RHS), F32), shape(NTERM, F32)),
        [SMEM] + [VMEM] * 9,
        (ANY, VMEM),
        [
            pltpu.VMEM((4, 16, RHS), F32),
            pltpu.VMEM((2, FACE, RHS), F32),
            pltpu.SemaphoreType.DMA((4,)),
        ],
    )(at, *blocks, kept, from_east, from_north, w, basis)


def along(x, axis, d):
    n = lax.axis_size(axis)
    return lax.ppermute(x, axis, [(s, (s + d) % n) for s in range(n)])


def exchanged(x, axis, stride, k):
    return lax.ppermute(x, axis, [(d ^ (k * stride), d) for d in range(lax.axis_size(axis))])


def four(x, axis, stride):
    return [x] + [exchanged(x, axis, stride, k) for k in (1, 2, 3)]


def local(
    interior_residual,
    interface_residual,
    owner_face_weight,
    interior_inverse_block,
    coupling,
    interface_block,
    corner_trace_basis,
    coarse_inv,
    corner_map,
    contact,
):
    i = lax.axis_index("row").astype(jnp.int32).reshape(1)
    j = lax.axis_index("col").astype(jnp.int32).reshape(1)
    faces_in = interface_residual[0, 0]
    r = interior_residual[0, 0]
    w = owner_face_weight[0, 0]
    inv, coup, block = interior_inverse_block[0, 0], coupling[0, 0], interface_block[0, 0]
    basis = corner_trace_basis[0, 0]

    to_north = north_face(i, faces_in, w)
    south = along(to_north, "row", 1)
    to_east, own = east_face(j, faces_in, w, (to_north,))
    west = along(to_east, "col", 1)
    e = table(i, j, corner_map, coarse_inv, (own,))
    p, g, bt = call(
        early_a_kernel,
        (shape(INTERIOR, F32), shape(8, F32, INTERIOR), shape(8, BF16, 4 * FACE)),
        [VMEM] * 5,
        (VMEM,) * 3,
        after=(e,),
        cost=10,
    )(coup, r, own, basis, contact[0, 0])
    k, q = call(early_b_kernel, (shape(8, F32, 4 * FACE), shape(8, F32)), [VMEM] * 4, (VMEM,) * 2, cost=10)(g, inv, coup, r)
    h, q, k = call(
        early_c_kernel,
        (shape(4 * FACE, F32), shape(8, F32), shape(16, BF16, 2 * FACE)),
        [VMEM] * 5,
        (VMEM,) * 3,
        cost=10,
    )(bt, block, own, k, q)

    sums = call(corner_kernel, shape(8, F32), [VMEM] * 4, VMEM)(q, k, west, south)
    other = lax.ppermute(sums, "col", [(s, s ^ 1) for s in range(COLS)])
    t = call(inner_kernel, shape(INTERIOR, BF16), [VMEM] * 4, VMEM, after=(sums,), cost=1)(coup, p, west, south)
    sums = call(pair_kernel, shape(10, F32), [SMEM, VMEM, VMEM], VMEM, after=(t,))(j, sums, other)
    blocks = four(sums, "row", 1)
    x, to_south, ub = call(
        solve_kernel,
        (shape(INTERIOR, F32), shape(SENT, BF16), shape(INTERIOR, BF16)),
        [SMEM] + [VMEM] * 8,
        (ANY, VMEM, VMEM),
        [pltpu.VMEM((INTERIOR, RHS), F32), pltpu.SemaphoreType.DMA((2,))],
        after=(sums,),
        cost=4,
    )(i, coup, inv, block, t, h, west, south, basis)
    from_north = along(to_south, "row", -1)
    sums = call(
        rows_kernel, shape(19, F32), [SMEM] + [VMEM] * 4, VMEM, [pltpu.VMEM((4, 10, RHS), F32)], after=(to_south,)
    )(i, *blocks)
    blocks = four(sums, "col", 2)
    to_west = call(west_kernel, shape(SENT, BF16), [SMEM] + [VMEM] * 7, VMEM, after=(sums,), cost=1)(
        j, coup, block, h, ub, west, south, basis
    )
    from_east = along(to_west, "col", -1)
    shares = call(
        columns_kernel,
        (shape(16, F32),) * 4,
        [SMEM, SMEM] + [VMEM] * 5,
        (VMEM,) * 4,
        [pltpu.VMEM((4, 19, RHS), F32), pltpu.VMEM((48, RHS), F32), pltpu.VMEM((4, 16, RHS), F32)],
        after=(to_west,),
    )(i, j, *blocks, e)
    kept = call(kept_kernel, shape(2 * FACE, F32), [VMEM] * 6, VMEM, after=(shares[0],), cost=30)(
        coup, block, h, ub, west, south
    )
    blocks = [shares[0]] + [exchanged(shares[k], "row", 4, k) for k in (1, 2, 3)]
    z, currents = final(i, blocks, kept, from_east, from_north, w, basis)
    return x[None, None], z[None, None], currents


def solution(mesh):
    return jax.shard_map(
        local,
        mesh=mesh,
        in_specs=(
            P("row", "col", None, None),
            P("row", "col", None, None, None),
            P("row", "col", None, None),
            P("row", "col", None, None),
            P("row", "col", None, None),
            P("row", "col", None, None),
            P("row", "col", None, None),
            P(),
            P(),
            P("row", "col", None, None),
        ),
        out_specs=(P("row", "col", None, None), P("row", "col", None, None, None), P()),
        check_vma=False,
    )
```

```python
import jax
import jax.numpy as jnp
from jax import lax
from jax.experimental import pallas as pl
from jax.experimental.pallas import tpu as pltpu
from jax.sharding import PartitionSpec as P

FACE = 512
RHS = 512
INTERIOR = 1024
NTERM = 4
ROWS = 16
COLS = 8
SENT = FACE + 16
HIGHEST = lax.Precision.HIGHEST
F32 = jnp.float32
BF16 = jnp.bfloat16
VMEM = pl.BlockSpec(memory_space=pltpu.VMEM)
SMEM = pl.BlockSpec(memory_space=pltpu.SMEM)
ANY = pl.BlockSpec(memory_space=pl.ANY)


def mm(a, b):
    return jnp.dot(a, b, preferred_element_type=F32)


def mm_nt(a, b):
    return lax.dot_general(a, b, (((1,), (1,)), ((), ())), preferred_element_type=F32)


def mm_tn(a, b):
    return lax.dot_general(a, b, (((0,), (0,)), ((), ())), preferred_element_type=F32)


def two_terms(a):
    high = a.astype(BF16)
    low = (a - high.astype(F32)).astype(BF16)
    return jnp.concatenate([high, low], axis=0)


def folded(a):
    half = a.shape[0] // 2
    return a[:half] + a[half:]


def column(row):
    return jnp.transpose(jnp.broadcast_to(row, (8, row.shape[1])))[:, :1]


def call(kernel, outs, in_specs, out_specs, scratch=(), after=(), through=None, vmem=16, cost=0):
    n = len(in_specs)
    several = isinstance(outs, tuple)
    outs, out_specs = (outs, out_specs) if several else ((outs,), (out_specs,))
    extra = list(after)
    aliases = {}
    if through is not None:
        aliases = {n + len(extra): len(outs)}
        extra.append(through)
        outs = (*outs, jax.ShapeDtypeStruct(through.shape, through.dtype))
        out_specs = (*out_specs, ANY)
    m = len(outs) - len(aliases)

    def body(*refs):
        rest = refs[n + len(extra) :]
        kernel(*refs[:n], *rest[:m], *rest[len(outs) :])

    run = pl.pallas_call(
        body,
        name=kernel.__name__,
        out_shape=outs,
        in_specs=list(in_specs) + [ANY] * len(extra),
        out_specs=out_specs,
        scratch_shapes=list(scratch),
        input_output_aliases=aliases,
        compiler_params=pltpu.CompilerParams(vmem_limit_bytes=vmem << 20),
        cost_estimate=pl.CostEstimate(flops=1000 + cost * 1_000_000_000, bytes_accessed=1000 + cost * 3_000_000, transcendentals=0),
    )

    def made(*args):
        result = run(*args, *extra)
        return result if several or aliases else result[0]

    return made


def shape(rows, kind, columns=RHS):
    return jax.ShapeDtypeStruct((rows, columns), kind)


def north_kernel(pos, faces, weights, out, face, w, sem):
    parts, rows = 4, FACE // 4
    get_w = pltpu.make_async_copy(weights, w, sem.at[parts])
    get_w.start()
    copies = [
        pltpu.make_async_copy(faces.at[1, pl.ds(c * rows, rows)], face.at[pl.ds(c * rows, rows)], sem.at[c])
        for c in range(parts)
    ]
    for copy in copies:
        copy.start()
    get_w.wait()
    keep = (pos[0] < ROWS - 1).astype(F32)
    scale = (1.0 - column(w[1:2, :])) * keep
    for c, copy in enumerate(copies):
        copy.wait()
        at = slice(c * rows, (c + 1) * rows)
        out[at] = (scale[at] * face[at]).astype(BF16)


def north_face(i, faces, w):
    return call(
        north_kernel,
        shape(FACE, BF16),
        [SMEM, ANY, ANY],
        VMEM,
        [pltpu.VMEM((FACE, RHS), F32), pltpu.VMEM((2, FACE), F32), pltpu.SemaphoreType.DMA((5,))],
        vmem=52,
        cost=4,
    )(i, faces, w)


def east_kernel(pos, faces, w, out, own):
    keep = (pos[0] < COLS - 1).astype(F32)
    c = column(w[0:1, :])
    out[...] = ((1.0 - c) * keep * faces[0]).astype(BF16)
    own[:FACE] = (c * faces[0]).astype(BF16)
    own[FACE:] = (column(w[1:2, :]) * faces[1]).astype(BF16)


def east_face(j, faces, w, after):
    return call(east_kernel, (shape(FACE, BF16), shape(2 * FACE, BF16)), [SMEM, VMEM, VMEM], (VMEM, VMEM), after=after, cost=4)(j, faces, w)


def table_kernel(i, j, cm, cmv, cinv, out, rows, lat):
    n_i, n_j = ROWS, COLS
    corners = cinv.shape[0]
    own_j = j[0]
    east_j = jnp.minimum(own_j + 1, n_j - 1)
    rows[...] = jnp.zeros_like(rows)
    for y in range(4):
        own_i = 4 * y + lax.rem(i[0], 4)
        north_i = jnp.minimum(own_i + 1, n_i - 1)
        for g, (a, b) in enumerate(((own_i, own_j), (own_i, east_j), (north_i, own_j))):
            for c in range(4):
                n = 16 * y + 4 * g + c
                rows[n : n + 1] = cinv[pl.ds(cm[4 * b + c, a], 1), :]
    ids = cmv[...].astype(F32)
    at = lax.broadcasted_iota(jnp.int32, (4 * n_j, n_j + 1), 0)
    col = lax.broadcasted_iota(jnp.int32, (4 * n_j, n_j + 1), 1)
    first = (at == jnp.where(col == n_j, 4 * n_j - 3, 4 * col)).astype(F32)
    last = (at == jnp.where(col == n_j, 4 * n_j - 1, 4 * col + 2)).astype(F32)
    flip = lambda s: lax.dot_general(ids, s, (((0,), (0,)), ((), ())), precision=HIGHEST, preferred_element_type=F32)
    lat[0:n_i] = flip(first)
    lat[n_i : n_i + 1] = flip(last)[n_i - 1 : n_i]
    base = 4 * lax.div(i[0], 4)
    line = jnp.concatenate([lat[pl.ds(base + a, 1), :] for a in range(5)], axis=1)
    slots = lax.broadcasted_iota(jnp.int32, (corners, 5 * (n_j + 1)), 0).astype(F32)
    out[:, :45] = jnp.dot(rows[...], (slots == line).astype(F32), precision=HIGHEST, preferred_element_type=F32)
    out[:, 45:] = jnp.zeros((64, 3), F32)


def table(i, j, corner_map, coarse_inv, after):
    cm = corner_map.transpose(1, 2, 0).reshape(4 * COLS, ROWS)
    return call(
        table_kernel,
        jax.ShapeDtypeStruct((64, 48), F32),
        [SMEM, SMEM, SMEM, VMEM, VMEM],
        VMEM,
        [pltpu.VMEM((64, coarse_inv.shape[0]), F32), pltpu.VMEM((24, COLS + 1), F32)],
        after=after,
    )(i, j, cm, cm, coarse_inv)


def early_a_kernel(coup, r, own, basis, contact, p, g, bt):
    labels = lax.broadcasted_iota(jnp.int32, (NTERM, FACE), 0) + 1
    marks = jnp.concatenate([(contact[f : f + 1, :] == labels).astype(F32) for f in range(4)], axis=1)
    bt[...] = jnp.concatenate([basis[...].astype(F32), marks], axis=0).astype(BF16)
    g[...] = mm_nt(bt[...], coup[...])
    for c in range(2):
        at = slice(512 * c, 512 * c + 512)
        p[at] = r[at] - mm(coup[at, : 2 * FACE], own[...])


def early_b_kernel(g, inv, coup, r, k, q):
    m = folded(mm(two_terms(g[...]), inv[...]))
    m2 = two_terms(m)
    k[...] = -folded(mm(m2, coup[...]))
    high = r[...].astype(BF16)
    low = (r[...] - high.astype(F32)).astype(BF16)
    q[...] = folded(mm(m2, high)) + mm(m2[:8], low)


def early_c_kernel(bt, block, own, k, qr, coup, p, west, h, q, k_out, p_out):
    own_n, with_west = 2 * FACE, 3 * FACE
    k2 = two_terms(k[...] + mm(bt[...], block[...]))
    for c in range(4):
        at = slice(512 * c, 512 * c + 512)
        h[at] = mm(block[at, :own_n], own[...]) + mm(block[at, own_n:with_west], west[...])
    for c in range(2):
        at = slice(512 * c, 512 * c + 512)
        p_out[at] = p[at] - mm(coup[at, own_n:with_west], west[...])
    q[...] = qr[...] + folded(mm(k2[:, :own_n], own[...]) + mm(k2[:, own_n:with_west], west[...]))
    k_out[...] = k2[:, with_west:]


def corner_kernel(q, k, south, out):
    out[...] = q[...] + folded(mm(k[...], south[...]))


def inner_kernel(coup, p, south, t):
    for c in range(2):
        at = slice(c * 512, (c + 1) * 512)
        t[at] = (p[at] - mm(coup[at, 3 * FACE :], south[...])).astype(BF16)


def interior_kernel(inv, t, x_h, ub, xbuf, sem):
    rows = 512
    copies = []
    for c in range(2):
        at = slice(c * rows, (c + 1) * rows)
        x = mm(inv[at], t[...])
        xbuf[at] = x
        ub[at] = x.astype(BF16)
        copies.append(pltpu.make_async_copy(xbuf.at[pl.ds(c * rows, rows)], x_h.at[pl.ds(c * rows, rows)], sem.at[c]))
        copies[c].start()
    for copy in copies:
        copy.wait()


def result(f, coup, block, h, ub, south):
    at = slice(f * FACE, (f + 1) * FACE)
    return h[at] + mm(block[at, 3 * FACE :], south[...]) + mm_tn(coup[:, at], ub[...])


def sent_face(f, pos, coup, block, h, ub, south, basis, sent):
    keep = (pos[0] > 0).astype(F32)
    sent[:FACE] = (result(f, coup, block, h, ub, south) * keep).astype(BF16)
    rows = basis[:, f * FACE : (f + 1) * FACE].astype(F32)
    sent[FACE:] = (jnp.concatenate([rows, jnp.zeros((12, FACE), F32)], axis=0) * keep).astype(BF16)


def south_kernel(*refs):
    sent_face(3, *refs)


def west_kernel(*refs):
    sent_face(2, *refs)


def kept_east_kernel(coup, block, h, ub, south, kept):
    kept[...] = result(0, coup, block, h, ub, south)


def kept_north_kernel(coup, block, h, ub, south, kept):
    kept[...] = result(1, coup, block, h, ub, south)


def ordered(bit, mine, theirs):
    first = bit == 0
    a, b = mine[...], theirs[...]
    return jnp.where(first, a, b), jnp.where(first, b, a)


def side_by_side(low, high, rows, m, out):
    n = 2 * m - 1
    for r in range(rows):
        out[n * r : n * r + m - 1] = low[m * r : m * r + m - 1]
        out[n * r + m - 1 : n * r + m] = low[m * r + m - 1 : m * r + m] + high[m * r : m * r + 1]
        out[n * r + m : n * r + n] = high[m * r + 1 : m * r + m]
    return low[m * rows : m * rows + 4] + high[m * rows : m * rows + 4]


def above(low, high, rows, m, out):
    n = (rows - 1) * m
    out[0:n] = low[0:n]
    out[n : n + m] = low[n : n + m] + high[0:m]
    out[n + m : 2 * n + m] = high[m : m + n]
    out[2 * n + m : 2 * n + m + 4] = low[n + m : n + m + 4] + high[n + m : n + m + 4]


def core_kernel(pos, mine, theirs, out):
    low, high = ordered(lax.rem(pos[0], 2), mine, theirs)
    out[6:10] = side_by_side(low, high, 2, 2, out)


def z1_kernel(pos, mine, theirs, out):
    low, high = ordered(lax.rem(pos[0], 2), mine, theirs)
    above(low, high, 2, 3, out)


def z2_kernel(pos, mine, theirs, out):
    low, high = ordered(lax.rem(lax.div(pos[0], 2), 2), mine, theirs)
    above(low, high, 3, 3, out)


def x1_kernel(pos, mine, theirs, out):
    low, high = ordered(lax.rem(lax.div(pos[0], 2), 2), mine, theirs)
    out[25:29] = side_by_side(low, high, 5, 3, out)


def x2_kernel(i, j, mine, theirs, e, o0, o1, o2, o3, full, shares):
    low, high = ordered(lax.div(j[0], 4), mine, theirs)
    total = side_by_side(low, high, 5, 5, full)
    full[45:] = jnp.zeros((3, RHS), F32)
    e2, q2 = two_terms(e[...]), two_terms(full[...])
    all_shares = folded(mm(e2, q2[:48])) + mm(e2[:64], q2[48:])
    for y in range(4):
        shares[y] = all_shares[16 * y : 16 * y + 16]
        shares[y, 12:16] = total
    at = lax.div(i[0], 4)
    for k, out in enumerate((o0, o1, o2, o3)):
        out[...] = shares[at ^ k]


def joined(kernel, at, mine, theirs, rows, after):
    return call(kernel, shape(rows, F32), [SMEM, VMEM, VMEM], VMEM, after=after)(at, mine, theirs)


def placed(at, blocks, slots):
    for k, block in enumerate(blocks):
        slots[at ^ k] = block[...]


def summed(slots, n):
    return (slots[0, n : n + 4] + slots[1, n : n + 4]) + (slots[2, n : n + 4] + slots[3, n : n + 4])


def final_kernel(pos, b0, b1, b2, b3, kept_e, kept_n, from_east, from_north, w, basis, z, cur, slots, zbuf, sem):
    placed(lax.div(pos[0], 4), (b0, b1, b2, b3), slots)
    cur[...] = summed(slots, 12) / FACE
    cc = (slots[0] + slots[1]) + (slots[2] + slots[3])
    copies = []
    for f, (kept, got) in enumerate(((kept_e, from_east), (kept_n, from_north))):
        wr = w[f : f + 1, :]
        mine = basis[:, f * FACE : (f + 1) * FACE].astype(F32) * wr
        other = got[FACE:].astype(F32)[:4] * (1.0 - wr)
        x = jnp.concatenate([mine, other], axis=0)
        c = jnp.concatenate([cc[0:4], cc[4 + 4 * f : 8 + 4 * f]], axis=0)
        xh, ch = x.astype(BF16).astype(F32), c.astype(BF16).astype(F32)
        pad = jnp.zeros((8, RHS), F32)
        left = jnp.concatenate([xh, x - xh, xh, pad], axis=0).astype(BF16)
        right = jnp.concatenate([ch, ch, c - ch, pad], axis=0).astype(BF16)
        wc = column(wr)
        for n in range(2):
            rows = slice(n * 256, (n + 1) * 256)
            part = wc[rows] * kept[rows] + (1.0 - wc[rows]) * got[rows].astype(F32)
            zbuf[f, rows] = part + mm_tn(left[:, rows], right)
            here = pl.ds(n * 256, 256)
            copy = pltpu.make_async_copy(zbuf.at[f, here], z.at[f, here], sem.at[2 * f + n])
            copy.start()
            copies.append(copy)
    for copy in copies:
        copy.wait()


def final(at, blocks, kept_e, kept_n, from_east, from_north, w, basis):
    return call(
        final_kernel,
        (jax.ShapeDtypeStruct((2, FACE, RHS), F32), shape(NTERM, F32)),
        [SMEM] + [VMEM] * 10,
        (ANY, VMEM),
        [
            pltpu.VMEM((4, 16, RHS), F32),
            pltpu.VMEM((2, FACE, RHS), F32),
            pltpu.SemaphoreType.DMA((4,)),
        ],
    )(at, *blocks, kept_e, kept_n, from_east, from_north, w, basis)


def along(x, axis, d):
    n = lax.axis_size(axis)
    return lax.ppermute(x, axis, [(s, (s + d) % n) for s in range(n)])


def exchanged(x, axis, stride, k):
    return lax.ppermute(x, axis, [(d ^ (k * stride), d) for d in range(lax.axis_size(axis))])


def local(
    interior_residual,
    interface_residual,
    owner_face_weight,
    interior_inverse_block,
    coupling,
    interface_block,
    corner_trace_basis,
    coarse_inv,
    corner_map,
    contact,
):
    i = lax.axis_index("row").astype(jnp.int32).reshape(1)
    j = lax.axis_index("col").astype(jnp.int32).reshape(1)
    faces_in = interface_residual[0, 0]
    r = interior_residual[0, 0]
    w = owner_face_weight[0, 0]
    inv, coup, block = interior_inverse_block[0, 0], coupling[0, 0], interface_block[0, 0]
    basis = corner_trace_basis[0, 0]

    to_north = north_face(i, faces_in, w)
    south = along(to_north, "row", 1)
    to_east, own = east_face(j, faces_in, w, (to_north,))
    west = along(to_east, "col", 1)
    e = table(i, j, corner_map, coarse_inv, (own,))
    p, g, bt = call(
        early_a_kernel,
        (shape(INTERIOR, F32), shape(8, F32, INTERIOR), shape(8, BF16, 4 * FACE)),
        [VMEM] * 5,
        (VMEM,) * 3,
        after=(e,),
        cost=10,
    )(coup, r, own, basis, contact[0, 0])
    k, q = call(early_b_kernel, (shape(8, F32, 4 * FACE), shape(8, F32)), [VMEM] * 4, (VMEM,) * 2, cost=10)(g, inv, coup, r)
    h, q, k, p = call(
        early_c_kernel,
        (shape(4 * FACE, F32), shape(8, F32), shape(16, BF16, FACE), shape(INTERIOR, F32)),
        [VMEM] * 8,
        (VMEM,) * 4,
        cost=10,
    )(bt, block, own, k, q, coup, p, west)

    sums = call(corner_kernel, shape(8, F32), [VMEM] * 3, VMEM)(q, k, south)
    other = lax.ppermute(sums, "col", [(s, s ^ 1) for s in range(COLS)])
    t = call(inner_kernel, shape(INTERIOR, BF16), [VMEM] * 3, VMEM, after=(sums,), cost=1)(coup, p, south)
    sums = joined(core_kernel, j, sums, other, 10, (t,))

    other = exchanged(sums, "row", 1, 1)
    x, ub = call(
        interior_kernel,
        (shape(INTERIOR, F32), shape(INTERIOR, BF16)),
        [VMEM] * 2,
        (ANY, VMEM),
        [pltpu.VMEM((INTERIOR, RHS), F32), pltpu.SemaphoreType.DMA((2,))],
        after=(sums,),
        cost=2,
    )(inv, t)
    sums = joined(z1_kernel, i, sums, other, 13, (ub,))

    other = exchanged(sums, "row", 1, 2)
    to_south = call(south_kernel, shape(SENT, BF16), [SMEM] + [VMEM] * 6, VMEM, after=(sums,), cost=1)(
        i, coup, block, h, ub, south, basis
    )
    from_north = along(to_south, "row", -1)
    sums = joined(z2_kernel, i, sums, other, 19, (to_south,))

    other = exchanged(sums, "col", 2, 1)
    to_west = call(west_kernel, shape(SENT, BF16), [SMEM] + [VMEM] * 6, VMEM, after=(sums,), cost=1)(
        j, coup, block, h, ub, south, basis
    )
    from_east = along(to_west, "col", -1)
    sums = joined(x1_kernel, j, sums, other, 29, (to_west,))

    other = exchanged(sums, "col", 2, 2)
    kept_e = call(kept_east_kernel, shape(FACE, F32), [VMEM] * 5, VMEM, after=(sums,), cost=10)(coup, block, h, ub, south)
    shares = call(
        x2_kernel,
        (shape(16, F32),) * 4,
        [SMEM, SMEM] + [VMEM] * 3,
        (VMEM,) * 4,
        [pltpu.VMEM((48, RHS), F32), pltpu.VMEM((4, 16, RHS), F32)],
        after=(kept_e,),
    )(i, j, sums, other, e)
    blocks = [shares[0]] + [exchanged(shares[k], "row", 4, k) for k in (1, 2, 3)]
    kept_n = call(kept_north_kernel, shape(FACE, F32), [VMEM] * 5, VMEM, after=(shares[0],), cost=30)(coup, block, h, ub, south)
    z, currents = final(i, blocks, kept_e, kept_n, from_east, from_north, w, basis)
    return x[None, None], z[None, None], currents


def solution(mesh):
    return jax.shard_map(
        local,
        mesh=mesh,
        in_specs=(
            P("row", "col", None, None),
            P("row", "col", None, None, None),
            P("row", "col", None, None),
            P("row", "col", None, None),
            P("row", "col", None, None),
            P("row", "col", None, None),
            P("row", "col", None, None),
            P(),
            P(),
            P("row", "col", None, None),
        ),
        out_specs=(P("row", "col", None, None), P("row", "col", None, None, None), P()),
        check_vma=False,
    )
```

```python
import jax
import jax.numpy as jnp
from jax import lax
from jax.experimental import pallas as pl
from jax.experimental.pallas import tpu as pltpu
from jax.sharding import PartitionSpec as P

FACE = 512
RHS = 512
INTERIOR = 1024
NTERM = 4
ROWS = 16
COLS = 8
SENT = FACE + 16
HIGHEST = lax.Precision.HIGHEST
F32 = jnp.float32
BF16 = jnp.bfloat16
VMEM = pl.BlockSpec(memory_space=pltpu.VMEM)
SMEM = pl.BlockSpec(memory_space=pltpu.SMEM)
ANY = pl.BlockSpec(memory_space=pl.ANY)


def mm(a, b):
    return jnp.dot(a, b, preferred_element_type=F32)


def mm_nt(a, b):
    return lax.dot_general(a, b, (((1,), (1,)), ((), ())), preferred_element_type=F32)


def mm_tn(a, b):
    return lax.dot_general(a, b, (((0,), (0,)), ((), ())), preferred_element_type=F32)


def two_terms(a):
    high = a.astype(BF16)
    low = (a - high.astype(F32)).astype(BF16)
    return jnp.concatenate([high, low], axis=0)


def folded(a):
    half = a.shape[0] // 2
    return a[:half] + a[half:]


def column(row):
    return jnp.transpose(jnp.broadcast_to(row, (8, row.shape[1])))[:, :1]


def call(kernel, outs, in_specs, out_specs, scratch=(), after=(), through=None, vmem=16, cost=0):
    n = len(in_specs)
    several = isinstance(outs, tuple)
    outs, out_specs = (outs, out_specs) if several else ((outs,), (out_specs,))
    extra = list(after)
    aliases = {}
    if through is not None:
        aliases = {n + len(extra): len(outs)}
        extra.append(through)
        outs = (*outs, jax.ShapeDtypeStruct(through.shape, through.dtype))
        out_specs = (*out_specs, ANY)
    m = len(outs) - len(aliases)

    def body(*refs):
        rest = refs[n + len(extra) :]
        kernel(*refs[:n], *rest[:m], *rest[len(outs) :])

    run = pl.pallas_call(
        body,
        name=kernel.__name__,
        out_shape=outs,
        in_specs=list(in_specs) + [ANY] * len(extra),
        out_specs=out_specs,
        scratch_shapes=list(scratch),
        input_output_aliases=aliases,
        compiler_params=pltpu.CompilerParams(vmem_limit_bytes=vmem << 20),
        cost_estimate=pl.CostEstimate(flops=1000 + cost * 1_000_000_000, bytes_accessed=1000 + cost * 3_000_000, transcendentals=0),
    )

    def made(*args):
        result = run(*args, *extra)
        return result if several or aliases else result[0]

    return made


def shape(rows, kind, columns=RHS):
    return jax.ShapeDtypeStruct((rows, columns), kind)


def north_kernel(pos, faces, weights, out, face, w, sem):
    parts, rows = 4, FACE // 4
    get_w = pltpu.make_async_copy(weights, w, sem.at[parts])
    get_w.start()
    copies = [
        pltpu.make_async_copy(faces.at[1, pl.ds(c * rows, rows)], face.at[pl.ds(c * rows, rows)], sem.at[c])
        for c in range(parts)
    ]
    for copy in copies:
        copy.start()
    get_w.wait()
    keep = (pos[0] < ROWS - 1).astype(F32)
    scale = (1.0 - column(w[1:2, :])) * keep
    for c, copy in enumerate(copies):
        copy.wait()
        at = slice(c * rows, (c + 1) * rows)
        out[at] = (scale[at] * face[at]).astype(BF16)


def north_face(i, faces, w):
    return call(
        north_kernel,
        shape(FACE, BF16),
        [SMEM, ANY, ANY],
        VMEM,
        [pltpu.VMEM((FACE, RHS), F32), pltpu.VMEM((2, FACE), F32), pltpu.SemaphoreType.DMA((5,))],
        vmem=52,
        cost=4,
    )(i, faces, w)


def east_kernel(pos, faces, w, out, own):
    keep = (pos[0] < COLS - 1).astype(F32)
    c = column(w[0:1, :])
    out[...] = ((1.0 - c) * keep * faces[0]).astype(BF16)
    own[:FACE] = (c * faces[0]).astype(BF16)
    own[FACE:] = (column(w[1:2, :]) * faces[1]).astype(BF16)


def east_face(j, faces, w, after):
    return call(east_kernel, (shape(FACE, BF16), shape(2 * FACE, BF16)), [SMEM, VMEM, VMEM], (VMEM, VMEM), after=after, cost=4)(j, faces, w)


def table_kernel(i, j, cm, cmv, cinv, out, rows, lat):
    n_i, n_j = ROWS, COLS
    corners = cinv.shape[0]
    own_j = j[0]
    east_j = jnp.minimum(own_j + 1, n_j - 1)
    rows[...] = jnp.zeros_like(rows)
    for y in range(4):
        own_i = 4 * y + lax.rem(i[0], 4)
        north_i = jnp.minimum(own_i + 1, n_i - 1)
        for g, (a, b) in enumerate(((own_i, own_j), (own_i, east_j), (north_i, own_j))):
            for c in range(4):
                n = 16 * y + 4 * g + c
                rows[n : n + 1] = cinv[pl.ds(cm[4 * b + c, a], 1), :]
    ids = cmv[...].astype(F32)
    at = lax.broadcasted_iota(jnp.int32, (4 * n_j, n_j + 1), 0)
    col = lax.broadcasted_iota(jnp.int32, (4 * n_j, n_j + 1), 1)
    first = (at == jnp.where(col == n_j, 4 * n_j - 3, 4 * col)).astype(F32)
    last = (at == jnp.where(col == n_j, 4 * n_j - 1, 4 * col + 2)).astype(F32)
    flip = lambda s: lax.dot_general(ids, s, (((0,), (0,)), ((), ())), precision=HIGHEST, preferred_element_type=F32)
    lat[0:n_i] = flip(first)
    lat[n_i : n_i + 1] = flip(last)[n_i - 1 : n_i]
    base = 4 * lax.div(i[0], 4)
    line = jnp.concatenate([lat[pl.ds(base + a, 1), :] for a in range(5)], axis=1)
    slots = lax.broadcasted_iota(jnp.int32, (corners, 5 * (n_j + 1)), 0).astype(F32)
    out[:, :45] = jnp.dot(rows[...], (slots == line).astype(F32), precision=HIGHEST, preferred_element_type=F32)
    out[:, 45:] = jnp.zeros((64, 3), F32)


def table(i, j, corner_map, coarse_inv, after):
    cm = corner_map.transpose(1, 2, 0).reshape(4 * COLS, ROWS)
    return call(
        table_kernel,
        jax.ShapeDtypeStruct((64, 48), F32),
        [SMEM, SMEM, SMEM, VMEM, VMEM],
        VMEM,
        [pltpu.VMEM((64, coarse_inv.shape[0]), F32), pltpu.VMEM((24, COLS + 1), F32)],
        after=after,
    )(i, j, cm, cm, coarse_inv)


def early_a_kernel(coup, r, own, basis, contact, p, g, bt):
    labels = lax.broadcasted_iota(jnp.int32, (NTERM, FACE), 0) + 1
    marks = jnp.concatenate([(contact[f : f + 1, :] == labels).astype(F32) for f in range(4)], axis=1)
    bt[...] = jnp.concatenate([basis[...].astype(F32), marks], axis=0).astype(BF16)
    g[...] = mm_nt(bt[...], coup[...])
    for c in range(2):
        at = slice(512 * c, 512 * c + 512)
        p[at] = r[at] - mm(coup[at, : 2 * FACE], own[...])


def early_b_kernel(g, inv, coup, r, k, q):
    m = folded(mm(two_terms(g[...]), inv[...]))
    m2 = two_terms(m)
    k[...] = -folded(mm(m2, coup[...]))
    high = r[...].astype(BF16)
    low = (r[...] - high.astype(F32)).astype(BF16)
    q[...] = folded(mm(m2, high)) + mm(m2[:8], low)


def early_c_kernel(bt, block, own, k, qr, h, q, k_out):
    k2 = two_terms(k[...] + mm(bt[...], block[...]))
    q[...] = qr[...] + folded(mm(k2[:, : 2 * FACE], own[...]))
    k_out[...] = k2[:, 2 * FACE :]
    for c in range(4):
        at = slice(512 * c, 512 * c + 512)
        h[at] = mm(block[at, : 2 * FACE], own[...])


def west_terms_kernel(coup, block, p, h, q, k, west, p_out, h_out, q_out):
    own_n, with_west = 2 * FACE, 3 * FACE
    for c in range(2):
        at = slice(512 * c, 512 * c + 512)
        p_out[at] = p[at] - mm(coup[at, own_n:with_west], west[...])
    for c in range(4):
        at = slice(512 * c, 512 * c + 512)
        h_out[at] = h[at] + mm(block[at, own_n:with_west], west[...])
    q_out[...] = q[...] + folded(mm(k[:, :FACE], west[...]))


def corner_kernel(q, k, south, out):
    out[...] = q[...] + folded(mm(k[:, FACE:], south[...]))


def inner_kernel(coup, p, south, t):
    for c in range(2):
        at = slice(c * 512, (c + 1) * 512)
        t[at] = (p[at] - mm(coup[at, 3 * FACE :], south[...])).astype(BF16)


def result(f, coup, block, h, ub, south):
    at = slice(f * FACE, (f + 1) * FACE)
    return h[at] + mm(block[at, 3 * FACE :], south[...]) + mm_tn(coup[:, at], ub[...])


def tail(basis, f, keep):
    rows = basis[:, f * FACE : (f + 1) * FACE].astype(F32)
    return (jnp.concatenate([rows, jnp.zeros((12, FACE), F32)], axis=0) * keep).astype(BF16)


def solve_kernel(pos, coup, inv, block, t, h, south, basis, x_h, sent, ub, xbuf, sem):
    rows = 512
    copies = []
    for c in range(2):
        at = slice(c * rows, (c + 1) * rows)
        x = mm(inv[at], t[...])
        xbuf[at] = x
        ub[at] = x.astype(BF16)
        copies.append(pltpu.make_async_copy(xbuf.at[pl.ds(c * rows, rows)], x_h.at[pl.ds(c * rows, rows)], sem.at[c]))
        copies[c].start()
    keep = (pos[0] > 0).astype(F32)
    sent[:FACE] = (result(3, coup, block, h, ub, south) * keep).astype(BF16)
    sent[FACE:] = tail(basis, 3, keep)
    for copy in copies:
        copy.wait()


def west_kernel(pos, coup, block, h, ub, south, basis, sent):
    keep = (pos[0] > 0).astype(F32)
    sent[:FACE] = (result(2, coup, block, h, ub, south) * keep).astype(BF16)
    sent[FACE:] = tail(basis, 2, keep)


def kept_kernel(coup, block, h, ub, south, kept):
    for f in range(2):
        kept[f * FACE : (f + 1) * FACE] = result(f, coup, block, h, ub, south)


def pair_kernel(pos, mine, theirs, out):
    first = lax.rem(pos[0], 2) == 0
    a, b = mine[...], theirs[...]
    low = jnp.where(first, a, b)
    high = jnp.where(first, b, a)
    for r in range(2):
        out[3 * r : 3 * r + 1] = low[2 * r : 2 * r + 1]
        out[3 * r + 1 : 3 * r + 2] = low[2 * r + 1 : 2 * r + 2] + high[2 * r : 2 * r + 1]
        out[3 * r + 2 : 3 * r + 3] = high[2 * r + 1 : 2 * r + 2]
    out[6:10] = low[4:8] + high[4:8]


def placed(at, blocks, slots):
    for k, block in enumerate(blocks):
        slots[at ^ k] = block[...]


def summed(slots, n):
    return (slots[0, n : n + 4] + slots[1, n : n + 4]) + (slots[2, n : n + 4] + slots[3, n : n + 4])


def rows_kernel(pos, b0, b1, b2, b3, out, slots):
    placed(lax.rem(pos[0], 4), (b0, b1, b2, b3), slots)
    out[0:3] = slots[0, 0:3]
    for b in range(1, 4):
        out[3 * b : 3 * b + 3] = slots[b - 1, 3:6] + slots[b, 0:3]
    out[12:15] = slots[3, 3:6]
    out[15:19] = summed(slots, 6)


def columns_kernel(i, j, b0, b1, b2, b3, e, o0, o1, o2, o3, slots, full, shares):
    placed(lax.div(j[0], 2), (b0, b1, b2, b3), slots)
    full[40:] = jnp.zeros((8, RHS), F32)
    for r in range(5):
        for c in range(9):
            b = min(c // 2, 3)
            n = 3 * r + c - 2 * b
            row = slots[b, n : n + 1]
            if c % 2 == 0 and 0 < c < 8:
                row = slots[b - 1, 3 * r + 2 : 3 * r + 3] + row
            full[9 * r + c : 9 * r + c + 1] = row
    e2, q2 = two_terms(e[...]), two_terms(full[...])
    all_shares = folded(mm(e2, q2[:48])) + mm(e2[:64], q2[48:])
    total = summed(slots, 15)
    for y in range(4):
        shares[y] = all_shares[16 * y : 16 * y + 16]
        shares[y, 12:16] = total
    at = lax.div(i[0], 4)
    for k, out in enumerate((o0, o1, o2, o3)):
        out[...] = shares[at ^ k]


def final_kernel(pos, b0, b1, b2, b3, kept, from_east, from_north, w, basis, z, cur, slots, zbuf, sem):
    placed(lax.div(pos[0], 4), (b0, b3, b2, b1), slots)
    cur[...] = summed(slots, 12) / FACE
    cc = (slots[0] + slots[1]) + (slots[2] + slots[3])
    copies = []
    for f, got in enumerate((from_east, from_north)):
        wr = w[f : f + 1, :]
        mine = basis[:, f * FACE : (f + 1) * FACE].astype(F32) * wr
        other = got[FACE:].astype(F32)[:4] * (1.0 - wr)
        x = jnp.concatenate([mine, other], axis=0)
        c = jnp.concatenate([cc[0:4], cc[4 + 4 * f : 8 + 4 * f]], axis=0)
        xh, ch = x.astype(BF16).astype(F32), c.astype(BF16).astype(F32)
        pad = jnp.zeros((8, RHS), F32)
        left = jnp.concatenate([xh, x - xh, xh, pad], axis=0).astype(BF16)
        right = jnp.concatenate([ch, ch, c - ch, pad], axis=0).astype(BF16)
        wc = column(wr)
        for n in range(2):
            rows = slice(n * 256, (n + 1) * 256)
            part = wc[rows] * kept[f * FACE + n * 256 : f * FACE + (n + 1) * 256] + (1.0 - wc[rows]) * got[rows].astype(F32)
            zbuf[f, rows] = part + mm_tn(left[:, rows], right)
            here = pl.ds(n * 256, 256)
            copy = pltpu.make_async_copy(zbuf.at[f, here], z.at[f, here], sem.at[2 * f + n])
            copy.start()
            copies.append(copy)
    for copy in copies:
        copy.wait()


def final(at, blocks, kept, from_east, from_north, w, basis):
    return call(
        final_kernel,
        (jax.ShapeDtypeStruct((2, FACE, RHS), F32), shape(NTERM, F32)),
        [SMEM] + [VMEM] * 9,
        (ANY, VMEM),
        [
            pltpu.VMEM((4, 16, RHS), F32),
            pltpu.VMEM((2, FACE, RHS), F32),
            pltpu.SemaphoreType.DMA((4,)),
        ],
    )(at, *blocks, kept, from_east, from_north, w, basis)


def along(x, axis, d):
    n = lax.axis_size(axis)
    return lax.ppermute(x, axis, [(s, (s + d) % n) for s in range(n)])


def exchanged(x, axis, stride, k):
    return lax.ppermute(x, axis, [(d ^ (k * stride), d) for d in range(lax.axis_size(axis))])


def four(x, axis, stride):
    far, middle, near = [exchanged(x, axis, stride, k) for k in (3, 2, 1)]
    return [x, near, middle, far]


def local(
    interior_residual,
    interface_residual,
    owner_face_weight,
    interior_inverse_block,
    coupling,
    interface_block,
    corner_trace_basis,
    coarse_inv,
    corner_map,
    contact,
):
    i = lax.axis_index("row").astype(jnp.int32).reshape(1)
    j = lax.axis_index("col").astype(jnp.int32).reshape(1)
    faces_in = interface_residual[0, 0]
    r = interior_residual[0, 0]
    w = owner_face_weight[0, 0]
    inv, coup, block = interior_inverse_block[0, 0], coupling[0, 0], interface_block[0, 0]
    basis = corner_trace_basis[0, 0]

    to_north = north_face(i, faces_in, w)
    south = along(to_north, "row", 1)
    to_east, own = east_face(j, faces_in, w, (to_north,))
    west = along(to_east, "col", 1)
    e = table(i, j, corner_map, coarse_inv, (own,))
    p, g, bt = call(
        early_a_kernel,
        (shape(INTERIOR, F32), shape(8, F32, INTERIOR), shape(8, BF16, 4 * FACE)),
        [VMEM] * 5,
        (VMEM,) * 3,
        after=(e,),
        cost=10,
    )(coup, r, own, basis, contact[0, 0])
    k, q = call(early_b_kernel, (shape(8, F32, 4 * FACE), shape(8, F32)), [VMEM] * 4, (VMEM,) * 2, cost=10)(g, inv, coup, r)
    h, q, k = call(
        early_c_kernel,
        (shape(4 * FACE, F32), shape(8, F32), shape(16, BF16, 2 * FACE)),
        [VMEM] * 5,
        (VMEM,) * 3,
        cost=10,
    )(bt, block, own, k, q)

    p, h, q = call(
        west_terms_kernel,
        (shape(INTERIOR, F32), shape(4 * FACE, F32), shape(8, F32)),
        [VMEM] * 7,
        (VMEM,) * 3,
        cost=2,
    )(coup, block, p, h, q, k, west)

    sums = call(corner_kernel, shape(8, F32), [VMEM] * 3, VMEM)(q, k, south)
    other = lax.ppermute(sums, "col", [(s, s ^ 1) for s in range(COLS)])
    t = call(inner_kernel, shape(INTERIOR, BF16), [VMEM] * 3, VMEM, after=(sums,), cost=1)(coup, p, south)
    sums = call(pair_kernel, shape(10, F32), [SMEM, VMEM, VMEM], VMEM, after=(t,))(j, sums, other)
    blocks = four(sums, "row", 1)
    x, to_south, ub = call(
        solve_kernel,
        (shape(INTERIOR, F32), shape(SENT, BF16), shape(INTERIOR, BF16)),
        [SMEM] + [VMEM] * 7,
        (ANY, VMEM, VMEM),
        [pltpu.VMEM((INTERIOR, RHS), F32), pltpu.SemaphoreType.DMA((2,))],
        after=(sums,),
        cost=4,
    )(i, coup, inv, block, t, h, south, basis)
    from_north = along(to_south, "row", -1)
    sums = call(
        rows_kernel, shape(19, F32), [SMEM] + [VMEM] * 4, VMEM, [pltpu.VMEM((4, 10, RHS), F32)], after=(to_south,)
    )(i, *blocks)
    blocks = four(sums, "col", 2)
    to_west = call(west_kernel, shape(SENT, BF16), [SMEM] + [VMEM] * 6, VMEM, after=(sums,), cost=1)(
        j, coup, block, h, ub, south, basis
    )
    from_east = along(to_west, "col", -1)
    shares = call(
        columns_kernel,
        (shape(16, F32),) * 4,
        [SMEM, SMEM] + [VMEM] * 5,
        (VMEM,) * 4,
        [pltpu.VMEM((4, 19, RHS), F32), pltpu.VMEM((48, RHS), F32), pltpu.VMEM((4, 16, RHS), F32)],
        after=(to_west,),
    )(i, j, *blocks, e)
    kept = call(kept_kernel, shape(2 * FACE, F32), [VMEM] * 5, VMEM, after=(shares[0],), cost=30)(
        coup, block, h, ub, south
    )
    far, middle, near = [exchanged(shares[k], "row", 4, k) for k in (3, 2, 1)]
    blocks = [shares[0], far, middle, near]
    z, currents = final(i, blocks, kept, from_east, from_north, w, basis)
    return x[None, None], z[None, None], currents


def solution(mesh):
    return jax.shard_map(
        local,
        mesh=mesh,
        in_specs=(
            P("row", "col", None, None),
            P("row", "col", None, None, None),
            P("row", "col", None, None),
            P("row", "col", None, None),
            P("row", "col", None, None),
            P("row", "col", None, None),
            P("row", "col", None, None),
            P(),
            P(),
            P("row", "col", None, None),
        ),
        out_specs=(P("row", "col", None, None), P("row", "col", None, None, None), P()),
        check_vma=False,
    )
```

```python
import jax
import jax.numpy as jnp
from jax import lax
from jax.experimental import pallas as pl
from jax.experimental.pallas import tpu as pltpu
from jax.sharding import PartitionSpec as P

FACE = 512
RHS = 512
INTERIOR = 1024
NTERM = 4
ROWS = 16
COLS = 8
SENT = FACE + 16
HIGHEST = lax.Precision.HIGHEST
F32 = jnp.float32
BF16 = jnp.bfloat16
VMEM = pl.BlockSpec(memory_space=pltpu.VMEM)
SMEM = pl.BlockSpec(memory_space=pltpu.SMEM)
ANY = pl.BlockSpec(memory_space=pl.ANY)


def mm(a, b):
    return jnp.dot(a, b, preferred_element_type=F32)


def mm_nt(a, b):
    return lax.dot_general(a, b, (((1,), (1,)), ((), ())), preferred_element_type=F32)


def mm_tn(a, b):
    return lax.dot_general(a, b, (((0,), (0,)), ((), ())), preferred_element_type=F32)


def two_terms(a):
    high = a.astype(BF16)
    low = (a - high.astype(F32)).astype(BF16)
    return jnp.concatenate([high, low], axis=0)


def folded(a):
    half = a.shape[0] // 2
    return a[:half] + a[half:]


def column(row):
    return jnp.transpose(jnp.broadcast_to(row, (8, row.shape[1])))[:, :1]


def call(kernel, outs, in_specs, out_specs, scratch=(), after=(), into=None, vmem=16, cost=0):
    n = len(in_specs)
    several = isinstance(outs, tuple)
    outs, out_specs = (outs, out_specs) if several else ((outs,), (out_specs,))
    extra = list(after)
    aliases = {}
    if into is not None:
        aliases = {n + len(extra): len(outs)}
        extra.append(into)
        outs = (*outs, jax.ShapeDtypeStruct(into.shape, into.dtype))
        out_specs = (*out_specs, ANY)

    def body(*refs):
        kernel(*refs[:n], *refs[n + len(extra) :])

    run = pl.pallas_call(
        body,
        name=kernel.__name__,
        out_shape=outs,
        in_specs=list(in_specs) + [ANY] * len(extra),
        out_specs=out_specs,
        scratch_shapes=list(scratch),
        input_output_aliases=aliases,
        compiler_params=pltpu.CompilerParams(vmem_limit_bytes=vmem << 20),
        cost_estimate=pl.CostEstimate(flops=1000 + cost * 1_000_000_000, bytes_accessed=1000 + cost * 3_000_000, transcendentals=0),
    )

    def made(*args):
        result = run(*args, *extra)
        return result if several or aliases else result[0]

    return made


def shape(rows, kind, columns=RHS):
    return jax.ShapeDtypeStruct((rows, columns), kind)


def load_kernel(faces, face, sem):
    copy = pltpu.make_async_copy(faces.at[1], face, sem)
    copy.start()
    copy.wait()


def north_kernel(pos, face, w, out):
    keep = (pos[0] < ROWS - 1).astype(F32)
    out[...] = ((1.0 - column(w[1:2, :])) * keep * face[...]).astype(BF16)


def north_face(i, faces, w):
    face = call(load_kernel, shape(FACE, F32), [ANY], VMEM, [pltpu.SemaphoreType.DMA(())], vmem=52, cost=4)(faces)
    return call(north_kernel, shape(FACE, BF16), [SMEM, VMEM, VMEM], VMEM)(i, face, w)


def east_kernel(pos, faces, w, out, own):
    keep = (pos[0] < COLS - 1).astype(F32)
    c = column(w[0:1, :])
    out[...] = ((1.0 - c) * keep * faces[0]).astype(BF16)
    own[:FACE] = (c * faces[0]).astype(BF16)
    own[FACE:] = (column(w[1:2, :]) * faces[1]).astype(BF16)


def east_face(j, faces, w, after):
    return call(east_kernel, (shape(FACE, BF16), shape(2 * FACE, BF16)), [SMEM, VMEM, VMEM], (VMEM, VMEM), after=after, cost=4)(j, faces, w)


def table_kernel(i, j, cm, cmv, cinv, out, rows, lat):
    n_i, n_j = ROWS, COLS
    corners = cinv.shape[0]
    own_j = j[0]
    east_j = jnp.minimum(own_j + 1, n_j - 1)
    rows[...] = jnp.zeros_like(rows)
    for y in range(4):
        own_i = 4 * y + lax.rem(i[0], 4)
        north_i = jnp.minimum(own_i + 1, n_i - 1)
        for g, (a, b) in enumerate(((own_i, own_j), (own_i, east_j), (north_i, own_j))):
            for c in range(4):
                n = 16 * y + 4 * g + c
                rows[n : n + 1] = cinv[pl.ds(cm[4 * b + c, a], 1), :]
    ids = cmv[...].astype(F32)
    at = lax.broadcasted_iota(jnp.int32, (4 * n_j, n_j + 1), 0)
    col = lax.broadcasted_iota(jnp.int32, (4 * n_j, n_j + 1), 1)
    first = (at == jnp.where(col == n_j, 4 * n_j - 3, 4 * col)).astype(F32)
    last = (at == jnp.where(col == n_j, 4 * n_j - 1, 4 * col + 2)).astype(F32)
    flip = lambda s: lax.dot_general(ids, s, (((0,), (0,)), ((), ())), precision=HIGHEST, preferred_element_type=F32)
    lat[0:n_i] = flip(first)
    lat[n_i : n_i + 1] = flip(last)[n_i - 1 : n_i]
    base = 4 * lax.div(i[0], 4)
    line = jnp.concatenate([lat[pl.ds(base + a, 1), :] for a in range(5)], axis=1)
    slots = lax.broadcasted_iota(jnp.int32, (corners, 5 * (n_j + 1)), 0).astype(F32)
    out[:, :45] = jnp.dot(rows[...], (slots == line).astype(F32), precision=HIGHEST, preferred_element_type=F32)
    out[:, 45:] = jnp.zeros((64, 3), F32)


def table(i, j, corner_map, coarse_inv, after):
    cm = corner_map.transpose(1, 2, 0).reshape(4 * COLS, ROWS)
    return call(
        table_kernel,
        jax.ShapeDtypeStruct((64, 48), F32),
        [SMEM, SMEM, SMEM, VMEM, VMEM],
        VMEM,
        [pltpu.VMEM((64, coarse_inv.shape[0]), F32), pltpu.VMEM((24, COLS + 1), F32)],
        after=after,
    )(i, j, cm, cm, coarse_inv)


def early_a_kernel(coup, r, own, basis, contact, p, g, bt):
    labels = lax.broadcasted_iota(jnp.int32, (NTERM, FACE), 0) + 1
    marks = jnp.concatenate([(contact[f : f + 1, :] == labels).astype(F32) for f in range(4)], axis=1)
    bt[...] = jnp.concatenate([basis[...].astype(F32), marks], axis=0).astype(BF16)
    g[...] = mm_nt(bt[...], coup[...])
    for c in range(2):
        at = slice(512 * c, 512 * c + 512)
        p[at] = r[at] - mm(coup[at, : 2 * FACE], own[...])


def early_b_kernel(g, inv, coup, r, k, q):
    m = folded(mm(two_terms(g[...]), inv[...]))
    m2 = two_terms(m)
    k[...] = -folded(mm(m2, coup[...]))
    high = r[...].astype(BF16)
    low = (r[...] - high.astype(F32)).astype(BF16)
    q[...] = folded(mm(m2, high)) + mm(m2[:8], low)


def early_c_kernel(bt, block, own, k, qr, h, q, k_out):
    k2 = two_terms(k[...] + mm(bt[...], block[...]))
    q[...] = qr[...] + folded(mm(k2[:, : 2 * FACE], own[...]))
    k_out[...] = k2[:, 2 * FACE :]
    for c in range(4):
        at = slice(512 * c, 512 * c + 512)
        h[at] = mm(block[at, : 2 * FACE], own[...])


def west_terms_kernel(coup, block, p, h, q, k, west, p_out, h_out, q_out):
    own_n, with_west = 2 * FACE, 3 * FACE
    for c in range(2):
        at = slice(512 * c, 512 * c + 512)
        p_out[at] = p[at] - mm(coup[at, own_n:with_west], west[...])
    for c in range(4):
        at = slice(512 * c, 512 * c + 512)
        h_out[at] = h[at] + mm(block[at, own_n:with_west], west[...])
    q_out[...] = q[...] + folded(mm(k[:, :FACE], west[...]))


def corner_kernel(q, k, south, out):
    out[...] = q[...] + folded(mm(k[:, FACE:], south[...]))


def inner_kernel(coup, p, south, t):
    for c in range(2):
        at = slice(c * 512, (c + 1) * 512)
        t[at] = (p[at] - mm(coup[at, 3 * FACE :], south[...])).astype(BF16)


def result(f, coup, block, h, ub, south):
    at = slice(f * FACE, (f + 1) * FACE)
    return h[at] + mm(block[at, 3 * FACE :], south[...]) + mm_tn(coup[:, at], ub[...])


def tail(basis, f, keep):
    rows = basis[:, f * FACE : (f + 1) * FACE].astype(F32)
    return (jnp.concatenate([rows, jnp.zeros((12, FACE), F32)], axis=0) * keep).astype(BF16)


def solve_kernel(pos, coup, inv, block, t, h, south, basis, x_h, sent, ub, xbuf, sem):
    rows = 512
    copies = []
    for c in range(2):
        at = slice(c * rows, (c + 1) * rows)
        x = mm(inv[at], t[...])
        xbuf[at] = x
        ub[at] = x.astype(BF16)
        copies.append(pltpu.make_async_copy(xbuf.at[pl.ds(c * rows, rows)], x_h.at[pl.ds(c * rows, rows)], sem.at[c]))
        copies[c].start()
    keep = (pos[0] > 0).astype(F32)
    sent[:FACE] = (result(3, coup, block, h, ub, south) * keep).astype(BF16)
    sent[FACE:] = tail(basis, 3, keep)
    for copy in copies:
        copy.wait()


def west_kernel(pos, coup, block, h, ub, south, basis, sent):
    keep = (pos[0] > 0).astype(F32)
    sent[:FACE] = (result(2, coup, block, h, ub, south) * keep).astype(BF16)
    sent[FACE:] = tail(basis, 2, keep)


def kept_kernel(coup, block, h, ub, south, kept):
    for f in range(2):
        kept[f * FACE : (f + 1) * FACE] = result(f, coup, block, h, ub, south)


def pair_kernel(pos, mine, theirs, out):
    first = lax.rem(pos[0], 2) == 0
    a, b = mine[...], theirs[...]
    low = jnp.where(first, a, b)
    high = jnp.where(first, b, a)
    for r in range(2):
        out[3 * r : 3 * r + 1] = low[2 * r : 2 * r + 1]
        out[3 * r + 1 : 3 * r + 2] = low[2 * r + 1 : 2 * r + 2] + high[2 * r : 2 * r + 1]
        out[3 * r + 2 : 3 * r + 3] = high[2 * r + 1 : 2 * r + 2]
    out[6:10] = low[4:8] + high[4:8]


def placed(at, blocks, slots):
    for k, block in enumerate(blocks):
        slots[at ^ k] = block[...]


def summed(slots, n):
    return (slots[0, n : n + 4] + slots[1, n : n + 4]) + (slots[2, n : n + 4] + slots[3, n : n + 4])


def rows_kernel(pos, b0, b1, b2, b3, out, slots):
    placed(lax.rem(pos[0], 4), (b0, b1, b2, b3), slots)
    out[0:3] = slots[0, 0:3]
    for b in range(1, 4):
        out[3 * b : 3 * b + 3] = slots[b - 1, 3:6] + slots[b, 0:3]
    out[12:15] = slots[3, 3:6]
    out[15:19] = summed(slots, 6)


def columns_kernel(i, j, b0, b1, b2, b3, e, o0, o1, o2, o3, slots, full, shares):
    placed(lax.div(j[0], 2), (b0, b1, b2, b3), slots)
    full[40:] = jnp.zeros((8, RHS), F32)
    for r in range(5):
        for c in range(9):
            b = min(c // 2, 3)
            n = 3 * r + c - 2 * b
            row = slots[b, n : n + 1]
            if c % 2 == 0 and 0 < c < 8:
                row = slots[b - 1, 3 * r + 2 : 3 * r + 3] + row
            full[9 * r + c : 9 * r + c + 1] = row
    e2, q2 = two_terms(e[...]), two_terms(full[...])
    all_shares = folded(mm(e2, q2[:48])) + mm(e2[:64], q2[48:])
    total = summed(slots, 15)
    for y in range(4):
        shares[y] = all_shares[16 * y : 16 * y + 16]
        shares[y, 12:16] = total
    at = lax.div(i[0], 4)
    for k, out in enumerate((o0, o1, o2, o3)):
        out[...] = shares[at ^ k]


def base_kernel(kept, got, w, out):
    wc = column(w[1:2, :])
    out[...] = wc * kept[FACE:] + (1.0 - wc) * got[:FACE].astype(F32)


def correction(f, cc, got, w, basis):
    wr = w[f : f + 1, :]
    mine = basis[:, f * FACE : (f + 1) * FACE].astype(F32) * wr
    other = got[FACE:].astype(F32)[:4] * (1.0 - wr)
    x = jnp.concatenate([mine, other], axis=0)
    c = jnp.concatenate([cc[0:4], cc[4 + 4 * f : 8 + 4 * f]], axis=0)
    xh, ch = x.astype(BF16).astype(F32), c.astype(BF16).astype(F32)
    pad = jnp.zeros((8, RHS), F32)
    left = jnp.concatenate([xh, x - xh, xh, pad], axis=0).astype(BF16)
    right = jnp.concatenate([ch, ch, c - ch, pad], axis=0).astype(BF16)
    return left, right


def written(f, n, part, zbuf, z, sem):
    here = pl.ds(n * 128, 128)
    zbuf[n * 128 : (n + 1) * 128] = part
    copy = pltpu.make_async_copy(zbuf.at[here], z.at[f, here], sem.at[n])
    copy.start()
    return copy


def final_north_kernel(pos, b0, b1, b2, b3, base, got, w, basis, z, cur, cc, slots, zbuf, sem):
    placed(lax.div(pos[0], 4), (b0, b3, b2, b1), slots)
    cur[...] = summed(slots, 12) / FACE
    cc[...] = (slots[0] + slots[1]) + (slots[2] + slots[3])
    left, right = correction(1, cc[...], got, w, basis)
    copies = []
    for n in range(4):
        rows = slice(n * 128, (n + 1) * 128)
        copies.append(written(1, n, base[rows] + mm_tn(left[:, rows], right), zbuf, z, sem))
    for copy in copies:
        copy.wait()


def final_east_kernel(cc, kept, got, w, basis, z, zbuf, sem):
    left, right = correction(0, cc[...], got, w, basis)
    wc = column(w[0:1, :])
    copies = []
    for n in range(4):
        rows = slice(n * 128, (n + 1) * 128)
        part = wc[rows] * kept[rows] + (1.0 - wc[rows]) * got[rows].astype(F32)
        copies.append(written(0, n, part + mm_tn(left[:, rows], right), zbuf, z, sem))
    for copy in copies:
        copy.wait()


def final(at, blocks, kept, base, from_east, from_north, w, basis):
    own = [pltpu.VMEM((FACE, RHS), F32), pltpu.SemaphoreType.DMA((4,))]
    z, currents, cc = call(
        final_north_kernel,
        (jax.ShapeDtypeStruct((2, FACE, RHS), F32), shape(NTERM, F32), shape(16, F32)),
        [SMEM] + [VMEM] * 8,
        (ANY, VMEM, VMEM),
        [pltpu.VMEM((4, 16, RHS), F32)] + own,
    )(at, *blocks, base, from_north, w, basis)
    (z,) = call(final_east_kernel, (), [VMEM] * 5, (), own, into=z)(cc, kept, from_east, w, basis)
    return z, currents


def along(x, axis, d):
    n = lax.axis_size(axis)
    return lax.ppermute(x, axis, [(s, (s + d) % n) for s in range(n)])


def exchanged(x, axis, stride, k):
    return lax.ppermute(x, axis, [(d ^ (k * stride), d) for d in range(lax.axis_size(axis))])


def four(x, axis, stride):
    far, middle, near = [exchanged(x, axis, stride, k) for k in (3, 2, 1)]
    return [x, near, middle, far]


def local(
    interior_residual,
    interface_residual,
    owner_face_weight,
    interior_inverse_block,
    coupling,
    interface_block,
    corner_trace_basis,
    coarse_inv,
    corner_map,
    contact,
):
    i = lax.axis_index("row").astype(jnp.int32).reshape(1)
    j = lax.axis_index("col").astype(jnp.int32).reshape(1)
    faces_in = interface_residual[0, 0]
    r = interior_residual[0, 0]
    w = owner_face_weight[0, 0]
    inv, coup, block = interior_inverse_block[0, 0], coupling[0, 0], interface_block[0, 0]
    basis = corner_trace_basis[0, 0]

    to_north = north_face(i, faces_in, w)
    south = along(to_north, "row", 1)
    to_east, own = east_face(j, faces_in, w, (to_north,))
    west = along(to_east, "col", 1)
    e = table(i, j, corner_map, coarse_inv, (own,))
    p, g, bt = call(
        early_a_kernel,
        (shape(INTERIOR, F32), shape(8, F32, INTERIOR), shape(8, BF16, 4 * FACE)),
        [VMEM] * 5,
        (VMEM,) * 3,
        after=(e,),
        cost=10,
    )(coup, r, own, basis, contact[0, 0])
    k, q = call(early_b_kernel, (shape(8, F32, 4 * FACE), shape(8, F32)), [VMEM] * 4, (VMEM,) * 2, cost=10)(g, inv, coup, r)
    h, q, k = call(
        early_c_kernel,
        (shape(4 * FACE, F32), shape(8, F32), shape(16, BF16, 2 * FACE)),
        [VMEM] * 5,
        (VMEM,) * 3,
        cost=10,
    )(bt, block, own, k, q)

    p, h, q = call(
        west_terms_kernel,
        (shape(INTERIOR, F32), shape(4 * FACE, F32), shape(8, F32)),
        [VMEM] * 7,
        (VMEM,) * 3,
        cost=2,
    )(coup, block, p, h, q, k, west)

    sums = call(corner_kernel, shape(8, F32), [VMEM] * 3, VMEM)(q, k, south)
    other = lax.ppermute(sums, "col", [(s, s ^ 1) for s in range(COLS)])
    t = call(inner_kernel, shape(INTERIOR, BF16), [VMEM] * 3, VMEM, after=(sums,), cost=1)(coup, p, south)
    sums = call(pair_kernel, shape(10, F32), [SMEM, VMEM, VMEM], VMEM, after=(t,))(j, sums, other)
    blocks = four(sums, "row", 1)
    x, to_south, ub = call(
        solve_kernel,
        (shape(INTERIOR, F32), shape(SENT, BF16), shape(INTERIOR, BF16)),
        [SMEM] + [VMEM] * 7,
        (ANY, VMEM, VMEM),
        [pltpu.VMEM((INTERIOR, RHS), F32), pltpu.SemaphoreType.DMA((2,))],
        after=(sums,),
        cost=4,
    )(i, coup, inv, block, t, h, south, basis)
    from_north = along(to_south, "row", -1)
    sums = call(
        rows_kernel, shape(19, F32), [SMEM] + [VMEM] * 4, VMEM, [pltpu.VMEM((4, 10, RHS), F32)], after=(to_south,)
    )(i, *blocks)
    blocks = four(sums, "col", 2)
    to_west = call(west_kernel, shape(SENT, BF16), [SMEM] + [VMEM] * 6, VMEM, after=(sums,), cost=1)(
        j, coup, block, h, ub, south, basis
    )
    from_east = along(to_west, "col", -1)
    kept = call(kept_kernel, shape(2 * FACE, F32), [VMEM] * 5, VMEM, after=(sums, to_west), cost=30)(
        coup, block, h, ub, south
    )
    shares = call(
        columns_kernel,
        (shape(16, F32),) * 4,
        [SMEM, SMEM] + [VMEM] * 5,
        (VMEM,) * 4,
        [pltpu.VMEM((4, 19, RHS), F32), pltpu.VMEM((48, RHS), F32), pltpu.VMEM((4, 16, RHS), F32)],
        after=(kept,),
    )(i, j, *blocks, e)
    far, middle, near = [exchanged(shares[k], "row", 4, k) for k in (3, 2, 1)]
    blocks = [shares[0], far, middle, near]
    base = call(base_kernel, shape(FACE, F32), [VMEM] * 3, VMEM, after=(shares[0],), cost=60)(kept, from_north, w)
    z, currents = final(i, blocks, kept, base, from_east, from_north, w, basis)
    return x[None, None], z[None, None], currents


def solution(mesh):
    return jax.shard_map(
        local,
        mesh=mesh,
        in_specs=(
            P("row", "col", None, None),
            P("row", "col", None, None, None),
            P("row", "col", None, None),
            P("row", "col", None, None),
            P("row", "col", None, None),
            P("row", "col", None, None),
            P("row", "col", None, None),
            P(),
            P(),
            P("row", "col", None, None),
        ),
        out_specs=(P("row", "col", None, None), P("row", "col", None, None, None), P()),
        check_vma=False,
    )
```

```python
import jax
import jax.numpy as jnp
from jax import lax
from jax.experimental import pallas as pl
from jax.experimental.pallas import tpu as pltpu
from jax.sharding import PartitionSpec as P

FACE = 512
RHS = 512
INTERIOR = 1024
NTERM = 4
ROWS = 16
COLS = 8
SENT = FACE + 16
HIGHEST = lax.Precision.HIGHEST
F32 = jnp.float32
BF16 = jnp.bfloat16
VMEM = pl.BlockSpec(memory_space=pltpu.VMEM)
SMEM = pl.BlockSpec(memory_space=pltpu.SMEM)
ANY = pl.BlockSpec(memory_space=pl.ANY)


def mm(a, b):
    return jnp.dot(a, b, preferred_element_type=F32)


def mm_nt(a, b):
    return lax.dot_general(a, b, (((1,), (1,)), ((), ())), preferred_element_type=F32)


def mm_tn(a, b):
    return lax.dot_general(a, b, (((0,), (0,)), ((), ())), preferred_element_type=F32)


def two_terms(a):
    high = a.astype(BF16)
    low = (a - high.astype(F32)).astype(BF16)
    return jnp.concatenate([high, low], axis=0)


def folded(a):
    half = a.shape[0] // 2
    return a[:half] + a[half:]


def column(row):
    return jnp.transpose(jnp.broadcast_to(row, (8, row.shape[1])))[:, :1]


def call(kernel, outs, in_specs, out_specs, scratch=(), after=(), vmem=16, cost=0):
    n = len(in_specs)

    def body(*refs):
        kernel(*refs[:n], *refs[n + len(after) :])

    run = pl.pallas_call(
        body,
        name=kernel.__name__,
        out_shape=outs,
        in_specs=list(in_specs) + [ANY] * len(after),
        out_specs=out_specs,
        scratch_shapes=list(scratch),
        compiler_params=pltpu.CompilerParams(vmem_limit_bytes=vmem << 20),
        cost_estimate=pl.CostEstimate(flops=1000 + cost * 1_000_000_000, bytes_accessed=1000 + cost * 3_000_000, transcendentals=0),
    )
    return lambda *args: run(*args, *after)


def shape(rows, kind, columns=RHS):
    return jax.ShapeDtypeStruct((rows, columns), kind)


def load_kernel(faces, face, sem):
    copy = pltpu.make_async_copy(faces.at[1], face, sem)
    copy.start()
    copy.wait()


def north_kernel(pos, face, w, out):
    keep = (pos[0] < ROWS - 1).astype(F32)
    out[...] = ((1.0 - column(w[1:2, :])) * keep * face[...]).astype(BF16)


def north_face(i, faces, w):
    face = call(load_kernel, shape(FACE, F32), [ANY], VMEM, [pltpu.SemaphoreType.DMA(())], vmem=52, cost=4)(faces)
    return call(north_kernel, shape(FACE, BF16), [SMEM, VMEM, VMEM], VMEM)(i, face, w)


def east_kernel(pos, faces, w, out, own):
    keep = (pos[0] < COLS - 1).astype(F32)
    c = column(w[0:1, :])
    out[...] = ((1.0 - c) * keep * faces[0]).astype(BF16)
    own[:FACE] = (c * faces[0]).astype(BF16)
    own[FACE:] = (column(w[1:2, :]) * faces[1]).astype(BF16)


def east_face(j, faces, w, after):
    return call(east_kernel, (shape(FACE, BF16), shape(2 * FACE, BF16)), [SMEM, VMEM, VMEM], (VMEM, VMEM), after=after, cost=4)(j, faces, w)


def table_kernel(i, j, cm, cmv, cinv, out, rows, lat):
    n_i, n_j = ROWS, COLS
    corners = cinv.shape[0]
    own_j = j[0]
    east_j = jnp.minimum(own_j + 1, n_j - 1)
    rows[...] = jnp.zeros_like(rows)
    for y in range(4):
        own_i = 4 * y + lax.rem(i[0], 4)
        north_i = jnp.minimum(own_i + 1, n_i - 1)
        for g, (a, b) in enumerate(((own_i, own_j), (own_i, east_j), (north_i, own_j))):
            for c in range(4):
                n = 16 * y + 4 * g + c
                rows[n : n + 1] = cinv[pl.ds(cm[4 * b + c, a], 1), :]
    ids = cmv[...].astype(F32)
    at = lax.broadcasted_iota(jnp.int32, (4 * n_j, n_j + 1), 0)
    col = lax.broadcasted_iota(jnp.int32, (4 * n_j, n_j + 1), 1)
    first = (at == jnp.where(col == n_j, 4 * n_j - 3, 4 * col)).astype(F32)
    last = (at == jnp.where(col == n_j, 4 * n_j - 1, 4 * col + 2)).astype(F32)
    flip = lambda s: lax.dot_general(ids, s, (((0,), (0,)), ((), ())), precision=HIGHEST, preferred_element_type=F32)
    lat[0:n_i] = flip(first)
    lat[n_i : n_i + 1] = flip(last)[n_i - 1 : n_i]
    base = 4 * lax.div(i[0], 4)
    line = jnp.concatenate([lat[pl.ds(base + a, 1), :] for a in range(5)], axis=1)
    slots = lax.broadcasted_iota(jnp.int32, (corners, 5 * (n_j + 1)), 0).astype(F32)
    out[:, :45] = jnp.dot(rows[...], (slots == line).astype(F32), precision=HIGHEST, preferred_element_type=F32)
    out[:, 45:] = jnp.zeros((64, 3), F32)


def table(i, j, corner_map, coarse_inv, after):
    cm = corner_map.transpose(1, 2, 0).reshape(4 * COLS, ROWS)
    return call(
        table_kernel,
        jax.ShapeDtypeStruct((64, 48), F32),
        [SMEM, SMEM, SMEM, VMEM, VMEM],
        VMEM,
        [pltpu.VMEM((64, coarse_inv.shape[0]), F32), pltpu.VMEM((24, COLS + 1), F32)],
        after=after,
    )(i, j, cm, cm, coarse_inv)


def early_a_kernel(coup, r, own, basis, contact, p, g, bt):
    labels = lax.broadcasted_iota(jnp.int32, (NTERM, FACE), 0) + 1
    marks = jnp.concatenate([(contact[f : f + 1, :] == labels).astype(F32) for f in range(4)], axis=1)
    bt[...] = jnp.concatenate([basis[...].astype(F32), marks], axis=0).astype(BF16)
    g[...] = mm_nt(bt[...], coup[...])
    for c in range(2):
        at = slice(512 * c, 512 * c + 512)
        p[at] = r[at] - mm(coup[at, : 2 * FACE], own[...])


def early_b_kernel(g, inv, coup, r, k, q):
    m = folded(mm(two_terms(g[...]), inv[...]))
    m2 = two_terms(m)
    k[...] = -folded(mm(m2, coup[...]))
    high = r[...].astype(BF16)
    low = (r[...] - high.astype(F32)).astype(BF16)
    q[...] = folded(mm(m2, high)) + mm(m2[:8], low)


def early_c_kernel(bt, block, own, k, qr, h, q, k_out):
    k2 = two_terms(k[...] + mm(bt[...], block[...]))
    q[...] = qr[...] + folded(mm(k2[:, : 2 * FACE], own[...]))
    k_out[...] = k2[:, 2 * FACE :]
    for c in range(4):
        at = slice(512 * c, 512 * c + 512)
        h[at] = mm(block[at, : 2 * FACE], own[...])


def west_terms_kernel(coup, block, p, h, q, k, west, p_out, h_out, q_out):
    own_n, with_west = 2 * FACE, 3 * FACE
    for c in range(2):
        at = slice(512 * c, 512 * c + 512)
        p_out[at] = p[at] - mm(coup[at, own_n:with_west], west[...])
    for c in range(4):
        at = slice(512 * c, 512 * c + 512)
        h_out[at] = h[at] + mm(block[at, own_n:with_west], west[...])
    q_out[...] = q[...] + folded(mm(k[:, :FACE], west[...]))


def corner_kernel(q, k, south, out):
    out[...] = q[...] + folded(mm(k[:, FACE:], south[...]))


def inner_kernel(coup, p, south, t):
    for c in range(2):
        at = slice(c * 512, (c + 1) * 512)
        t[at] = (p[at] - mm(coup[at, 3 * FACE :], south[...])).astype(BF16)


def result(f, coup, block, h, ub, south):
    at = slice(f * FACE, (f + 1) * FACE)
    return h[at] + mm(block[at, 3 * FACE :], south[...]) + mm_tn(coup[:, at], ub[...])


def tail(basis, f, keep):
    rows = basis[:, f * FACE : (f + 1) * FACE].astype(F32)
    return (jnp.concatenate([rows, jnp.zeros((12, FACE), F32)], axis=0) * keep).astype(BF16)


def solve_kernel(pos, coup, inv, block, t, h, south, basis, x_h, sent, ub, xbuf, sem):
    rows = 512
    copies = []
    for c in range(2):
        at = slice(c * rows, (c + 1) * rows)
        x = mm(inv[at], t[...])
        xbuf[at] = x
        ub[at] = x.astype(BF16)
        copies.append(pltpu.make_async_copy(xbuf.at[pl.ds(c * rows, rows)], x_h.at[pl.ds(c * rows, rows)], sem.at[c]))
        copies[c].start()
    keep = (pos[0] > 0).astype(F32)
    sent[:FACE] = (result(3, coup, block, h, ub, south) * keep).astype(BF16)
    sent[FACE:] = tail(basis, 3, keep)
    for copy in copies:
        copy.wait()


def west_kernel(pos, coup, block, h, ub, south, basis, sent):
    keep = (pos[0] > 0).astype(F32)
    sent[:FACE] = (result(2, coup, block, h, ub, south) * keep).astype(BF16)
    sent[FACE:] = tail(basis, 2, keep)


def kept_kernel(coup, block, h, ub, south, kept):
    for f in range(2):
        kept[f * FACE : (f + 1) * FACE] = result(f, coup, block, h, ub, south)


def pair_kernel(pos, mine, theirs, out):
    first = lax.rem(pos[0], 2) == 0
    a, b = mine[...], theirs[...]
    low = jnp.where(first, a, b)
    high = jnp.where(first, b, a)
    for r in range(2):
        out[3 * r : 3 * r + 1] = low[2 * r : 2 * r + 1]
        out[3 * r + 1 : 3 * r + 2] = low[2 * r + 1 : 2 * r + 2] + high[2 * r : 2 * r + 1]
        out[3 * r + 2 : 3 * r + 3] = high[2 * r + 1 : 2 * r + 2]
    out[6:10] = low[4:8] + high[4:8]


def placed(at, blocks, slots):
    for k, block in enumerate(blocks):
        slots[at ^ k] = block[...]


def summed(slots, n):
    return (slots[0, n : n + 4] + slots[1, n : n + 4]) + (slots[2, n : n + 4] + slots[3, n : n + 4])


def rows_kernel(pos, b0, b1, b2, b3, out, slots):
    placed(lax.rem(pos[0], 4), (b0, b1, b2, b3), slots)
    out[0:3] = slots[0, 0:3]
    for b in range(1, 4):
        out[3 * b : 3 * b + 3] = slots[b - 1, 3:6] + slots[b, 0:3]
    out[12:15] = slots[3, 3:6]
    out[15:19] = summed(slots, 6)


def columns_kernel(i, j, b0, b1, b2, b3, e, o0, o1, o2, o3, slots, full, shares):
    placed(lax.div(j[0], 2), (b0, b1, b2, b3), slots)
    full[40:] = jnp.zeros((8, RHS), F32)
    for r in range(5):
        for c in range(9):
            b = min(c // 2, 3)
            n = 3 * r + c - 2 * b
            row = slots[b, n : n + 1]
            if c % 2 == 0 and 0 < c < 8:
                row = slots[b - 1, 3 * r + 2 : 3 * r + 3] + row
            full[9 * r + c : 9 * r + c + 1] = row
    e2, q2 = two_terms(e[...]), two_terms(full[...])
    all_shares = folded(mm(e2, q2[:48])) + mm(e2[:64], q2[48:])
    total = summed(slots, 15)
    for y in range(4):
        shares[y] = all_shares[16 * y : 16 * y + 16]
        shares[y, 12:16] = total
    at = lax.div(i[0], 4)
    for k, out in enumerate((o0, o1, o2, o3)):
        out[...] = shares[at ^ k]


def base_kernel(kept, got, w, out):
    wc = column(w[1:2, :])
    out[...] = wc * kept[FACE:] + (1.0 - wc) * got[:FACE].astype(F32)


def correction(f, cc, got, w, basis):
    wr = w[f : f + 1, :]
    mine = basis[:, f * FACE : (f + 1) * FACE].astype(F32) * wr
    other = got[FACE:].astype(F32)[:4] * (1.0 - wr)
    x = jnp.concatenate([mine, other], axis=0)
    c = jnp.concatenate([cc[0:4], cc[4 + 4 * f : 8 + 4 * f]], axis=0)
    xh, ch = x.astype(BF16).astype(F32), c.astype(BF16).astype(F32)
    pad = jnp.zeros((8, RHS), F32)
    left = jnp.concatenate([xh, x - xh, xh, pad], axis=0).astype(BF16)
    right = jnp.concatenate([ch, ch, c - ch, pad], axis=0).astype(BF16)
    return left, right


def final_kernel(pos, b0, b1, b2, b3, kept, base, from_east, from_north, w, basis, z, cur, slots, zbuf, sem):
    placed(lax.div(pos[0], 4), (b0, b3, b2, b1), slots)
    cc = (slots[0] + slots[1]) + (slots[2] + slots[3])
    wc = column(w[0:1, :])
    copies = []
    for f, got in ((1, from_north), (0, from_east)):
        left, right = correction(f, cc, got, w, basis)
        for n in range(4):
            rows = slice(n * 128, (n + 1) * 128)
            part = base[rows] if f else wc[rows] * kept[rows] + (1.0 - wc[rows]) * got[rows].astype(F32)
            zbuf[f, rows] = part + mm_tn(left[:, rows], right)
            here = pl.ds(n * 128, 128)
            copy = pltpu.make_async_copy(zbuf.at[f, here], z.at[f, here], sem.at[4 * f + n])
            copy.start()
            copies.append(copy)
    cur[...] = summed(slots, 12) / FACE
    for copy in copies:
        copy.wait()


def final(at, blocks, kept, base, from_east, from_north, w, basis):
    return call(
        final_kernel,
        (jax.ShapeDtypeStruct((2, FACE, RHS), F32), shape(NTERM, F32)),
        [SMEM] + [VMEM] * 10,
        (ANY, VMEM),
        [
            pltpu.VMEM((4, 16, RHS), F32),
            pltpu.VMEM((2, FACE, RHS), F32),
            pltpu.SemaphoreType.DMA((8,)),
        ],
    )(at, *blocks, kept, base, from_east, from_north, w, basis)


def along(x, axis, d):
    n = lax.axis_size(axis)
    return lax.ppermute(x, axis, [(s, (s + d) % n) for s in range(n)])


def exchanged(x, axis, stride, k):
    return lax.ppermute(x, axis, [(d ^ (k * stride), d) for d in range(lax.axis_size(axis))])


def four(x, axis, stride):
    far, middle, near = [exchanged(x, axis, stride, k) for k in (3, 2, 1)]
    return [x, near, middle, far]


def local(
    interior_residual,
    interface_residual,
    owner_face_weight,
    interior_inverse_block,
    coupling,
    interface_block,
    corner_trace_basis,
    coarse_inv,
    corner_map,
    contact,
):
    i = lax.axis_index("row").astype(jnp.int32).reshape(1)
    j = lax.axis_index("col").astype(jnp.int32).reshape(1)
    faces_in = interface_residual[0, 0]
    r = interior_residual[0, 0]
    w = owner_face_weight[0, 0]
    inv, coup, block = interior_inverse_block[0, 0], coupling[0, 0], interface_block[0, 0]
    basis = corner_trace_basis[0, 0]

    to_north = north_face(i, faces_in, w)
    south = along(to_north, "row", 1)
    to_east, own = east_face(j, faces_in, w, (to_north,))
    west = along(to_east, "col", 1)
    e = table(i, j, corner_map, coarse_inv, (own,))
    p, g, bt = call(
        early_a_kernel,
        (shape(INTERIOR, F32), shape(8, F32, INTERIOR), shape(8, BF16, 4 * FACE)),
        [VMEM] * 5,
        (VMEM,) * 3,
        after=(e,),
        cost=10,
    )(coup, r, own, basis, contact[0, 0])
    k, q = call(early_b_kernel, (shape(8, F32, 4 * FACE), shape(8, F32)), [VMEM] * 4, (VMEM,) * 2, cost=10)(g, inv, coup, r)
    h, q, k = call(
        early_c_kernel,
        (shape(4 * FACE, F32), shape(8, F32), shape(16, BF16, 2 * FACE)),
        [VMEM] * 5,
        (VMEM,) * 3,
        cost=10,
    )(bt, block, own, k, q)

    p, h, q = call(
        west_terms_kernel,
        (shape(INTERIOR, F32), shape(4 * FACE, F32), shape(8, F32)),
        [VMEM] * 7,
        (VMEM,) * 3,
        cost=2,
    )(coup, block, p, h, q, k, west)

    sums = call(corner_kernel, shape(8, F32), [VMEM] * 3, VMEM)(q, k, south)
    other = lax.ppermute(sums, "col", [(s, s ^ 1) for s in range(COLS)])
    t = call(inner_kernel, shape(INTERIOR, BF16), [VMEM] * 3, VMEM, after=(sums,), cost=1)(coup, p, south)
    sums = call(pair_kernel, shape(10, F32), [SMEM, VMEM, VMEM], VMEM, after=(t,))(j, sums, other)
    blocks = four(sums, "row", 1)
    x, to_south, ub = call(
        solve_kernel,
        (shape(INTERIOR, F32), shape(SENT, BF16), shape(INTERIOR, BF16)),
        [SMEM] + [VMEM] * 7,
        (ANY, VMEM, VMEM),
        [pltpu.VMEM((INTERIOR, RHS), F32), pltpu.SemaphoreType.DMA((2,))],
        after=(sums,),
        cost=4,
    )(i, coup, inv, block, t, h, south, basis)
    from_north = along(to_south, "row", -1)
    sums = call(
        rows_kernel, shape(19, F32), [SMEM] + [VMEM] * 4, VMEM, [pltpu.VMEM((4, 10, RHS), F32)], after=(to_south,)
    )(i, *blocks)
    blocks = four(sums, "col", 2)
    to_west = call(west_kernel, shape(SENT, BF16), [SMEM] + [VMEM] * 6, VMEM, after=(sums,), cost=1)(
        j, coup, block, h, ub, south, basis
    )
    from_east = along(to_west, "col", -1)
    kept = call(kept_kernel, shape(2 * FACE, F32), [VMEM] * 5, VMEM, after=(sums, to_west), cost=30)(
        coup, block, h, ub, south
    )
    shares = call(
        columns_kernel,
        (shape(16, F32),) * 4,
        [SMEM, SMEM] + [VMEM] * 5,
        (VMEM,) * 4,
        [pltpu.VMEM((4, 19, RHS), F32), pltpu.VMEM((48, RHS), F32), pltpu.VMEM((4, 16, RHS), F32)],
        after=(kept,),
    )(i, j, *blocks, e)
    far, middle, near = [exchanged(shares[k], "row", 4, k) for k in (3, 2, 1)]
    blocks = [shares[0], far, middle, near]
    base = call(base_kernel, shape(FACE, F32), [VMEM] * 3, VMEM, after=(shares[0],), cost=60)(kept, from_north, w)
    z, currents = final(i, blocks, kept, base, from_east, from_north, w, basis)
    return x[None, None], z[None, None], currents


def solution(mesh):
    return jax.shard_map(
        local,
        mesh=mesh,
        in_specs=(
            P("row", "col", None, None),
            P("row", "col", None, None, None),
            P("row", "col", None, None),
            P("row", "col", None, None),
            P("row", "col", None, None),
            P("row", "col", None, None),
            P("row", "col", None, None),
            P(),
            P(),
            P("row", "col", None, None),
        ),
        out_specs=(P("row", "col", None, None), P("row", "col", None, None, None), P()),
        check_vma=False,
    )
```

```python
import jax
import jax.numpy as jnp
from jax import lax
from jax.experimental import pallas as pl
from jax.experimental.pallas import tpu as pltpu
from jax.sharding import PartitionSpec as P

FACE = 512
RHS = 512
INTERIOR = 1024
NTERM = 4
ROWS = 16
COLS = 8
SENT = FACE + 16
HIGHEST = lax.Precision.HIGHEST
F32 = jnp.float32
BF16 = jnp.bfloat16
VMEM = pl.BlockSpec(memory_space=pltpu.VMEM)
SMEM = pl.BlockSpec(memory_space=pltpu.SMEM)
ANY = pl.BlockSpec(memory_space=pl.ANY)


def mm(a, b):
    return jnp.dot(a, b, preferred_element_type=F32)


def mm_nt(a, b):
    return lax.dot_general(a, b, (((1,), (1,)), ((), ())), preferred_element_type=F32)


def mm_tn(a, b):
    return lax.dot_general(a, b, (((0,), (0,)), ((), ())), preferred_element_type=F32)


def two_terms(a):
    high = a.astype(BF16)
    low = (a - high.astype(F32)).astype(BF16)
    return jnp.concatenate([high, low], axis=0)


def folded(a):
    half = a.shape[0] // 2
    return a[:half] + a[half:]


def column(row):
    return jnp.transpose(jnp.broadcast_to(row, (8, row.shape[1])))[:, :1]


def call(kernel, outs, in_specs, out_specs, scratch=(), after=(), vmem=16, cost=0):
    n = len(in_specs)

    def body(*refs):
        kernel(*refs[:n], *refs[n + len(after) :])

    run = pl.pallas_call(
        body,
        name=kernel.__name__,
        out_shape=outs,
        in_specs=list(in_specs) + [ANY] * len(after),
        out_specs=out_specs,
        scratch_shapes=list(scratch),
        compiler_params=pltpu.CompilerParams(vmem_limit_bytes=vmem << 20),
        cost_estimate=pl.CostEstimate(flops=1000 + cost * 1_000_000_000, bytes_accessed=1000 + cost * 3_000_000, transcendentals=0),
    )
    return lambda *args: run(*args, *after)


def shape(rows, kind, columns=RHS):
    return jax.ShapeDtypeStruct((rows, columns), kind)


def load_kernel(faces, face, sem):
    copy = pltpu.make_async_copy(faces.at[1], face, sem)
    copy.start()
    copy.wait()


def north_kernel(pos, face, w, out):
    keep = (pos[0] < ROWS - 1).astype(F32)
    out[...] = ((1.0 - column(w[1:2, :])) * keep * face[...]).astype(BF16)


def north_face(i, faces, w):
    face = call(load_kernel, shape(FACE, F32), [ANY], VMEM, [pltpu.SemaphoreType.DMA(())], vmem=52, cost=4)(faces)
    return call(north_kernel, shape(FACE, BF16), [SMEM, VMEM, VMEM], VMEM)(i, face, w), face


def east_kernel(pos, faces, north, w, out, own, face, sem):
    rows = FACE // 2
    copies = [
        pltpu.make_async_copy(faces.at[0, pl.ds(c * rows, rows)], face.at[pl.ds(c * rows, rows)], sem.at[c])
        for c in range(2)
    ]
    for copy in copies:
        copy.start()
    own[FACE:] = (column(w[1:2, :]) * north[...]).astype(BF16)
    keep = (pos[0] < COLS - 1).astype(F32)
    wc = column(w[0:1, :])
    for c, copy in enumerate(copies):
        copy.wait()
        at = slice(c * rows, (c + 1) * rows)
        out[at] = ((1.0 - wc[at]) * keep * face[at]).astype(BF16)
        own[at] = (wc[at] * face[at]).astype(BF16)


def east_face(j, faces, north, w, after):
    return call(
        east_kernel,
        (shape(FACE, BF16), shape(2 * FACE, BF16)),
        [SMEM, ANY, VMEM, VMEM],
        (VMEM, VMEM),
        [pltpu.VMEM((FACE, RHS), F32), pltpu.SemaphoreType.DMA((2,))],
        after=after,
        vmem=50,
        cost=4,
    )(j, faces, north, w)


def table_kernel(i, j, cm, cmv, cinv, out, rows, lat):
    n_i, n_j = ROWS, COLS
    corners = cinv.shape[0]
    own_j = j[0]
    east_j = jnp.minimum(own_j + 1, n_j - 1)
    rows[...] = jnp.zeros_like(rows)
    for y in range(4):
        own_i = 4 * y + lax.rem(i[0], 4)
        north_i = jnp.minimum(own_i + 1, n_i - 1)
        for g, (a, b) in enumerate(((own_i, own_j), (own_i, east_j), (north_i, own_j))):
            for c in range(4):
                n = 16 * y + 4 * g + c
                rows[n : n + 1] = cinv[pl.ds(cm[4 * b + c, a], 1), :]
    ids = cmv[...].astype(F32)
    at = lax.broadcasted_iota(jnp.int32, (4 * n_j, n_j + 1), 0)
    col = lax.broadcasted_iota(jnp.int32, (4 * n_j, n_j + 1), 1)
    first = (at == jnp.where(col == n_j, 4 * n_j - 3, 4 * col)).astype(F32)
    last = (at == jnp.where(col == n_j, 4 * n_j - 1, 4 * col + 2)).astype(F32)
    flip = lambda s: lax.dot_general(ids, s, (((0,), (0,)), ((), ())), precision=HIGHEST, preferred_element_type=F32)
    lat[0:n_i] = flip(first)
    lat[n_i : n_i + 1] = flip(last)[n_i - 1 : n_i]
    base = 4 * lax.div(i[0], 4)
    line = jnp.concatenate([lat[pl.ds(base + a, 1), :] for a in range(5)], axis=1)
    slots = lax.broadcasted_iota(jnp.int32, (corners, 5 * (n_j + 1)), 0).astype(F32)
    out[:, :45] = jnp.dot(rows[...], (slots == line).astype(F32), precision=HIGHEST, preferred_element_type=F32)
    out[:, 45:] = jnp.zeros((64, 3), F32)


def table(i, j, corner_map, coarse_inv, after):
    cm = corner_map.transpose(1, 2, 0).reshape(4 * COLS, ROWS)
    return call(
        table_kernel,
        jax.ShapeDtypeStruct((64, 48), F32),
        [SMEM, SMEM, SMEM, VMEM, VMEM],
        VMEM,
        [pltpu.VMEM((64, coarse_inv.shape[0]), F32), pltpu.VMEM((24, COLS + 1), F32)],
        after=after,
    )(i, j, cm, cm, coarse_inv)


def early_a_kernel(coup, r, own, basis, contact, p, g, bt):
    labels = lax.broadcasted_iota(jnp.int32, (NTERM, FACE), 0) + 1
    marks = jnp.concatenate([(contact[f : f + 1, :] == labels).astype(F32) for f in range(4)], axis=1)
    bt[...] = jnp.concatenate([basis[...].astype(F32), marks], axis=0).astype(BF16)
    g[...] = mm_nt(bt[...], coup[...])
    for c in range(2):
        at = slice(512 * c, 512 * c + 512)
        p[at] = r[at] - mm(coup[at, : 2 * FACE], own[...])


def early_b_kernel(g, inv, coup, r, k, q):
    m = folded(mm(two_terms(g[...]), inv[...]))
    m2 = two_terms(m)
    k[...] = -folded(mm(m2, coup[...]))
    high = r[...].astype(BF16)
    low = (r[...] - high.astype(F32)).astype(BF16)
    q[...] = folded(mm(m2, high)) + mm(m2[:8], low)


def early_c_kernel(bt, block, own, k, qr, h, q, k_out):
    k2 = two_terms(k[...] + mm(bt[...], block[...]))
    q[...] = qr[...] + folded(mm(k2[:, : 2 * FACE], own[...]))
    k_out[...] = k2[:, 2 * FACE :]
    for c in range(4):
        at = slice(512 * c, 512 * c + 512)
        h[at] = mm(block[at, : 2 * FACE], own[...])


def west_terms_kernel(coup, block, p, h, q, k, west, p_out, h_out, q_out):
    own_n, with_west = 2 * FACE, 3 * FACE
    for c in range(2):
        at = slice(512 * c, 512 * c + 512)
        p_out[at] = p[at] - mm(coup[at, own_n:with_west], west[...])
    for c in range(4):
        at = slice(512 * c, 512 * c + 512)
        h_out[at] = h[at] + mm(block[at, own_n:with_west], west[...])
    q_out[...] = q[...] + folded(mm(k[:, :FACE], west[...]))


def corner_kernel(q, k, south, out):
    out[...] = q[...] + folded(mm(k[:, FACE:], south[...]))


def inner_kernel(coup, p, south, t):
    for c in range(2):
        at = slice(c * 512, (c + 1) * 512)
        t[at] = (p[at] - mm(coup[at, 3 * FACE :], south[...])).astype(BF16)


def result(f, coup, block, h, ub, south):
    at = slice(f * FACE, (f + 1) * FACE)
    return h[at] + mm(block[at, 3 * FACE :], south[...]) + mm_tn(coup[:, at], ub[...])


def tail(basis, f, keep):
    rows = basis[:, f * FACE : (f + 1) * FACE].astype(F32)
    return (jnp.concatenate([rows, jnp.zeros((12, FACE), F32)], axis=0) * keep).astype(BF16)


def solve_kernel(pos, coup, inv, block, t, h, south, basis, x_h, sent, ub, xbuf, sem):
    rows = 512
    copies = []
    for c in range(2):
        at = slice(c * rows, (c + 1) * rows)
        x = mm(inv[at], t[...])
        xbuf[at] = x
        ub[at] = x.astype(BF16)
        copies.append(pltpu.make_async_copy(xbuf.at[pl.ds(c * rows, rows)], x_h.at[pl.ds(c * rows, rows)], sem.at[c]))
        copies[c].start()
    keep = (pos[0] > 0).astype(F32)
    sent[:FACE] = (result(3, coup, block, h, ub, south) * keep).astype(BF16)
    sent[FACE:] = tail(basis, 3, keep)
    for copy in copies:
        copy.wait()


def west_kernel(pos, coup, block, h, ub, south, basis, sent):
    keep = (pos[0] > 0).astype(F32)
    sent[:FACE] = (result(2, coup, block, h, ub, south) * keep).astype(BF16)
    sent[FACE:] = tail(basis, 2, keep)


def kept_kernel(coup, block, h, ub, south, kept):
    for f in range(2):
        kept[f * FACE : (f + 1) * FACE] = result(f, coup, block, h, ub, south)


def pair_kernel(pos, mine, theirs, out):
    first = lax.rem(pos[0], 2) == 0
    a, b = mine[...], theirs[...]
    low = jnp.where(first, a, b)
    high = jnp.where(first, b, a)
    for r in range(2):
        out[3 * r : 3 * r + 1] = low[2 * r : 2 * r + 1]
        out[3 * r + 1 : 3 * r + 2] = low[2 * r + 1 : 2 * r + 2] + high[2 * r : 2 * r + 1]
        out[3 * r + 2 : 3 * r + 3] = high[2 * r + 1 : 2 * r + 2]
    out[6:10] = low[4:8] + high[4:8]


def placed(at, blocks, slots):
    for k, block in enumerate(blocks):
        slots[at ^ k] = block[...]


def summed(slots, n):
    return (slots[0, n : n + 4] + slots[1, n : n + 4]) + (slots[2, n : n + 4] + slots[3, n : n + 4])


def rows_kernel(pos, b0, b1, b2, b3, out, slots):
    placed(lax.rem(pos[0], 4), (b0, b1, b2, b3), slots)
    out[0:3] = slots[0, 0:3]
    for b in range(1, 4):
        out[3 * b : 3 * b + 3] = slots[b - 1, 3:6] + slots[b, 0:3]
    out[12:15] = slots[3, 3:6]
    out[15:19] = summed(slots, 6)


def columns_kernel(i, j, b0, b1, b2, b3, e, o0, o1, o2, o3, slots, full, shares):
    placed(lax.div(j[0], 2), (b0, b1, b2, b3), slots)
    full[40:] = jnp.zeros((8, RHS), F32)
    for r in range(5):
        for c in range(9):
            b = min(c // 2, 3)
            n = 3 * r + c - 2 * b
            row = slots[b, n : n + 1]
            if c % 2 == 0 and 0 < c < 8:
                row = slots[b - 1, 3 * r + 2 : 3 * r + 3] + row
            full[9 * r + c : 9 * r + c + 1] = row
    e2, q2 = two_terms(e[...]), two_terms(full[...])
    all_shares = folded(mm(e2, q2[:48])) + mm(e2[:64], q2[48:])
    total = summed(slots, 15)
    for y in range(4):
        shares[y] = all_shares[16 * y : 16 * y + 16]
        shares[y, 12:16] = total
    at = lax.div(i[0], 4)
    for k, out in enumerate((o0, o1, o2, o3)):
        out[...] = shares[at ^ k]


def base_kernel(kept, got, w, out):
    wc = column(w[1:2, :])
    out[...] = wc * kept[FACE:] + (1.0 - wc) * got[:FACE].astype(F32)


def correction(f, cc, got, w, basis):
    wr = w[f : f + 1, :]
    mine = basis[:, f * FACE : (f + 1) * FACE].astype(F32) * wr
    other = got[FACE:].astype(F32)[:4] * (1.0 - wr)
    x = jnp.concatenate([mine, other], axis=0)
    c = jnp.concatenate([cc[0:4], cc[4 + 4 * f : 8 + 4 * f]], axis=0)
    xh, ch = x.astype(BF16).astype(F32), c.astype(BF16).astype(F32)
    pad = jnp.zeros((8, RHS), F32)
    left = jnp.concatenate([xh, x - xh, xh, pad], axis=0).astype(BF16)
    right = jnp.concatenate([ch, ch, c - ch, pad], axis=0).astype(BF16)
    return left, right


def final_kernel(pos, b0, b1, b2, b3, kept, base, from_east, from_north, w, basis, z, cur, slots, zbuf, sem):
    placed(lax.div(pos[0], 4), (b0, b3, b2, b1), slots)
    cc = (slots[0] + slots[1]) + (slots[2] + slots[3])
    wc = column(w[0:1, :])
    copies = []
    for f, got in ((1, from_north), (0, from_east)):
        left, right = correction(f, cc, got, w, basis)
        for n in range(4):
            rows = slice(n * 128, (n + 1) * 128)
            part = base[rows] if f else wc[rows] * kept[rows] + (1.0 - wc[rows]) * got[rows].astype(F32)
            zbuf[f, rows] = part + mm_tn(left[:, rows], right)
            here = pl.ds(n * 128, 128)
            copy = pltpu.make_async_copy(zbuf.at[f, here], z.at[f, here], sem.at[4 * f + n])
            copy.start()
            copies.append(copy)
    cur[...] = summed(slots, 12) / FACE
    for copy in copies:
        copy.wait()


def final(at, blocks, kept, base, from_east, from_north, w, basis):
    return call(
        final_kernel,
        (jax.ShapeDtypeStruct((2, FACE, RHS), F32), shape(NTERM, F32)),
        [SMEM] + [VMEM] * 10,
        (ANY, VMEM),
        [
            pltpu.VMEM((4, 16, RHS), F32),
            pltpu.VMEM((2, FACE, RHS), F32),
            pltpu.SemaphoreType.DMA((8,)),
        ],
    )(at, *blocks, kept, base, from_east, from_north, w, basis)


def along(x, axis, d):
    n = lax.axis_size(axis)
    return lax.ppermute(x, axis, [(s, (s + d) % n) for s in range(n)])


def exchanged(x, axis, stride, k):
    return lax.ppermute(x, axis, [(d ^ (k * stride), d) for d in range(lax.axis_size(axis))])


def four(x, axis, stride):
    far, middle, near = [exchanged(x, axis, stride, k) for k in (3, 2, 1)]
    return [x, near, middle, far]


def local(
    interior_residual,
    interface_residual,
    owner_face_weight,
    interior_inverse_block,
    coupling,
    interface_block,
    corner_trace_basis,
    coarse_inv,
    corner_map,
    contact,
):
    i = lax.axis_index("row").astype(jnp.int32).reshape(1)
    j = lax.axis_index("col").astype(jnp.int32).reshape(1)
    faces_in = interface_residual[0, 0]
    r = interior_residual[0, 0]
    w = owner_face_weight[0, 0]
    inv, coup, block = interior_inverse_block[0, 0], coupling[0, 0], interface_block[0, 0]
    basis = corner_trace_basis[0, 0]

    to_north, north = north_face(i, faces_in, w)
    south = along(to_north, "row", 1)
    to_east, own = east_face(j, faces_in, north, w, (to_north,))
    west = along(to_east, "col", 1)
    e = table(i, j, corner_map, coarse_inv, (own,))
    p, g, bt = call(
        early_a_kernel,
        (shape(INTERIOR, F32), shape(8, F32, INTERIOR), shape(8, BF16, 4 * FACE)),
        [VMEM] * 5,
        (VMEM,) * 3,
        after=(e,),
        cost=10,
    )(coup, r, own, basis, contact[0, 0])
    k, q = call(early_b_kernel, (shape(8, F32, 4 * FACE), shape(8, F32)), [VMEM] * 4, (VMEM,) * 2, cost=10)(g, inv, coup, r)
    h, q, k = call(
        early_c_kernel,
        (shape(4 * FACE, F32), shape(8, F32), shape(16, BF16, 2 * FACE)),
        [VMEM] * 5,
        (VMEM,) * 3,
        cost=10,
    )(bt, block, own, k, q)

    p, h, q = call(
        west_terms_kernel,
        (shape(INTERIOR, F32), shape(4 * FACE, F32), shape(8, F32)),
        [VMEM] * 7,
        (VMEM,) * 3,
        cost=2,
    )(coup, block, p, h, q, k, west)

    sums = call(corner_kernel, shape(8, F32), [VMEM] * 3, VMEM)(q, k, south)
    other = lax.ppermute(sums, "col", [(s, s ^ 1) for s in range(COLS)])
    t = call(inner_kernel, shape(INTERIOR, BF16), [VMEM] * 3, VMEM, after=(sums,), cost=1)(coup, p, south)
    sums = call(pair_kernel, shape(10, F32), [SMEM, VMEM, VMEM], VMEM, after=(t,))(j, sums, other)
    blocks = four(sums, "row", 1)
    x, to_south, ub = call(
        solve_kernel,
        (shape(INTERIOR, F32), shape(SENT, BF16), shape(INTERIOR, BF16)),
        [SMEM] + [VMEM] * 7,
        (ANY, VMEM, VMEM),
        [pltpu.VMEM((INTERIOR, RHS), F32), pltpu.SemaphoreType.DMA((2,))],
        after=(sums,),
        cost=4,
    )(i, coup, inv, block, t, h, south, basis)
    from_north = along(to_south, "row", -1)
    sums = call(
        rows_kernel, shape(19, F32), [SMEM] + [VMEM] * 4, VMEM, [pltpu.VMEM((4, 10, RHS), F32)], after=(to_south,)
    )(i, *blocks)
    blocks = four(sums, "col", 2)
    to_west = call(west_kernel, shape(SENT, BF16), [SMEM] + [VMEM] * 6, VMEM, after=(sums,), cost=1)(
        j, coup, block, h, ub, south, basis
    )
    from_east = along(to_west, "col", -1)
    kept = call(kept_kernel, shape(2 * FACE, F32), [VMEM] * 5, VMEM, after=(sums, to_west), cost=30)(
        coup, block, h, ub, south
    )
    shares = call(
        columns_kernel,
        (shape(16, F32),) * 4,
        [SMEM, SMEM] + [VMEM] * 5,
        (VMEM,) * 4,
        [pltpu.VMEM((4, 19, RHS), F32), pltpu.VMEM((48, RHS), F32), pltpu.VMEM((4, 16, RHS), F32)],
        after=(kept,),
    )(i, j, *blocks, e)
    far, middle, near = [exchanged(shares[k], "row", 4, k) for k in (3, 2, 1)]
    blocks = [shares[0], far, middle, near]
    base = call(base_kernel, shape(FACE, F32), [VMEM] * 3, VMEM, after=(shares[0],), cost=60)(kept, from_north, w)
    z, currents = final(i, blocks, kept, base, from_east, from_north, w, basis)
    return x[None, None], z[None, None], currents


def solution(mesh):
    return jax.shard_map(
        local,
        mesh=mesh,
        in_specs=(
            P("row", "col", None, None),
            P("row", "col", None, None, None),
            P("row", "col", None, None),
            P("row", "col", None, None),
            P("row", "col", None, None),
            P("row", "col", None, None),
            P("row", "col", None, None),
            P(),
            P(),
            P("row", "col", None, None),
        ),
        out_specs=(P("row", "col", None, None), P("row", "col", None, None, None), P()),
        check_vma=False,
    )
```

```python
import jax
import jax.numpy as jnp
from jax import lax
from jax.experimental import pallas as pl
from jax.experimental.pallas import tpu as pltpu
from jax.sharding import PartitionSpec as P

FACE = 512
RHS = 512
INTERIOR = 1024
NTERM = 4
ROWS = 16
COLS = 8
SENT = FACE + 16
HIGHEST = lax.Precision.HIGHEST
F32 = jnp.float32
BF16 = jnp.bfloat16
VMEM = pl.BlockSpec(memory_space=pltpu.VMEM)
SMEM = pl.BlockSpec(memory_space=pltpu.SMEM)
ANY = pl.BlockSpec(memory_space=pl.ANY)


def mm(a, b):
    return jnp.dot(a, b, preferred_element_type=F32)


def mm_nt(a, b):
    return lax.dot_general(a, b, (((1,), (1,)), ((), ())), preferred_element_type=F32)


def mm_tn(a, b):
    return lax.dot_general(a, b, (((0,), (0,)), ((), ())), preferred_element_type=F32)


def two_terms(a):
    high = a.astype(BF16)
    low = (a - high.astype(F32)).astype(BF16)
    return jnp.concatenate([high, low], axis=0)


def folded(a):
    half = a.shape[0] // 2
    return a[:half] + a[half:]


def column(row):
    return jnp.transpose(jnp.broadcast_to(row, (8, row.shape[1])))[:, :1]


def call(kernel, outs, in_specs, out_specs, scratch=(), after=(), vmem=16, cost=0):
    n = len(in_specs)

    def body(*refs):
        kernel(*refs[:n], *refs[n + len(after) :])

    run = pl.pallas_call(
        body,
        name=kernel.__name__,
        out_shape=outs,
        in_specs=list(in_specs) + [ANY] * len(after),
        out_specs=out_specs,
        scratch_shapes=list(scratch),
        compiler_params=pltpu.CompilerParams(vmem_limit_bytes=vmem << 20),
        cost_estimate=pl.CostEstimate(flops=1000 + cost * 1_000_000_000, bytes_accessed=1000 + cost * 3_000_000, transcendentals=0),
    )
    return lambda *args: run(*args, *after)


def shape(rows, kind, columns=RHS):
    return jax.ShapeDtypeStruct((rows, columns), kind)


def load_kernel(faces, face, sem):
    copy = pltpu.make_async_copy(faces.at[1], face, sem)
    copy.start()
    copy.wait()


def north_kernel(pos, face, w, out):
    keep = (pos[0] < ROWS - 1).astype(F32)
    out[...] = ((1.0 - column(w[1:2, :])) * keep * face[...]).astype(BF16)


def north_face(i, faces, w):
    face = call(load_kernel, shape(FACE, F32), [ANY], VMEM, [pltpu.SemaphoreType.DMA(())], vmem=52, cost=4)(faces)
    return call(north_kernel, shape(FACE, BF16), [SMEM, VMEM, VMEM], VMEM)(i, face, w)


def east_kernel(pos, faces, w, out, own):
    keep = (pos[0] < COLS - 1).astype(F32)
    c = column(w[0:1, :])
    out[...] = ((1.0 - c) * keep * faces[0]).astype(BF16)
    own[:FACE] = (c * faces[0]).astype(BF16)
    own[FACE:] = (column(w[1:2, :]) * faces[1]).astype(BF16)


def east_face(j, faces, w, after):
    return call(east_kernel, (shape(FACE, BF16), shape(2 * FACE, BF16)), [SMEM, VMEM, VMEM], (VMEM, VMEM), after=after, cost=4)(j, faces, w)


def table_kernel(i, j, cm, cmv, cinv, out, rows, lat):
    n_i, n_j = ROWS, COLS
    corners = cinv.shape[0]
    own_j = j[0]
    east_j = jnp.minimum(own_j + 1, n_j - 1)
    rows[...] = jnp.zeros_like(rows)
    for y in range(4):
        own_i = 4 * y + lax.rem(i[0], 4)
        north_i = jnp.minimum(own_i + 1, n_i - 1)
        for g, (a, b) in enumerate(((own_i, own_j), (own_i, east_j), (north_i, own_j))):
            for c in range(4):
                n = 16 * y + 4 * g + c
                rows[n : n + 1] = cinv[pl.ds(cm[4 * b + c, a], 1), :]
    ids = cmv[...].astype(F32)
    at = lax.broadcasted_iota(jnp.int32, (4 * n_j, n_j + 1), 0)
    col = lax.broadcasted_iota(jnp.int32, (4 * n_j, n_j + 1), 1)
    first = (at == jnp.where(col == n_j, 4 * n_j - 3, 4 * col)).astype(F32)
    last = (at == jnp.where(col == n_j, 4 * n_j - 1, 4 * col + 2)).astype(F32)
    flip = lambda s: lax.dot_general(ids, s, (((0,), (0,)), ((), ())), precision=HIGHEST, preferred_element_type=F32)
    lat[0:n_i] = flip(first)
    lat[n_i : n_i + 1] = flip(last)[n_i - 1 : n_i]
    base = 4 * lax.div(i[0], 4)
    line = jnp.concatenate([lat[pl.ds(base + a, 1), :] for a in range(5)], axis=1)
    slots = lax.broadcasted_iota(jnp.int32, (corners, 5 * (n_j + 1)), 0).astype(F32)
    out[:, :45] = jnp.dot(rows[...], (slots == line).astype(F32), precision=HIGHEST, preferred_element_type=F32)
    out[:, 45:] = jnp.zeros((64, 3), F32)


def table(i, j, corner_map, coarse_inv, after):
    cm = corner_map.transpose(1, 2, 0).reshape(4 * COLS, ROWS)
    return call(
        table_kernel,
        jax.ShapeDtypeStruct((64, 48), F32),
        [SMEM, SMEM, SMEM, VMEM, VMEM],
        VMEM,
        [pltpu.VMEM((64, coarse_inv.shape[0]), F32), pltpu.VMEM((24, COLS + 1), F32)],
        after=after,
    )(i, j, cm, cm, coarse_inv)


def early_a_kernel(coup, r, own, basis, contact, p, g, bt):
    labels = lax.broadcasted_iota(jnp.int32, (NTERM, FACE), 0) + 1
    marks = jnp.concatenate([(contact[f : f + 1, :] == labels).astype(F32) for f in range(4)], axis=1)
    bt[...] = jnp.concatenate([basis[...].astype(F32), marks], axis=0).astype(BF16)
    g[...] = mm_nt(bt[...], coup[...])
    for c in range(2):
        at = slice(512 * c, 512 * c + 512)
        p[at] = r[at] - mm(coup[at, : 2 * FACE], own[...])


def early_b_kernel(g, inv, coup, r, k, q):
    m = folded(mm(two_terms(g[...]), inv[...]))
    m2 = two_terms(m)
    k[...] = -folded(mm(m2, coup[...]))
    high = r[...].astype(BF16)
    low = (r[...] - high.astype(F32)).astype(BF16)
    q[...] = folded(mm(m2, high)) + mm(m2[:8], low)


def early_c_kernel(bt, block, own, k, qr, h, q, k_out):
    k2 = two_terms(k[...] + mm(bt[...], block[...]))
    q[...] = qr[...] + folded(mm(k2[:, : 2 * FACE], own[...]))
    k_out[...] = k2[:, 2 * FACE :]
    for c in range(4):
        at = slice(512 * c, 512 * c + 512)
        h[at] = mm(block[at, : 2 * FACE], own[...])


def west_terms_kernel(coup, block, p, h, q, k, west, p_out, h_out, q_out):
    own_n, with_west = 2 * FACE, 3 * FACE
    for c in range(2):
        at = slice(512 * c, 512 * c + 512)
        p_out[at] = p[at] - mm(coup[at, own_n:with_west], west[...])
    for c in range(4):
        at = slice(512 * c, 512 * c + 512)
        h_out[at] = h[at] + mm(block[at, own_n:with_west], west[...])
    q_out[...] = q[...] + folded(mm(k[:, :FACE], west[...]))


def corner_kernel(q, k, south, out):
    out[...] = q[...] + folded(mm(k[:, FACE:], south[...]))


def inner_kernel(coup, p, south, t):
    for c in range(2):
        at = slice(c * 512, (c + 1) * 512)
        t[at] = (p[at] - mm(coup[at, 3 * FACE :], south[...])).astype(BF16)


def result(f, coup, block, h, ub, south):
    at = slice(f * FACE, (f + 1) * FACE)
    return h[at] + mm(block[at, 3 * FACE :], south[...]) + mm_tn(coup[:, at], ub[...])


def tail(basis, f, keep):
    rows = basis[:, f * FACE : (f + 1) * FACE].astype(F32)
    return (jnp.concatenate([rows, jnp.zeros((12, FACE), F32)], axis=0) * keep).astype(BF16)


def solve_kernel(pos, coup, inv, block, t, h, south, basis, x_h, sent, ub, xbuf, sem):
    rows = 512
    copies = []
    for c in range(2):
        at = slice(c * rows, (c + 1) * rows)
        x = mm(inv[at], t[...])
        xbuf[at] = x
        ub[at] = x.astype(BF16)
        copies.append(pltpu.make_async_copy(xbuf.at[pl.ds(c * rows, rows)], x_h.at[pl.ds(c * rows, rows)], sem.at[c]))
        copies[c].start()
    keep = (pos[0] > 0).astype(F32)
    sent[:FACE] = (result(3, coup, block, h, ub, south) * keep).astype(BF16)
    sent[FACE:] = tail(basis, 3, keep)
    for copy in copies:
        copy.wait()


def west_kernel(pos, coup, block, h, ub, south, basis, sent):
    keep = (pos[0] > 0).astype(F32)
    sent[:FACE] = (result(2, coup, block, h, ub, south) * keep).astype(BF16)
    sent[FACE:] = tail(basis, 2, keep)


def kept_kernel(coup, block, h, ub, south, w, kept):
    for f in range(2):
        kept[f * FACE : (f + 1) * FACE] = column(w[f : f + 1, :]) * result(f, coup, block, h, ub, south)


def pair_kernel(pos, mine, theirs, out):
    first = lax.rem(pos[0], 2) == 0
    a, b = mine[...], theirs[...]
    low = jnp.where(first, a, b)
    high = jnp.where(first, b, a)
    for r in range(2):
        out[3 * r : 3 * r + 1] = low[2 * r : 2 * r + 1]
        out[3 * r + 1 : 3 * r + 2] = low[2 * r + 1 : 2 * r + 2] + high[2 * r : 2 * r + 1]
        out[3 * r + 2 : 3 * r + 3] = high[2 * r + 1 : 2 * r + 2]
    out[6:10] = low[4:8] + high[4:8]


def placed(at, blocks, slots):
    for k, block in enumerate(blocks):
        slots[at ^ k] = block[...]


def summed(slots, n):
    return (slots[0, n : n + 4] + slots[1, n : n + 4]) + (slots[2, n : n + 4] + slots[3, n : n + 4])


def rows_kernel(pos, b0, b1, b2, b3, out, slots):
    placed(lax.rem(pos[0], 4), (b0, b1, b2, b3), slots)
    out[0:3] = slots[0, 0:3]
    for b in range(1, 4):
        out[3 * b : 3 * b + 3] = slots[b - 1, 3:6] + slots[b, 0:3]
    out[12:15] = slots[3, 3:6]
    out[15:19] = summed(slots, 6)


def columns_kernel(i, j, b0, b1, b2, b3, e, o0, o1, o2, o3, slots, full, shares):
    placed(lax.div(j[0], 2), (b0, b1, b2, b3), slots)
    full[40:] = jnp.zeros((8, RHS), F32)
    for r in range(5):
        for c in range(9):
            b = min(c // 2, 3)
            n = 3 * r + c - 2 * b
            row = slots[b, n : n + 1]
            if c % 2 == 0 and 0 < c < 8:
                row = slots[b - 1, 3 * r + 2 : 3 * r + 3] + row
            full[9 * r + c : 9 * r + c + 1] = row
    e2, q2 = two_terms(e[...]), two_terms(full[...])
    all_shares = folded(mm(e2, q2[:48])) + mm(e2[:64], q2[48:])
    total = summed(slots, 15)
    for y in range(4):
        shares[y] = all_shares[16 * y : 16 * y + 16]
        shares[y, 12:16] = total
    at = lax.div(i[0], 4)
    for k, out in enumerate((o0, o1, o2, o3)):
        out[...] = shares[at ^ k]


def base_kernel(kept, got, w, out):
    wc = column(w[1:2, :])
    out[...] = kept[FACE:] + (1.0 - wc) * got[:FACE].astype(F32)


def correction(f, cc, got, w, basis):
    wr = w[f : f + 1, :]
    mine = basis[:, f * FACE : (f + 1) * FACE].astype(F32) * wr
    other = got[FACE:].astype(F32)[:4] * (1.0 - wr)
    x = jnp.concatenate([mine, other], axis=0)
    c = jnp.concatenate([cc[0:4], cc[4 + 4 * f : 8 + 4 * f]], axis=0)
    xh, ch = x.astype(BF16).astype(F32), c.astype(BF16).astype(F32)
    pad = jnp.zeros((8, RHS), F32)
    left = jnp.concatenate([xh, x - xh, xh, pad], axis=0).astype(BF16)
    right = jnp.concatenate([ch, ch, c - ch, pad], axis=0).astype(BF16)
    return left, right


def final_kernel(pos, b0, b1, b2, b3, kept, base, from_east, from_north, w, basis, z, cur, slots, zbuf, sem):
    placed(lax.div(pos[0], 4), (b0, b3, b2, b1), slots)
    cc = (slots[0] + slots[1]) + (slots[2] + slots[3])
    wc = column(w[0:1, :])
    copies = []
    for f, got in ((1, from_north), (0, from_east)):
        left, right = correction(f, cc, got, w, basis)
        for n in range(4):
            rows = slice(n * 128, (n + 1) * 128)
            part = base[rows] if f else kept[rows] + (1.0 - wc[rows]) * got[rows].astype(F32)
            zbuf[f, rows] = part + mm_tn(left[:, rows], right)
            here = pl.ds(n * 128, 128)
            copy = pltpu.make_async_copy(zbuf.at[f, here], z.at[f, here], sem.at[4 * f + n])
            copy.start()
            copies.append(copy)
    cur[...] = summed(slots, 12) / FACE
    for copy in copies:
        copy.wait()


def final(at, blocks, kept, base, from_east, from_north, w, basis):
    return call(
        final_kernel,
        (jax.ShapeDtypeStruct((2, FACE, RHS), F32), shape(NTERM, F32)),
        [SMEM] + [VMEM] * 10,
        (ANY, VMEM),
        [
            pltpu.VMEM((4, 16, RHS), F32),
            pltpu.VMEM((2, FACE, RHS), F32),
            pltpu.SemaphoreType.DMA((8,)),
        ],
    )(at, *blocks, kept, base, from_east, from_north, w, basis)


def along(x, axis, d):
    n = lax.axis_size(axis)
    return lax.ppermute(x, axis, [(s, (s + d) % n) for s in range(n)])


def exchanged(x, axis, stride, k):
    return lax.ppermute(x, axis, [(d ^ (k * stride), d) for d in range(lax.axis_size(axis))])


def four(x, axis, stride):
    far, middle, near = [exchanged(x, axis, stride, k) for k in (3, 2, 1)]
    return [x, near, middle, far]


def local(
    interior_residual,
    interface_residual,
    owner_face_weight,
    interior_inverse_block,
    coupling,
    interface_block,
    corner_trace_basis,
    coarse_inv,
    corner_map,
    contact,
):
    i = lax.axis_index("row").astype(jnp.int32).reshape(1)
    j = lax.axis_index("col").astype(jnp.int32).reshape(1)
    faces_in = interface_residual[0, 0]
    r = interior_residual[0, 0]
    w = owner_face_weight[0, 0]
    inv, coup, block = interior_inverse_block[0, 0], coupling[0, 0], interface_block[0, 0]
    basis = corner_trace_basis[0, 0]

    to_north = north_face(i, faces_in, w)
    south = along(to_north, "row", 1)
    to_east, own = east_face(j, faces_in, w, (to_north,))
    west = along(to_east, "col", 1)
    e = table(i, j, corner_map, coarse_inv, (own,))
    p, g, bt = call(
        early_a_kernel,
        (shape(INTERIOR, F32), shape(8, F32, INTERIOR), shape(8, BF16, 4 * FACE)),
        [VMEM] * 5,
        (VMEM,) * 3,
        after=(e,),
        cost=10,
    )(coup, r, own, basis, contact[0, 0])
    k, q = call(early_b_kernel, (shape(8, F32, 4 * FACE), shape(8, F32)), [VMEM] * 4, (VMEM,) * 2, cost=10)(g, inv, coup, r)
    h, q, k = call(
        early_c_kernel,
        (shape(4 * FACE, F32), shape(8, F32), shape(16, BF16, 2 * FACE)),
        [VMEM] * 5,
        (VMEM,) * 3,
        cost=10,
    )(bt, block, own, k, q)

    p, h, q = call(
        west_terms_kernel,
        (shape(INTERIOR, F32), shape(4 * FACE, F32), shape(8, F32)),
        [VMEM] * 7,
        (VMEM,) * 3,
        cost=2,
    )(coup, block, p, h, q, k, west)

    sums = call(corner_kernel, shape(8, F32), [VMEM] * 3, VMEM)(q, k, south)
    other = lax.ppermute(sums, "col", [(s, s ^ 1) for s in range(COLS)])
    t = call(inner_kernel, shape(INTERIOR, BF16), [VMEM] * 3, VMEM, after=(sums,), cost=1)(coup, p, south)
    sums = call(pair_kernel, shape(10, F32), [SMEM, VMEM, VMEM], VMEM, after=(t,))(j, sums, other)
    blocks = four(sums, "row", 1)
    x, to_south, ub = call(
        solve_kernel,
        (shape(INTERIOR, F32), shape(SENT, BF16), shape(INTERIOR, BF16)),
        [SMEM] + [VMEM] * 7,
        (ANY, VMEM, VMEM),
        [pltpu.VMEM((INTERIOR, RHS), F32), pltpu.SemaphoreType.DMA((2,))],
        after=(sums,),
        cost=4,
    )(i, coup, inv, block, t, h, south, basis)
    from_north = along(to_south, "row", -1)
    sums = call(
        rows_kernel, shape(19, F32), [SMEM] + [VMEM] * 4, VMEM, [pltpu.VMEM((4, 10, RHS), F32)], after=(to_south,)
    )(i, *blocks)
    blocks = four(sums, "col", 2)
    to_west = call(west_kernel, shape(SENT, BF16), [SMEM] + [VMEM] * 6, VMEM, after=(sums,), cost=1)(
        j, coup, block, h, ub, south, basis
    )
    from_east = along(to_west, "col", -1)
    kept = call(kept_kernel, shape(2 * FACE, F32), [VMEM] * 6, VMEM, after=(sums, to_west), cost=30)(
        coup, block, h, ub, south, w
    )
    shares = call(
        columns_kernel,
        (shape(16, F32),) * 4,
        [SMEM, SMEM] + [VMEM] * 5,
        (VMEM,) * 4,
        [pltpu.VMEM((4, 19, RHS), F32), pltpu.VMEM((48, RHS), F32), pltpu.VMEM((4, 16, RHS), F32)],
        after=(kept,),
    )(i, j, *blocks, e)
    far, middle, near = [exchanged(shares[k], "row", 4, k) for k in (3, 2, 1)]
    blocks = [shares[0], far, middle, near]
    base = call(base_kernel, shape(FACE, F32), [VMEM] * 3, VMEM, after=(shares[0],), cost=60)(kept, from_north, w)
    z, currents = final(i, blocks, kept, base, from_east, from_north, w, basis)
    return x[None, None], z[None, None], currents


def solution(mesh):
    return jax.shard_map(
        local,
        mesh=mesh,
        in_specs=(
            P("row", "col", None, None),
            P("row", "col", None, None, None),
            P("row", "col", None, None),
            P("row", "col", None, None),
            P("row", "col", None, None),
            P("row", "col", None, None),
            P("row", "col", None, None),
            P(),
            P(),
            P("row", "col", None, None),
        ),
        out_specs=(P("row", "col", None, None), P("row", "col", None, None, None), P()),
        check_vma=False,
    )
```
